32 devices in a mesh: tile: 8 (over z, x), slide: 4 (over y, core).
Axes of the slice: x: 2, y: 2, z: 4, core: 2. Of those that a mesh axis runs over, the one named last changes fastest.
Arguments:
- tiles: bfloat16 [4, 24, 7, 7, 2048], P('slide', 'tile'), may hold values from -6 to 6
- tile_counts: int32 [4, 8], P('slide', 'tile'), may hold values from 1 to 3, as said below
- tile_weights: float32 [4, 24], P('slide', 'tile'), may hold values from 0.1 to 2
- slide_of: int32 [4, 24, 1], P('slide', 'tile'), may hold values from 0 to 7, as said below
- owner_map: int32 [4, 8], P('slide'), may hold values from 0 to 7, each once within a row
- cotangent: bfloat16 [4, 8, 2048], P('slide', 'tile'), may hold values from -6 to 6
- conv_weight: bfloat16 [9, 64, 2048], replicated, may hold values from -0.25 to 0.25
Outputs:
- pooled: float32 [4, 8, 2048], P('slide', 'tile')
- input_grads: float32 [4, 24, 7, 7, 2048], P('slide', 'tile')
- weight_grads: float32 [9, 64, 2048], P(None, None, 'tile')
The draws below stay inside these ranges and needn't reach their ends.
Inputs may be any that keep to these rules, and one draw needn't show every extreme that they name: On every device the live tiles are the first tile_counts slots; in each slide group one device has all 3 slots live. `slide_of`: in each slide group, max(1, 2) slides name exactly one slot each, the first slot of some device; the other slots name the remaining slides evenly at random.
All inputs are finite; a program needn't handle non-finite values.
Results may differ from the reference program's by a relative error of at most 0.0065.
Values may be sent and summed in bfloat16 or wider, within the bound.
No kernel may reach another device: no remote copies, remote signals or barrier semaphores. Data moves between devices by JAX's collectives and lax.ppermute only.
A program may use at most 128 MiB of HBM per device.

```python
import math
import jax
import jax.numpy as jnp
from jax import lax

CHANNELS = 2048
GROUPS = 32
SIDE = 7
SLOTS = 3
GROUP_WIDTH = 64
TILES_GROUP = 24
N_TILE = 8
N_SLIDE = 4


def draw_tiles(key, part):
    key_noise, key_mean = jax.random.split(key, 2)
    full_shape = (N_SLIDE, TILES_GROUP, SIDE, SIDE, CHANNELS)
    mean_shape = (N_SLIDE, TILES_GROUP, 1, 1, CHANNELS)
    noise_part = jax.random.normal(key_noise, full_shape, jnp.float32) * 0.7
    tile_mean = jax.random.normal(key_mean, mean_shape, jnp.float32) * 0.8
    values = noise_part + tile_mean
    return jnp.clip(values, -6.0, 6.0).astype(jnp.bfloat16)


def draw_tile_counts(key, part):
    key_count, key_pick = jax.random.split(key)
    drawn = jax.random.randint(key_count, (N_SLIDE, N_TILE), 1, SLOTS + 1)
    picked = jax.random.randint(key_pick, (N_SLIDE, 1), 0, N_TILE)
    column = jnp.arange(N_TILE, dtype=jnp.int32)[None, :]
    return jnp.where(column == picked, SLOTS, drawn).astype(jnp.int32)


def shuffle_devices(subkey):
    return jax.random.permutation(subkey, N_TILE).astype(jnp.int32)


def draw_slide_of(key, part):
    key_dense, key_chosen, key_label = jax.random.split(jax.random.fold_in(key, 17), 3)
    sparse_count = max(1, N_TILE // 4)
    dense_count = N_TILE - sparse_count
    labels = jax.random.randint(key_dense, (N_SLIDE, TILES_GROUP), 0, dense_count).astype(jnp.int32)
    chosen = jax.vmap(shuffle_devices)(jax.random.split(key_chosen, N_SLIDE))
    positions = chosen[:, :sparse_count] * SLOTS
    group_rows = jnp.arange(N_SLIDE, dtype=jnp.int32)[:, None]
    sparse_labels = dense_count + jnp.arange(sparse_count, dtype=jnp.int32)[None, :]
    labels = labels.at[group_rows, positions].set(jnp.broadcast_to(sparse_labels, positions.shape))
    relabel = jax.vmap(shuffle_devices)(jax.random.split(key_label, N_SLIDE))
    return jnp.take_along_axis(relabel, labels, axis=1)[:, :, None].astype(jnp.int32)


def block_levels(own_key, dims, cuts, low, high):
    def one(axis_at, parts):
        steps = jax.random.uniform(jax.random.fold_in(jax.random.fold_in(own_key, 6), axis_at), (parts,), jnp.float32, low / len(cuts), high / len(cuts))
        return jnp.repeat(jnp.exp(steps), dims[axis_at] // parts).reshape((-1,) + (1,) * (len(dims) - axis_at - 1))

    factor_of = one(*cuts[0])
    for cut in cuts[1:]:
        factor_of = factor_of * one(*cut)
    return factor_of


def bell_draw(stream_key, dims, spread, most, cuts=(), kind=jnp.bfloat16):
    values = jax.random.normal(stream_key, dims, jnp.float32) * spread
    if len(cuts) > 0:
        values = block_levels(stream_key, dims, cuts, -0.22, 0.18) * values
    return jnp.clip(values, min=-most, max=most).astype(kind)


def setup_inputs(seed: int = 0) -> dict:
    streams_of = jax.random.split(jax.random.key(seed), 8)
    tiles = draw_tiles(jax.random.fold_in(streams_of[7], 71), 0)
    tile_counts = draw_tile_counts(jax.random.fold_in(streams_of[7], 71), 0)
    tile_weights = jnp.clip(jnp.exp(math.log(2.0) - 2.9957323 * jax.random.uniform(streams_of[2], (N_SLIDE, TILES_GROUP), jnp.float32) ** block_levels(streams_of[2], (N_SLIDE, TILES_GROUP), ((0, 4), (1, 8)), -0.2, 0.2)), 0.1, 2.0)
    slide_of = draw_slide_of(jax.random.fold_in(streams_of[7], 71), 0)
    owner_map = jax.vmap(lambda own: jax.random.permutation(own, N_TILE))(jax.random.split(streams_of[4], N_SLIDE)).reshape((N_SLIDE, N_TILE)).astype(jnp.int32)
    cotangent = bell_draw(streams_of[5], (N_SLIDE, N_TILE, CHANNELS), 1.0, 6.0, ((0, 4), (1, 8)))
    conv_weight = bell_draw(streams_of[6], (9, GROUP_WIDTH, CHANNELS), (9 * GROUP_WIDTH) ** -0.5, 0.25)
    return {"tiles": tiles, "tile_counts": tile_counts, "tile_weights": tile_weights, "slide_of": slide_of, "owner_map": owner_map, "cotangent": cotangent, "conv_weight": conv_weight}


loss_scale = 512.0


def conv_forward(features, weight):
    count_rows = features.shape[0]
    padded = jnp.pad(features.astype(jnp.float32), ((0, 0), (1, 1), (1, 1), (0, 0)))
    weight_f = weight.astype(jnp.float32)
    summed = jnp.zeros((count_rows, SIDE, SIDE, GROUPS, GROUP_WIDTH), jnp.float32)
    for offset in range(9):
        row_off, col_off = divmod(offset, 3)
        window = padded[:, row_off:row_off + SIDE, col_off:col_off + SIDE, :].reshape(count_rows, SIDE, SIDE, GROUPS, GROUP_WIDTH)
        tap = weight_f[offset].reshape(GROUP_WIDTH, GROUPS, GROUP_WIDTH)
        summed = summed + jnp.einsum("nhwgi,igo->nhwgo", window, tap)
    return summed.reshape(count_rows, SIDE, SIDE, CHANNELS)


def conv_backward(features, weight, pre_grad):
    count_rows = features.shape[0]
    padded = jnp.pad(features.astype(jnp.float32), ((0, 0), (1, 1), (1, 1), (0, 0)))
    weight_f = weight.astype(jnp.float32)
    grads_split = pre_grad.astype(jnp.float32).reshape(count_rows, SIDE, SIDE, GROUPS, GROUP_WIDTH)
    grads_padded = jnp.pad(grads_split, ((0, 0), (1, 1), (1, 1), (0, 0), (0, 0)))
    summed = jnp.zeros((count_rows, SIDE, SIDE, GROUPS, GROUP_WIDTH), jnp.float32)
    pieces = []
    for offset in range(9):
        row_off, col_off = divmod(offset, 3)
        window = padded[:, row_off:row_off + SIDE, col_off:col_off + SIDE, :].reshape(count_rows, SIDE, SIDE, GROUPS, GROUP_WIDTH)
        tap = weight_f[offset].reshape(GROUP_WIDTH, GROUPS, GROUP_WIDTH)
        pieces.append(jnp.einsum("nhwgi,nhwgo->igo", window, grads_split).reshape(GROUP_WIDTH, CHANNELS))
        shifted = grads_padded[:, 2 - row_off:2 - row_off + SIDE, 2 - col_off:2 - col_off + SIDE]
        summed = summed + jnp.einsum("nhwgo,igo->nhwgi", shifted, tap)
    input_grads = summed.reshape(count_rows, SIDE, SIDE, CHANNELS)
    return input_grads, jnp.stack(pieces, axis=0)


def reference(tiles, tile_counts, tile_weights, slide_of, owner_map, cotangent, conv_weight):
    slot_index = jnp.arange(TILES_GROUP, dtype=jnp.int32) % SLOTS
    device_of = jnp.arange(TILES_GROUP, dtype=jnp.int32) // SLOTS
    alive = (slot_index[None, :] < tile_counts[:, device_of]).astype(jnp.float32)
    tile_coef = alive * tile_weights
    target = jnp.take_along_axis(owner_map, slide_of[:, :, 0], axis=1)

    def one_group(packed):
        features, coef_row, target_row, cot_row = packed
        pre = conv_forward(features, conv_weight)
        embedding = jnp.mean(jax.nn.silu(pre), axis=(1, 2)).astype(jnp.bfloat16)
        owner_ids = jnp.arange(N_TILE, dtype=jnp.int32)
        routing = (target_row[None, :] == owner_ids[:, None]).astype(jnp.float32) * coef_row[None, :]
        numerator = jnp.dot(routing, embedding.astype(jnp.float32), precision=lax.Precision.HIGHEST)
        denominator = jnp.maximum(jnp.sum(routing, axis=1), 1.0)
        pooled = numerator / denominator[:, None]
        scaled = (loss_scale * cot_row.astype(jnp.float32) / denominator[:, None]).astype(jnp.bfloat16)
        tile_grads = jnp.dot(routing.T, scaled.astype(jnp.float32), precision=lax.Precision.HIGHEST)
        sigma = jax.nn.sigmoid(pre)
        slope = sigma * (1.0 + pre * (1.0 - sigma))
        pre_grad = (tile_grads[:, None, None, :] / (SIDE * SIDE) * slope).astype(jnp.bfloat16)
        input_grads, weight_terms = conv_backward(features, conv_weight, pre_grad)
        return pooled, input_grads, weight_terms

    pooled, input_grads, weight_terms = lax.map(one_group, (tiles, tile_coef, target, cotangent))
    weight_grads = jnp.sum(weight_terms, axis=0) / loss_scale
    return pooled, input_grads, weight_grads
```

```python
import functools

import jax
import jax.numpy as jnp
from jax import lax
from jax.experimental import pallas as pl
from jax.experimental.pallas import tpu as pltpu
from jax.sharding import PartitionSpec as P

LOSS_SCALE = 512.0
BLOCK = 256
ROW = 8
F32 = jnp.float32
BF16 = jnp.bfloat16


def vmem_whole():
    return pl.BlockSpec(memory_space=pltpu.VMEM)


def smem_whole():
    return pl.BlockSpec(memory_space=pltpu.SMEM)


def own_scalars(counts_ref, weights_ref, slide_ref, owner_ref, slots):
    coefs, targets = [], []
    for slot in range(slots):
        live = counts_ref[0, 0] > slot
        coefs.append(jnp.where(live, weights_ref[0, slot], 0.0))
        targets.append(owner_ref[0, slide_ref[0, slot]])
    return coefs, targets


def block_diagonal(tap, mask):
    width, channels = tap.shape
    if channels == width:
        return tap
    return jnp.concatenate([tap] * (channels // width), axis=0) * mask


def diagonal_mask(channels, width):
    row = lax.broadcasted_iota(jnp.int32, (channels, channels), 0) // width
    col = lax.broadcasted_iota(jnp.int32, (channels, channels), 1) // width
    return (row == col).astype(F32).astype(BF16)


def shifted(rows):
    count = rows.shape[0]
    return (
        pltpu.roll(rows, 1, 0).astype(BF16),
        rows.astype(BF16),
        pltpu.roll(rows, count - 1, 0).astype(BF16),
    )


def conv_taps(rows_ref, weight_of, pitch, count, flip, dims):
    total = None
    for offset in range(9):
        row_off, col_off = divmod(offset, 3)
        if flip:
            row_off, col_off = 2 - row_off, 2 - col_off
        rows = rows_ref[col_off, pl.ds(row_off * pitch, count), :]
        term = lax.dot_general(rows, weight_of(offset), dims, preferred_element_type=F32)
        total = term if total is None else total + term
    return total


def routing_of(info, slots):
    devices = info.shape[0]
    owners = lax.broadcasted_iota(jnp.int32, (devices, 128), 1).astype(F32)
    routes = []
    total = jnp.zeros((1, 128), F32)
    for slot in range(slots):
        coef = (
            info[:, slot : slot + 1]
            + info[:, slots + slot : slots + slot + 1]
            + info[:, 2 * slots + slot : 2 * slots + slot + 1]
        )
        target = info[:, 3 * slots + slot : 3 * slots + slot + 1]
        route = jnp.where(target == owners, coef, 0.0)
        routes.append(route)
        total = total + jnp.sum(route, axis=0, keepdims=True)
    return routes, jnp.maximum(total, 1.0)


def scaled_rows(cot, denominator):
    rows = []
    for owner in range(cot.shape[0]):
        value = LOSS_SCALE * cot[owner : owner + 1] / denominator[:, owner : owner + 1]
        rows.append(value.astype(BF16).astype(F32))
    return rows


def info_row(coefs, targets, lanes):
    slots = len(coefs)
    lane = lax.broadcasted_iota(jnp.int32, (1, lanes), 1)
    value = jnp.zeros((1, lanes), F32)
    for slot in range(slots):
        for part in range(3):
            value = jnp.where(lane == part * slots + slot, coefs[slot], value)
        value = jnp.where(lane == 3 * slots + slot, targets[slot].astype(F32), value)
    high = value.astype(BF16).astype(F32)
    middle = (value - high).astype(BF16).astype(F32)
    low = (value - high - middle).astype(BF16).astype(F32)
    value = jnp.where((lane >= slots) & (lane < 2 * slots), middle, high)
    return jnp.where((lane >= 2 * slots) & (lane < 3 * slots), low, value)


def pack_kernel(packed, counts_ref, weights_ref, slide_ref, owner_ref, x_ref, cot_ref, out_ref, info_ref):
    devices, slots, side, _, lanes = out_ref.shape
    coefs, targets = own_scalars(counts_ref, weights_ref, slide_ref, owner_ref, slots)
    info = info_row(coefs, targets, info_ref.shape[1])
    info_ref[...] = info
    cot = cot_ref[0].astype(F32)
    for slot in range(slots):
        for high in range(side):
            index = slot * side + high
            rows = x_ref[0, slot, high].astype(F32)
            if packed and index < devices:
                spare = cot[:, index * lanes : (index + 1) * lanes]
            elif packed and index == devices:
                spare = info[:, :lanes]
            else:
                spare = jnp.zeros((1, lanes), F32)
            for device in range(devices):
                part = rows[:, device * lanes : (device + 1) * lanes]
                out_ref[device, slot, high] = jnp.concatenate([part, spare], axis=0).astype(BF16)


def local_kernel(
    counts_ref, weights_ref, slide_ref, owner_ref, x_ref, w_ref, slope_ref, share_ref, rows_ref
):
    step = pl.program_id(0)
    side, kept, lanes = slope_ref.shape
    slots = kept // ROW
    devices = share_ref.shape[0]
    pitch = rows_ref.shape[1] // (side + 2)
    width = w_ref.shape[1]
    for col in range(3):
        rows_ref[col, pl.ds(0, pitch), :] = jnp.zeros((pitch, lanes), BF16)
        rows_ref[col, pl.ds((side + 1) * pitch, pitch), :] = jnp.zeros((pitch, lanes), BF16)
    for high in range(side):
        pieces = []
        for slot in range(slots):
            pieces += [x_ref[0, slot, high].astype(F32), jnp.zeros((ROW - side, lanes), F32)]
        if pitch > kept:
            pieces.append(jnp.zeros((pitch - kept, lanes), F32))
        for col, rows in enumerate(shifted(jnp.concatenate(pieces, axis=0))):
            rows_ref[col, pl.ds((high + 1) * pitch, pitch), :] = rows
    mask = diagonal_mask(lanes, width)
    pre = conv_taps(
        rows_ref,
        lambda tap: block_diagonal(w_ref[tap], mask),
        pitch,
        side * pitch,
        False,
        (((1,), (0,)), ((), ())),
    )
    sigma = jax.nn.sigmoid(pre)
    slope = sigma * (1.0 + pre * (1.0 - sigma))
    active = pre * sigma
    total = active[:pitch]
    slope_ref[0] = slope[:kept]
    for high in range(1, side):
        slope_ref[high] = slope[high * pitch : high * pitch + kept]
        total = total + active[high * pitch : (high + 1) * pitch]
    place = lax.broadcasted_iota(jnp.int32, (ROW, lanes), 0)
    coefs, targets = own_scalars(counts_ref, weights_ref, slide_ref, owner_ref, slots)
    means = []
    for slot in range(slots):
        here = jnp.where(place < side, total[slot * ROW : (slot + 1) * ROW], 0.0)
        mean = jnp.sum(here, axis=0, keepdims=True) / (side * side)
        means.append(mean.astype(BF16).astype(F32))
    for owner in range(devices):
        share = jnp.zeros((1, lanes), F32)
        for slot in range(slots):
            share = share + jnp.where(targets[slot] == owner, coefs[slot], 0.0) * means[slot]
        share_ref[owner, pl.ds(step, 1), :] = share


def weight_kernel(packed, my_ref, got_ref, w_ref, *refs):
    if packed:
        out_ref, rows_ref, grad_ref = refs
    else:
        cot_ref, info_ref, out_ref, rows_ref, grad_ref = refs
    devices, slots, side, _, lanes = got_ref.shape
    width = w_ref.shape[1]
    part = devices * ROW
    pitch = slots * part
    if packed:
        mine = my_ref[0]
        cot = got_ref[:, mine // side, mine % side].astype(F32)[:, ROW - 1, :]
        info = got_ref[:, devices // side, devices % side].astype(F32)[:, ROW - 1, :]
    else:
        cot = cot_ref[...]
        info = info_ref[...]
    routes, denominator = routing_of(info, slots)
    scaled = scaled_rows(cot, denominator)
    place = lax.broadcasted_iota(jnp.int32, (devices, ROW, lanes), 1)
    tile_grads = []
    for slot in range(slots):
        rows = jnp.zeros((devices, lanes), F32)
        for owner in range(devices):
            rows = rows + routes[slot][:, owner : owner + 1] * scaled[owner]
        spread = jnp.broadcast_to(rows[:, None, :], (devices, ROW, lanes)) / (side * side)
        tile_grads.append(jnp.where(place < side, spread, 0.0).reshape(part, lanes))
    tile_grad = jnp.concatenate(tile_grads, axis=0)

    zero = jnp.zeros((pitch, lanes), BF16)
    for col in range(3):
        rows_ref[col, pl.ds(0, pitch), :] = zero
        rows_ref[col, pl.ds((side + 1) * pitch, pitch), :] = zero
    grad_ref[pl.ds(0, pitch), :] = zero
    grad_ref[pl.ds((side + 1) * pitch, pitch), :] = zero
    for high in range(side):
        for slot in range(slots):
            rows = jnp.where(place < side, got_ref[:, slot, high].astype(F32), 0.0)
            for col, moved in enumerate(shifted(rows.reshape(part, lanes))):
                rows_ref[col, pl.ds((high + 1) * pitch + slot * part, part), :] = moved
    mask = diagonal_mask(lanes, width) if lanes > width else None
    pre = conv_taps(
        rows_ref,
        lambda tap: block_diagonal(w_ref[tap], mask),
        pitch,
        side * pitch,
        False,
        (((1,), (0,)), ((), ())),
    )
    sigma = jax.nn.sigmoid(pre)
    slope = sigma * (1.0 + pre * (1.0 - sigma))
    for high in range(side):
        here = slope[high * pitch : (high + 1) * pitch] * tile_grad
        grad_ref[pl.ds((high + 1) * pitch, pitch), :] = here.astype(BF16)
    group = lax.broadcasted_iota(jnp.int32, (width, lanes), 1) // width
    for offset in range(9):
        row_off, col_off = divmod(offset, 3)
        product = lax.dot_general(
            rows_ref[col_off, pl.ds(pitch, side * pitch), :],
            grad_ref[pl.ds((2 - row_off) * pitch, side * pitch), :],
            (((0,), (0,)), ((), ())),
            preferred_element_type=F32,
        )
        result = product[:width]
        for index in range(1, lanes // width):
            result = jnp.where(group == index, product[index * width : (index + 1) * width], result)
        out_ref[offset] = result


def input_kernel(
    packed,
    my_ref,
    counts_ref,
    weights_ref,
    slide_ref,
    owner_ref,
    slope_ref,
    w_ref,
    cot_ref,
    info_ref,
    share_ref,
    out_ref,
    pooled_ref,
    rows_ref,
):
    step = pl.program_id(0)
    side, kept, lanes = slope_ref.shape
    slots = kept // ROW
    devices = share_ref.shape[0]
    pitch = rows_ref.shape[1] // (side + 2)
    width = w_ref.shape[1]
    if packed:
        cot = cot_ref[:, 0, 0].astype(F32)[:, ROW - 1, :]
        info = info_ref[:, 0, 0].astype(F32)[:, ROW - 1, :]
    else:
        cot = cot_ref[...]
        info = info_ref[...]
    _, denominator = routing_of(info, slots)
    scaled = scaled_rows(cot, denominator)
    owners = lax.broadcasted_iota(jnp.int32, (1, 128), 1)
    mine = jnp.sum(jnp.where(owners == my_ref[0], denominator, 0.0), axis=1, keepdims=True)
    shares = share_ref[:, pl.ds(step, 1), :]
    pooled_ref[0] = jnp.sum(shares, axis=0) / mine

    coefs, targets = own_scalars(counts_ref, weights_ref, slide_ref, owner_ref, slots)
    place = lax.broadcasted_iota(jnp.int32, (ROW, lanes), 0)
    pieces = []
    for slot in range(slots):
        row = jnp.zeros((1, lanes), F32)
        for owner in range(devices):
            row = row + jnp.where(targets[slot] == owner, coefs[slot], 0.0) * scaled[owner]
        spread = jnp.broadcast_to(row, (ROW, lanes)) / (side * side)
        pieces.append(jnp.where(place < side, spread, 0.0))
    tile_grad = jnp.concatenate(pieces, axis=0)

    for col in range(3):
        rows_ref[col, pl.ds(0, pitch), :] = jnp.zeros((pitch, lanes), BF16)
        rows_ref[col, pl.ds((side + 1) * pitch, pitch), :] = jnp.zeros((pitch, lanes), BF16)
    for high in range(side):
        rows = slope_ref[high] * tile_grad
        if pitch > kept:
            rows = jnp.concatenate([rows, jnp.zeros((pitch - kept, lanes), F32)], axis=0)
        for col, moved in enumerate(shifted(rows)):
            rows_ref[col, pl.ds((high + 1) * pitch, pitch), :] = moved
    mask = diagonal_mask(lanes, width)
    total = conv_taps(
        rows_ref,
        lambda tap: block_diagonal(w_ref[tap], mask),
        pitch,
        side * pitch,
        True,
        (((1,), (1,)), ((), ())),
    )
    for high in range(side):
        for slot in range(slots):
            start = high * pitch + slot * ROW
            for wide in range(side):
                out_ref[slot, high, wide] = total[start + wide : start + wide + 1]


def params(mebibytes):
    return pltpu.CompilerParams(vmem_limit_bytes=mebibytes * 2**20)


def cost(flops, moved):
    return pl.CostEstimate(flops=flops, bytes_accessed=moved, transcendentals=0)


def exchange_sum(value, axis, step):
    count = lax.axis_size(axis)
    return value, lax.ppermute(value, axis, [(i, i ^ step) for i in range(count)])


def shards(tiles, tile_counts, tile_weights, slide_of, owner_map, cotangent, conv_weight):
    _, slots, side, _, channels = tiles.shape
    taps, width, _ = conv_weight.shape
    devices = lax.axis_size("tile")
    lanes = channels // devices
    blocks = channels // BLOCK
    mine = lax.axis_index("tile").astype(jnp.int32).reshape(1)
    slides = slide_of[:, :, 0]
    packed = lanes == BLOCK and devices + 1 <= slots * side
    scalars = (tile_counts, tile_weights, slides, owner_map)
    kept = slots * ROW
    pitch = -(-kept // 16) * 16
    macs = slots * side * side * taps * width * channels

    chunks, info = pl.pallas_call(
        functools.partial(pack_kernel, packed),
        out_shape=(
            jax.ShapeDtypeStruct((devices, slots, side, ROW, lanes), BF16),
            jax.ShapeDtypeStruct((1, max(lanes, 128)), F32),
        ),
        in_specs=[smem_whole()] * 4 + [vmem_whole()] * 2,
        out_specs=(vmem_whole(), vmem_whole()),
        compiler_params=params(16),
    )(*scalars, tiles, cotangent)
    got = lax.all_to_all(chunks, "tile", 0, 0, tiled=True)

    slope, share = pl.pallas_call(
        local_kernel,
        grid=(blocks,),
        out_shape=(
            jax.ShapeDtypeStruct((side, kept, channels), F32),
            jax.ShapeDtypeStruct((devices, blocks, BLOCK), F32),
        ),
        in_specs=[smem_whole()] * 4
        + [
            pl.BlockSpec((1, slots, side, side, BLOCK), lambda j: (0, 0, 0, 0, j)),
            pl.BlockSpec((taps, width, BLOCK), lambda j: (0, 0, j)),
        ],
        out_specs=(
            pl.BlockSpec((side, kept, BLOCK), lambda j: (0, 0, j)),
            pl.BlockSpec((devices, blocks, BLOCK), lambda j: (0, 0, 0)),
        ),
        scratch_shapes=[pltpu.VMEM((3, (side + 2) * pitch, BLOCK), BF16)],
        compiler_params=params(24),
        cost_estimate=cost(8 * macs, 4 * 2**20),
    )(*scalars, tiles, conv_weight)
    shares = lax.all_to_all(share, "tile", 0, 0, tiled=True)

    own_weight = lax.dynamic_slice_in_dim(conv_weight, mine[0] * lanes, lanes, 2)
    if packed:
        extra = ()
        cot_args = (got, got)
        cot_specs = [
            pl.BlockSpec((devices, 1, 1, ROW, lanes), lambda j: (0, j // side, j % side, 0, 0)),
            pl.BlockSpec(
                (devices, 1, 1, ROW, lanes), lambda j: (0, devices // side, devices % side, 0, 0)
            ),
        ]
    else:
        cot_all = lax.all_gather(cotangent[0], "tile", axis=0, tiled=True).astype(F32)
        info_all = lax.all_gather(info, "tile", axis=0, tiled=True)
        extra = (lax.dynamic_slice_in_dim(cot_all, mine[0] * lanes, lanes, 1), info_all)
        cot_args = (cot_all, info_all)
        cot_specs = [
            pl.BlockSpec((devices, BLOCK), lambda j: (0, j)),
            pl.BlockSpec((devices, 128), lambda j: (0, 0)),
        ]
    pitch_all = slots * devices * ROW
    terms = pl.pallas_call(
        functools.partial(weight_kernel, packed),
        out_shape=jax.ShapeDtypeStruct((taps, width, lanes), F32),
        in_specs=[smem_whole()] + [vmem_whole()] * (2 + len(extra)),
        out_specs=vmem_whole(),
        scratch_shapes=[
            pltpu.VMEM((3, (side + 2) * pitch_all, lanes), BF16),
            pltpu.VMEM(((side + 2) * pitch_all, lanes), BF16),
        ],
        compiler_params=params(32),
        cost_estimate=cost(16 * macs, 4 * 2**20),
    )(mine, got, own_weight, *extra)

    own, other = exchange_sum(terms, "slide", 1)
    total = own + other
    step = 2
    while step < lax.axis_size("slide"):
        own, other = exchange_sum(total.astype(BF16), "slide", step)
        total = own.astype(F32) + other.astype(F32)
        step *= 2
    weight_grads = total / LOSS_SCALE

    grads, pooled = pl.pallas_call(
        functools.partial(input_kernel, packed),
        grid=(blocks,),
        out_shape=(
            jax.ShapeDtypeStruct((slots, side, side, 1, channels), F32),
            jax.ShapeDtypeStruct((1, 1, channels), F32),
        ),
        in_specs=[smem_whole()] * 5
        + [
            pl.BlockSpec((side, kept, BLOCK), lambda j: (0, 0, j)),
            pl.BlockSpec((taps, width, BLOCK), lambda j: (0, 0, j)),
        ]
        + cot_specs
        + [pl.BlockSpec((devices, blocks, BLOCK), lambda j: (0, 0, 0))],
        out_specs=(
            pl.BlockSpec((slots, side, side, 1, BLOCK), lambda j: (0, 0, 0, 0, j)),
            pl.BlockSpec((1, 1, BLOCK), lambda j: (0, 0, j)),
        ),
        scratch_shapes=[pltpu.VMEM((3, (side + 2) * pitch, BLOCK), BF16)],
        compiler_params=params(24),
        cost_estimate=cost(8 * macs, 4 * 2**20),
    )(mine, *scalars, slope, conv_weight, *cot_args, shares)
    input_grads = jnp.transpose(grads, (3, 0, 1, 2, 4))
    return (pooled, input_grads, weight_grads)


def solution(mesh):
    return jax.shard_map(
        shards,
        mesh=mesh,
        in_specs=(
            P("slide", "tile", None, None, None),
            P("slide", "tile"),
            P("slide", "tile"),
            P("slide", "tile", None),
            P("slide", None),
            P("slide", "tile", None),
            P(),
        ),
        out_specs=(
            P("slide", "tile", None),
            P("slide", "tile", None, None, None),
            P(None, None, "tile"),
        ),
        check_vma=False,
    )
```

```python
import functools

import jax
import jax.numpy as jnp
from jax import lax
from jax.experimental import pallas as pl
from jax.experimental.pallas import tpu as pltpu
from jax.sharding import PartitionSpec as P

LOSS_SCALE = 512.0
BLOCK = 256
ROW = 8
F32 = jnp.float32
BF16 = jnp.bfloat16


def vmem_whole():
    return pl.BlockSpec(memory_space=pltpu.VMEM)


def smem_whole():
    return pl.BlockSpec(memory_space=pltpu.SMEM)


def own_scalars(counts_ref, weights_ref, slide_ref, owner_ref, slots):
    coefs, targets = [], []
    for slot in range(slots):
        live = counts_ref[0, 0] > slot
        coefs.append(jnp.where(live, weights_ref[0, slot], 0.0))
        targets.append(owner_ref[0, slide_ref[0, slot]])
    return coefs, targets


def block_diagonal(tap, mask):
    width, channels = tap.shape
    if channels == width:
        return tap
    return jnp.concatenate([tap] * (channels // width), axis=0) * mask


def diagonal_mask(channels, width):
    row = lax.broadcasted_iota(jnp.int32, (channels, channels), 0) // width
    col = lax.broadcasted_iota(jnp.int32, (channels, channels), 1) // width
    return (row == col).astype(F32).astype(BF16)


def shifted(rows):
    count = rows.shape[0]
    return (
        pltpu.roll(rows, 1, 0).astype(BF16),
        rows.astype(BF16),
        pltpu.roll(rows, count - 1, 0).astype(BF16),
    )


def conv_taps(rows_ref, weight_of, pitch, count, flip, dims):
    total = None
    for offset in range(9):
        row_off, col_off = divmod(offset, 3)
        if flip:
            row_off, col_off = 2 - row_off, 2 - col_off
        rows = rows_ref[col_off, pl.ds(row_off * pitch, count), :]
        term = lax.dot_general(rows, weight_of(offset), dims, preferred_element_type=F32)
        total = term if total is None else total + term
    return total


def routing_of(info, slots):
    devices = info.shape[0]
    owners = lax.broadcasted_iota(jnp.int32, (devices, 128), 1).astype(F32)
    routes = []
    total = jnp.zeros((1, 128), F32)
    for slot in range(slots):
        coef = (
            info[:, slot : slot + 1]
            + info[:, slots + slot : slots + slot + 1]
            + info[:, 2 * slots + slot : 2 * slots + slot + 1]
        )
        target = info[:, 3 * slots + slot : 3 * slots + slot + 1]
        route = jnp.where(target == owners, coef, 0.0)
        routes.append(route)
        total = total + jnp.sum(route, axis=0, keepdims=True)
    return routes, jnp.maximum(total, 1.0)


def scaled_rows(cot, denominator):
    rows = []
    for owner in range(cot.shape[0]):
        value = LOSS_SCALE * cot[owner : owner + 1] / denominator[:, owner : owner + 1]
        rows.append(value.astype(BF16).astype(F32))
    return rows


def info_row(coefs, targets, lanes):
    slots = len(coefs)
    lane = lax.broadcasted_iota(jnp.int32, (1, lanes), 1)
    value = jnp.zeros((1, lanes), F32)
    for slot in range(slots):
        for part in range(3):
            value = jnp.where(lane == part * slots + slot, coefs[slot], value)
        value = jnp.where(lane == 3 * slots + slot, targets[slot].astype(F32), value)
    high = value.astype(BF16).astype(F32)
    middle = (value - high).astype(BF16).astype(F32)
    low = (value - high - middle).astype(BF16).astype(F32)
    value = jnp.where((lane >= slots) & (lane < 2 * slots), middle, high)
    return jnp.where((lane >= 2 * slots) & (lane < 3 * slots), low, value)


def own_row(coefs, targets):
    slots = len(coefs)
    lane = lax.broadcasted_iota(jnp.int32, (1, 128), 1)
    value = jnp.zeros((1, 128), F32)
    for slot in range(slots):
        value = jnp.where(lane == slot, coefs[slot], value)
        value = jnp.where(lane == slots + slot, targets[slot].astype(F32), value)
    return value


def own_route(own, slots, owner):
    return [
        jnp.where(own[:, slots + slot : slots + slot + 1] == owner, own[:, slot : slot + 1], 0.0)
        for slot in range(slots)
    ]


def pack_kernel(
    packed, counts_ref, weights_ref, slide_ref, owner_ref, x_ref, cot_ref, out_ref, info_ref, own_ref
):
    devices, slots, side, _, lanes = out_ref.shape
    coefs, targets = own_scalars(counts_ref, weights_ref, slide_ref, owner_ref, slots)
    info = info_row(coefs, targets, info_ref.shape[1])
    info_ref[...] = info
    own_ref[...] = own_row(coefs, targets)
    cot = cot_ref[0].astype(F32)
    for slot in range(slots):
        for high in range(side):
            index = slot * side + high
            rows = x_ref[0, slot, high].astype(F32)
            if packed and index < devices:
                spare = cot[:, index * lanes : (index + 1) * lanes]
            elif packed and index == devices:
                spare = info[:, :lanes]
            else:
                spare = jnp.zeros((1, lanes), F32)
            for device in range(devices):
                part = rows[:, device * lanes : (device + 1) * lanes]
                out_ref[device, slot, high] = jnp.concatenate([part, spare], axis=0).astype(BF16)


def local_kernel(my_ref, own_ref, x_ref, w_ref, slope_ref, *refs):
    *share_refs, rows_ref = refs
    step = pl.program_id(0)
    side, kept, lanes = slope_ref.shape
    slots = kept // ROW
    devices = len(share_refs) * share_refs[0].shape[0]
    pitch = rows_ref.shape[1] // (side + 2)
    width = w_ref.shape[1]
    for col in range(3):
        rows_ref[col, pl.ds(0, pitch), :] = jnp.zeros((pitch, lanes), BF16)
        rows_ref[col, pl.ds((side + 1) * pitch, pitch), :] = jnp.zeros((pitch, lanes), BF16)
    for high in range(side):
        pieces = []
        for slot in range(slots):
            pieces += [x_ref[0, slot, high].astype(F32), jnp.zeros((ROW - side, lanes), F32)]
        if pitch > kept:
            pieces.append(jnp.zeros((pitch - kept, lanes), F32))
        for col, rows in enumerate(shifted(jnp.concatenate(pieces, axis=0))):
            rows_ref[col, pl.ds((high + 1) * pitch, pitch), :] = rows
    mask = diagonal_mask(lanes, width)
    pre = conv_taps(
        rows_ref,
        lambda tap: block_diagonal(w_ref[tap], mask),
        pitch,
        side * pitch,
        False,
        (((1,), (0,)), ((), ())),
    )
    sigma = jax.nn.sigmoid(pre)
    slope = sigma * (1.0 + pre * (1.0 - sigma))
    active = pre * sigma
    total = active[:pitch]
    slope_ref[0] = slope[:kept]
    for high in range(1, side):
        slope_ref[high] = slope[high * pitch : high * pitch + kept]
        total = total + active[high * pitch : (high + 1) * pitch]
    place = lax.broadcasted_iota(jnp.int32, (ROW, lanes), 0)
    own = own_ref[...]
    means = []
    for slot in range(slots):
        here = jnp.where(place < side, total[slot * ROW : (slot + 1) * ROW], 0.0)
        mean = jnp.sum(here, axis=0, keepdims=True) / (side * side)
        means.append(mean.astype(BF16).astype(F32))
    for index in range(devices):
        owner = index if len(share_refs) == 1 else my_ref[0] ^ index
        share = jnp.zeros((1, lanes), F32)
        for mean, weight in zip(means, own_route(own, slots, jnp.float32(owner))):
            share = share + weight * mean
        place_ref = share_refs[index % len(share_refs)]
        place_ref[index // len(share_refs), pl.ds(step, 1), :] = share


def weight_kernel(packed, my_ref, got_ref, w_ref, *refs):
    if packed:
        out_ref, rows_ref, grad_ref = refs
    else:
        cot_ref, info_ref, out_ref, rows_ref, grad_ref = refs
    devices, slots, side, _, lanes = got_ref.shape
    width = w_ref.shape[1]
    part = devices * ROW
    pitch = slots * part
    if packed:
        mine = my_ref[0]
        cot = got_ref[:, mine // side, mine % side].astype(F32)[:, ROW - 1, :]
        info = got_ref[:, devices // side, devices % side].astype(F32)[:, ROW - 1, :]
    else:
        cot = cot_ref[...]
        info = info_ref[...]
    routes, denominator = routing_of(info, slots)
    scaled = scaled_rows(cot, denominator)
    place = lax.broadcasted_iota(jnp.int32, (devices, ROW, lanes), 1)
    tile_grads = []
    for slot in range(slots):
        rows = jnp.zeros((devices, lanes), F32)
        for owner in range(devices):
            rows = rows + routes[slot][:, owner : owner + 1] * scaled[owner]
        spread = jnp.broadcast_to(rows[:, None, :], (devices, ROW, lanes)) / (side * side)
        tile_grads.append(jnp.where(place < side, spread, 0.0).reshape(part, lanes))
    tile_grad = jnp.concatenate(tile_grads, axis=0)

    zero = jnp.zeros((pitch, lanes), BF16)
    for col in range(3):
        rows_ref[col, pl.ds(0, pitch), :] = zero
        rows_ref[col, pl.ds((side + 1) * pitch, pitch), :] = zero
    grad_ref[pl.ds(0, pitch), :] = zero
    grad_ref[pl.ds((side + 1) * pitch, pitch), :] = zero
    for high in range(side):
        for slot in range(slots):
            rows = jnp.where(place < side, got_ref[:, slot, high].astype(F32), 0.0)
            for col, moved in enumerate(shifted(rows.reshape(part, lanes))):
                rows_ref[col, pl.ds((high + 1) * pitch + slot * part, part), :] = moved
    mask = diagonal_mask(lanes, width) if lanes > width else None
    pre = conv_taps(
        rows_ref,
        lambda tap: block_diagonal(w_ref[tap], mask),
        pitch,
        side * pitch,
        False,
        (((1,), (0,)), ((), ())),
    )
    sigma = jax.nn.sigmoid(pre)
    slope = sigma * (1.0 + pre * (1.0 - sigma))
    for high in range(side):
        here = slope[high * pitch : (high + 1) * pitch] * tile_grad
        grad_ref[pl.ds((high + 1) * pitch, pitch), :] = here.astype(BF16)
    group = lax.broadcasted_iota(jnp.int32, (width, lanes), 1) // width
    for offset in range(9):
        row_off, col_off = divmod(offset, 3)
        product = lax.dot_general(
            rows_ref[col_off, pl.ds(pitch, side * pitch), :],
            grad_ref[pl.ds((2 - row_off) * pitch, side * pitch), :],
            (((0,), (0,)), ((), ())),
            preferred_element_type=F32,
        )
        result = product[:width]
        for index in range(1, lanes // width):
            result = jnp.where(group == index, product[index * width : (index + 1) * width], result)
        out_ref[offset] = result


def input_kernel(
    packed,
    my_ref,
    own_ref,
    slope_ref,
    w_ref,
    cot_ref,
    info_ref,
    *refs,
):
    *share_refs, out_ref, pooled_ref, rows_ref = refs
    step = pl.program_id(0)
    side, kept, lanes = slope_ref.shape
    slots = kept // ROW
    devices = cot_ref.shape[0]
    pitch = rows_ref.shape[1] // (side + 2)
    width = w_ref.shape[1]
    if packed:
        cot = cot_ref[:, 0, 0].astype(F32)[:, ROW - 1, :]
        info = info_ref[:, 0, 0].astype(F32)[:, ROW - 1, :]
    else:
        cot = cot_ref[...]
        info = info_ref[...]
    _, denominator = routing_of(info, slots)
    scaled = scaled_rows(cot, denominator)
    owners = lax.broadcasted_iota(jnp.int32, (1, 128), 1)
    mine = jnp.sum(jnp.where(owners == my_ref[0], denominator, 0.0), axis=1, keepdims=True)
    shares = [jnp.sum(ref[:, pl.ds(step, 1), :], axis=0) for ref in share_refs]
    pooled_ref[0] = sum(shares[1:], shares[0]) / mine

    place = lax.broadcasted_iota(jnp.int32, (ROW, lanes), 0)
    own = own_ref[...]
    pieces = []
    sums = [jnp.zeros((1, lanes), F32)] * slots
    for owner in range(devices):
        weights = own_route(own, slots, owner)
        sums = [sums[slot] + weights[slot] * scaled[owner] for slot in range(slots)]
    for slot in range(slots):
        spread = jnp.broadcast_to(sums[slot], (ROW, lanes)) / (side * side)
        pieces.append(jnp.where(place < side, spread, 0.0))
    tile_grad = jnp.concatenate(pieces, axis=0)

    for col in range(3):
        rows_ref[col, pl.ds(0, pitch), :] = jnp.zeros((pitch, lanes), BF16)
        rows_ref[col, pl.ds((side + 1) * pitch, pitch), :] = jnp.zeros((pitch, lanes), BF16)
    for high in range(side):
        rows = slope_ref[high] * tile_grad
        if pitch > kept:
            rows = jnp.concatenate([rows, jnp.zeros((pitch - kept, lanes), F32)], axis=0)
        for col, moved in enumerate(shifted(rows)):
            rows_ref[col, pl.ds((high + 1) * pitch, pitch), :] = moved
    mask = diagonal_mask(lanes, width)
    total = conv_taps(
        rows_ref,
        lambda tap: block_diagonal(w_ref[tap], mask),
        pitch,
        side * pitch,
        True,
        (((1,), (1,)), ((), ())),
    )
    for high in range(side):
        for slot in range(slots):
            start = high * pitch + slot * ROW
            for wide in range(side):
                out_ref[slot, high, wide] = total[start + wide : start + wide + 1]


def params(mebibytes):
    return pltpu.CompilerParams(vmem_limit_bytes=mebibytes * 2**20)


def cost(flops, moved):
    return pl.CostEstimate(flops=flops, bytes_accessed=moved, transcendentals=0)


def swap(value, axis, step):
    return lax.ppermute(value, axis, [(i, i ^ step) for i in range(lax.axis_size(axis))])


def shards(tiles, tile_counts, tile_weights, slide_of, owner_map, cotangent, conv_weight):
    _, slots, side, _, channels = tiles.shape
    taps, width, _ = conv_weight.shape
    devices = lax.axis_size("tile")
    lanes = channels // devices
    blocks = channels // BLOCK
    mine = lax.axis_index("tile").astype(jnp.int32).reshape(1)
    slides = slide_of[:, :, 0]
    packed = lanes == BLOCK and devices + 1 <= slots * side
    scalars = (tile_counts, tile_weights, slides, owner_map)
    kept = slots * ROW
    pitch = -(-kept // 16) * 16
    macs = slots * side * side * taps * width * channels

    chunks, info, routes = pl.pallas_call(
        functools.partial(pack_kernel, packed),
        out_shape=(
            jax.ShapeDtypeStruct((devices, slots, side, ROW, lanes), BF16),
            jax.ShapeDtypeStruct((1, max(lanes, 128)), F32),
            jax.ShapeDtypeStruct((1, 128), F32),
        ),
        in_specs=[smem_whole()] * 4 + [vmem_whole()] * 2,
        out_specs=(vmem_whole(), vmem_whole(), vmem_whole()),
        compiler_params=params(56),
    )(*scalars, tiles, cotangent)
    got = lax.all_to_all(chunks, "tile", 0, 0, tiled=True)

    halves = 2 if packed else 1
    slope, *sent = pl.pallas_call(
        local_kernel,
        grid=(blocks,),
        out_shape=(
            jax.ShapeDtypeStruct((side, kept, channels), F32),
        )
        + (jax.ShapeDtypeStruct((devices // halves, blocks, BLOCK), F32),) * halves,
        in_specs=[
            smem_whole(),
            pl.BlockSpec((1, 128), lambda j: (0, 0)),
            pl.BlockSpec((1, slots, side, side, BLOCK), lambda j: (0, 0, 0, 0, j)),
            pl.BlockSpec((taps, width, BLOCK), lambda j: (0, 0, j)),
        ],
        out_specs=(
            pl.BlockSpec((side, kept, BLOCK), lambda j: (0, 0, j)),
        )
        + (pl.BlockSpec((devices // halves, blocks, BLOCK), lambda j: (0, 0, 0)),) * halves,
        scratch_shapes=[pltpu.VMEM((3, (side + 2) * pitch, BLOCK), BF16)],
        compiler_params=params(56),
        cost_estimate=cost(8 * macs, 4 * 2**20),
    )(mine, routes, tiles, conv_weight)
    if packed:
        toward = sent[0] + swap(sent[1], "tile", 1)
    else:
        toward = sent[0]

    got, slope, _ = lax.optimization_barrier((got, slope, toward))
    if packed:
        shares = [toward[:1]]
        shares += [swap(toward[i : i + 1], "tile", 2 * i) for i in range(1, devices // 2)]
    else:
        shares = [lax.all_to_all(toward, "tile", 0, 0, tiled=True)]

    own_weight = lax.dynamic_slice_in_dim(conv_weight, mine[0] * lanes, lanes, 2)
    if packed:
        extra = ()
        cot_args = (got, got)
        cot_specs = [
            pl.BlockSpec((devices, 1, 1, ROW, lanes), lambda j: (0, j // side, j % side, 0, 0)),
            pl.BlockSpec(
                (devices, 1, 1, ROW, lanes), lambda j: (0, devices // side, devices % side, 0, 0)
            ),
        ]
    else:
        cot_all = lax.all_gather(cotangent[0], "tile", axis=0, tiled=True).astype(F32)
        info_all = lax.all_gather(info, "tile", axis=0, tiled=True)
        extra = (lax.dynamic_slice_in_dim(cot_all, mine[0] * lanes, lanes, 1), info_all)
        cot_args = (cot_all, info_all)
        cot_specs = [
            pl.BlockSpec((devices, BLOCK), lambda j: (0, j)),
            pl.BlockSpec((devices, 128), lambda j: (0, 0)),
        ]
    pitch_all = slots * devices * ROW
    terms = pl.pallas_call(
        functools.partial(weight_kernel, packed),
        out_shape=jax.ShapeDtypeStruct((taps, width, lanes), F32),
        in_specs=[smem_whole()] + [vmem_whole()] * (2 + len(extra)),
        out_specs=vmem_whole(),
        scratch_shapes=[
            pltpu.VMEM((3, (side + 2) * pitch_all, lanes), BF16),
            pltpu.VMEM(((side + 2) * pitch_all, lanes), BF16),
        ],
        compiler_params=params(32),
        cost_estimate=cost(16 * macs, 4 * 2**20),
    )(mine, got, own_weight, *extra)

    terms, shares = lax.optimization_barrier((terms, shares))
    total = terms + swap(terms, "slide", 1)
    step = 2
    while step < lax.axis_size("slide"):
        sent = total.astype(BF16)
        total = sent.astype(F32) + swap(sent, "slide", step).astype(F32)
        step *= 2
    weight_grads = total / LOSS_SCALE

    grads, pooled = pl.pallas_call(
        functools.partial(input_kernel, packed),
        grid=(blocks,),
        out_shape=(
            jax.ShapeDtypeStruct((slots, side, side, 1, channels), F32),
            jax.ShapeDtypeStruct((1, 1, channels), F32),
        ),
        in_specs=[
            smem_whole(),
            pl.BlockSpec((1, 128), lambda j: (0, 0)),
            pl.BlockSpec((side, kept, BLOCK), lambda j: (0, 0, j)),
            pl.BlockSpec((taps, width, BLOCK), lambda j: (0, 0, j)),
        ]
        + cot_specs
        + [pl.BlockSpec((part.shape[0], blocks, BLOCK), lambda j: (0, 0, 0)) for part in shares],
        out_specs=(
            pl.BlockSpec((slots, side, side, 1, BLOCK), lambda j: (0, 0, 0, 0, j)),
            pl.BlockSpec((1, 1, BLOCK), lambda j: (0, 0, j)),
        ),
        scratch_shapes=[pltpu.VMEM((3, (side + 2) * pitch, BLOCK), BF16)],
        compiler_params=params(24),
        cost_estimate=cost(8 * macs, 4 * 2**20),
    )(mine, routes, slope, conv_weight, *cot_args, *shares)
    input_grads = jnp.transpose(grads, (3, 0, 1, 2, 4))
    return (pooled, input_grads, weight_grads)


def solution(mesh):
    return jax.shard_map(
        shards,
        mesh=mesh,
        in_specs=(
            P("slide", "tile", None, None, None),
            P("slide", "tile"),
            P("slide", "tile"),
            P("slide", "tile", None),
            P("slide", None),
            P("slide", "tile", None),
            P(),
        ),
        out_specs=(
            P("slide", "tile", None),
            P("slide", "tile", None, None, None),
            P(None, None, "tile"),
        ),
        check_vma=False,
    )
```

```python
import functools

import jax
import jax.numpy as jnp
from jax import lax
from jax.experimental import pallas as pl
from jax.experimental.pallas import tpu as pltpu
from jax.sharding import PartitionSpec as P

LOSS_SCALE = 512.0
BLOCK = 256
STEP = 512
ROW = 8
F32 = jnp.float32
BF16 = jnp.bfloat16


def vmem_whole():
    return pl.BlockSpec(memory_space=pltpu.VMEM)


def smem_whole():
    return pl.BlockSpec(memory_space=pltpu.SMEM)


def own_scalars(counts_ref, weights_ref, slide_ref, owner_ref, slots):
    coefs, targets = [], []
    for slot in range(slots):
        live = counts_ref[0, 0] > slot
        coefs.append(jnp.where(live, weights_ref[0, slot], 0.0))
        targets.append(owner_ref[0, slide_ref[0, slot]])
    return coefs, targets


def block_diagonal(tap, mask):
    width, channels = tap.shape
    if channels == width:
        return tap
    return jnp.concatenate([tap] * (channels // width), axis=0) * mask


def diagonal_mask(channels, width):
    row = lax.broadcasted_iota(jnp.int32, (channels, channels), 0) // width
    col = lax.broadcasted_iota(jnp.int32, (channels, channels), 1) // width
    return (row == col).astype(F32).astype(BF16)


def shifted(rows):
    count = rows.shape[0]
    return (
        pltpu.roll(rows, 1, 0).astype(BF16),
        rows.astype(BF16),
        pltpu.roll(rows, count - 1, 0).astype(BF16),
    )


def conv_taps(rows_ref, weight_of, pitch, count, flip, dims):
    total = None
    for offset in range(9):
        row_off, col_off = divmod(offset, 3)
        if flip:
            row_off, col_off = 2 - row_off, 2 - col_off
        rows = rows_ref[col_off, pl.ds(row_off * pitch, count), :]
        term = lax.dot_general(rows, weight_of(offset), dims, preferred_element_type=F32)
        total = term if total is None else total + term
    return total


def left_half(count):
    return lax.broadcasted_iota(jnp.int32, (count, 128), 1) < 64


def split(low, middle, high):
    left = left_half(low.shape[0])
    turned = pltpu.roll(middle, 64, 1)
    first = (jnp.where(left, low, turned), jnp.where(left, high, 0.0))
    second = (jnp.where(left, turned, low), jnp.where(left, 0.0, high))
    return tuple(jnp.concatenate(parts, axis=1).astype(BF16) for parts in (first, second))


def joined(first, second):
    left = left_half(first.shape[0])
    low = jnp.where(left, first[:, :128], second[:, :128])
    middle = pltpu.roll(jnp.where(left, second[:, :128], first[:, :128]), 64, 1)
    high = jnp.where(left, first[:, 128:], second[:, 128:])
    return low, middle, high


def pair_weights(w_ref, lanes, backward):
    rows = []
    for outer in (-1, 0, 1):
        taps = []
        for inner in (-1, 0, 1):
            row, col = (-outer, -inner) if backward else (inner, outer)
            taps.append(w_ref[3 * (row + 1) + col + 1, :, lanes].astype(F32))
        rows.append(split(*taps))
    empty = jnp.zeros(rows[0][0].shape, BF16)
    first = jnp.concatenate([rows[0][0], rows[1][0], rows[2][0], empty], axis=0)
    second = jnp.concatenate([rows[1][1], rows[0][1], empty, rows[2][1]], axis=0)
    return first, second


def pair_rows(rows):
    return split(pltpu.roll(rows, 1, 0), rows, pltpu.roll(rows, rows.shape[0] - 1, 0))


def pair_conv(first, second, weights, pitch, dims):
    first = lax.dot_general(first, weights[0], dims, preferred_element_type=F32)
    second = lax.dot_general(second, weights[1], dims, preferred_element_type=F32)
    side = first.shape[0] // pitch
    parts = []
    for high in range(side):
        span = slice(high * pitch, (high + 1) * pitch)
        parts.append(joined(first[span], second[span]))
    sums = []
    for high in range(side):
        total = parts[high][1]
        if high > 0:
            total = total + parts[high - 1][0]
        if high + 1 < side:
            total = total + parts[high + 1][2]
        sums.append(total)
    return sums


def slope_of(pre):
    sigma = jax.nn.sigmoid(pre)
    return sigma, sigma * (1.0 + pre * (1.0 - sigma))


PLAIN = (((1,), (0,)), ((), ()))
TURNED = (((1,), (1,)), ((), ()))


def routing_of(info, slots):
    devices = info.shape[0]
    owners = lax.broadcasted_iota(jnp.int32, (devices, 128), 1).astype(F32)
    routes = []
    total = jnp.zeros((1, 128), F32)
    for slot in range(slots):
        coef = (
            info[:, slot : slot + 1]
            + info[:, slots + slot : slots + slot + 1]
            + info[:, 2 * slots + slot : 2 * slots + slot + 1]
        )
        target = info[:, 3 * slots + slot : 3 * slots + slot + 1]
        route = jnp.where(target == owners, coef, 0.0)
        routes.append(route)
        total = total + jnp.sum(route, axis=0, keepdims=True)
    return routes, jnp.maximum(total, 1.0)


def scaled_rows(cot, denominator):
    rows = []
    for owner in range(cot.shape[0]):
        value = LOSS_SCALE * cot[owner : owner + 1] / denominator[:, owner : owner + 1]
        rows.append(value.astype(BF16).astype(F32))
    return rows


def info_row(coefs, targets, lanes):
    slots = len(coefs)
    lane = lax.broadcasted_iota(jnp.int32, (1, lanes), 1)
    value = jnp.zeros((1, lanes), F32)
    for slot in range(slots):
        for part in range(3):
            value = jnp.where(lane == part * slots + slot, coefs[slot], value)
        value = jnp.where(lane == 3 * slots + slot, targets[slot].astype(F32), value)
    high = value.astype(BF16).astype(F32)
    middle = (value - high).astype(BF16).astype(F32)
    low = (value - high - middle).astype(BF16).astype(F32)
    value = jnp.where((lane >= slots) & (lane < 2 * slots), middle, high)
    return jnp.where((lane >= 2 * slots) & (lane < 3 * slots), low, value)


def own_row(coefs, targets):
    slots = len(coefs)
    lane = lax.broadcasted_iota(jnp.int32, (1, 128), 1)
    value = jnp.zeros((1, 128), F32)
    for slot in range(slots):
        value = jnp.where(lane == slot, coefs[slot], value)
        value = jnp.where(lane == slots + slot, targets[slot].astype(F32), value)
    return value


def own_route(own, slots, owner):
    return [
        jnp.where(own[:, slots + slot : slots + slot + 1] == owner, own[:, slot : slot + 1], 0.0)
        for slot in range(slots)
    ]


def pack_kernel(
    packed, counts_ref, weights_ref, slide_ref, owner_ref, x_ref, cot_ref, out_ref, info_ref, own_ref
):
    devices, slots, side, _, lanes = out_ref.shape
    coefs, targets = own_scalars(counts_ref, weights_ref, slide_ref, owner_ref, slots)
    info = info_row(coefs, targets, info_ref.shape[1])
    info_ref[...] = info
    own_ref[...] = own_row(coefs, targets)
    cot = cot_ref[0].astype(F32)
    for slot in range(slots):
        for high in range(side):
            index = slot * side + high
            rows = x_ref[0, slot, high].astype(F32)
            if packed and index < devices:
                spare = cot[:, index * lanes : (index + 1) * lanes]
            elif packed and index == devices:
                spare = info[:, :lanes]
            else:
                spare = jnp.zeros((1, lanes), F32)
            for device in range(devices):
                part = rows[:, device * lanes : (device + 1) * lanes]
                out_ref[device, slot, high] = jnp.concatenate([part, spare], axis=0).astype(BF16)


def local_kernel(my_ref, own_ref, x_ref, w_ref, slope_ref, *share_refs):
    step = pl.program_id(0)
    side, kept, lanes = slope_ref.shape
    slots = kept // ROW
    devices = len(share_refs) * share_refs[0].shape[0]
    pitch = -(-kept // 16) * 16
    totals = []
    for pair in range(lanes // 128):
        span = pl.ds(pair * 128, 128)
        firsts, seconds = [], []
        for high in range(side):
            pieces = []
            for slot in range(slots):
                pieces += [x_ref[0, slot, high, :, span].astype(F32), jnp.zeros((ROW - side, 128), F32)]
            if pitch > kept:
                pieces.append(jnp.zeros((pitch - kept, 128), F32))
            first, second = pair_rows(jnp.concatenate(pieces, axis=0))
            firsts.append(first)
            seconds.append(second)
        weights = pair_weights(w_ref, span, False)
        pres = pair_conv(
            jnp.concatenate(firsts, axis=0), jnp.concatenate(seconds, axis=0), weights, pitch, PLAIN
        )
        total = jnp.zeros((kept, 128), F32)
        for high in range(side):
            pre = pres[high][:kept]
            sigma, slope = slope_of(pre)
            slope_ref[high, :, span] = slope
            total = total + pre * sigma
        totals.append(total)
    total = jnp.concatenate(totals, axis=1)
    place = lax.broadcasted_iota(jnp.int32, (ROW, lanes), 0)
    own = own_ref[...]
    means = []
    for slot in range(slots):
        here = jnp.where(place < side, total[slot * ROW : (slot + 1) * ROW], 0.0)
        mean = jnp.sum(here, axis=0, keepdims=True) / (side * side)
        means.append(mean.astype(BF16).astype(F32))
    for index in range(devices):
        owner = index if len(share_refs) == 1 else my_ref[0] ^ index
        share = jnp.zeros((1, lanes), F32)
        for mean, weight in zip(means, own_route(own, slots, jnp.float32(owner))):
            share = share + weight * mean
        place_ref = share_refs[index % len(share_refs)]
        for part in range(lanes // BLOCK):
            at = pl.ds(step * (lanes // BLOCK) + part, 1)
            place_ref[index // len(share_refs), at, :] = share[:, part * BLOCK : (part + 1) * BLOCK]


def weight_kernel(packed, my_ref, got_ref, w_ref, *refs):
    if packed:
        out_ref, rows_ref, grad_ref = refs
    else:
        cot_ref, info_ref, out_ref, rows_ref, grad_ref = refs
    devices, slots, side, _, lanes = got_ref.shape
    width = w_ref.shape[1]
    part = devices * ROW
    pitch = slots * part
    if packed:
        mine = my_ref[0]
        cot = got_ref[:, mine // side, mine % side].astype(F32)[:, ROW - 1, :]
        info = got_ref[:, devices // side, devices % side].astype(F32)[:, ROW - 1, :]
    else:
        cot = cot_ref[...]
        info = info_ref[...]
    routes, denominator = routing_of(info, slots)
    scaled = scaled_rows(cot, denominator)
    place = lax.broadcasted_iota(jnp.int32, (devices, ROW, lanes), 1)
    tile_grads = []
    for slot in range(slots):
        rows = jnp.zeros((devices, lanes), F32)
        for owner in range(devices):
            rows = rows + routes[slot][:, owner : owner + 1] * scaled[owner]
        spread = jnp.broadcast_to(rows[:, None, :], (devices, ROW, lanes)) / (side * side)
        tile_grads.append(jnp.where(place < side, spread, 0.0).reshape(part, lanes))
    tile_grad = jnp.concatenate(tile_grads, axis=0)

    if lanes % 128 == 0:
        for pair in range(lanes // 128):
            span = pl.ds(pair * 128, 128)
            for high in range(side):
                rows = []
                for slot in range(slots):
                    here = jnp.where(place[:, :, :128] < side, got_ref[:, slot, high, :, span].astype(F32), 0.0)
                    rows.append(here.reshape(part, 128))
                first, second = pair_rows(jnp.concatenate(rows, axis=0))
                rows_ref[0, pl.ds(high * pitch, pitch), :] = first
                rows_ref[1, pl.ds(high * pitch, pitch), :] = second
            first, second = rows_ref[0, :, :], rows_ref[1, :, :]
            pres = pair_conv(first, second, pair_weights(w_ref, span, False), pitch, PLAIN)
            grads = [slope_of(pre)[1] * tile_grad[:, pair * 128 : (pair + 1) * 128] for pre in pres]
            none = jnp.zeros((pitch, 128), F32)
            for high in range(side):
                after = grads[high + 1] if high + 1 < side else none
                before = grads[high - 1] if high > 0 else none
                moved = split(after, grads[high], before)
                for index in range(2):
                    grad_ref[index, pl.ds(high * pitch, pitch), :] = moved[index]
            products = [
                lax.dot_general(
                    rows_ref[index, :, :], grad_ref[index, :, :], (((0,), (0,)), ((), ())),
                    preferred_element_type=F32,
                )
                for index in range(2)
            ]
            for col, quarter, other in ((0, 0, 1), (1, 1, 0), (2, 2, 3)):
                taps = joined(
                    products[0][quarter * width : (quarter + 1) * width],
                    products[1][other * width : (other + 1) * width],
                )
                for row in range(3):
                    out_ref[3 * row + col, :, span] = taps[row].astype(BF16)
        return

    zero = jnp.zeros((pitch, lanes), BF16)
    for col in range(3):
        rows_ref[col, pl.ds(0, pitch), :] = zero
        rows_ref[col, pl.ds((side + 1) * pitch, pitch), :] = zero
    grad_ref[pl.ds(0, pitch), :] = zero
    grad_ref[pl.ds((side + 1) * pitch, pitch), :] = zero
    for high in range(side):
        for slot in range(slots):
            rows = jnp.where(place < side, got_ref[:, slot, high].astype(F32), 0.0)
            for col, moved in enumerate(shifted(rows.reshape(part, lanes))):
                rows_ref[col, pl.ds((high + 1) * pitch + slot * part, part), :] = moved
    mask = diagonal_mask(lanes, width) if lanes > width else None
    pre = conv_taps(
        rows_ref,
        lambda tap: block_diagonal(w_ref[tap], mask),
        pitch,
        side * pitch,
        False,
        (((1,), (0,)), ((), ())),
    )
    sigma = jax.nn.sigmoid(pre)
    slope = sigma * (1.0 + pre * (1.0 - sigma))
    for high in range(side):
        here = slope[high * pitch : (high + 1) * pitch] * tile_grad
        grad_ref[pl.ds((high + 1) * pitch, pitch), :] = here.astype(BF16)
    group = lax.broadcasted_iota(jnp.int32, (width, lanes), 1) // width
    for offset in range(9):
        row_off, col_off = divmod(offset, 3)
        product = lax.dot_general(
            rows_ref[col_off, pl.ds(pitch, side * pitch), :],
            grad_ref[pl.ds((2 - row_off) * pitch, side * pitch), :],
            (((0,), (0,)), ((), ())),
            preferred_element_type=F32,
        )
        result = product[:width]
        for index in range(1, lanes // width):
            result = jnp.where(group == index, product[index * width : (index + 1) * width], result)
        out_ref[offset] = result.astype(BF16)


def input_kernel(
    packed,
    my_ref,
    own_ref,
    slope_ref,
    w_ref,
    info_ref,
    *refs,
):
    *refs, out_ref, pooled_ref = refs
    step = pl.program_id(0)
    side, kept, lanes = slope_ref.shape
    slots = kept // ROW
    devices = info_ref.shape[0]
    pitch = -(-kept // 16) * 16
    cot_refs, share_refs = refs[: lanes // BLOCK], refs[lanes // BLOCK :]
    if packed:
        cot = jnp.concatenate(
            [ref[:, 0, 0].astype(F32)[:, ROW - 1, :] for ref in cot_refs], axis=1
        )
        info = info_ref[:, 0, 0].astype(F32)[:, ROW - 1, :]
    else:
        cot = jnp.concatenate([ref[...] for ref in cot_refs], axis=1)
        info = info_ref[...]
    _, denominator = routing_of(info, slots)
    scaled = scaled_rows(cot, denominator)
    owners = lax.broadcasted_iota(jnp.int32, (1, 128), 1)
    mine = jnp.sum(jnp.where(owners == my_ref[0], denominator, 0.0), axis=1, keepdims=True)
    for part in range(lanes // BLOCK):
        at = pl.ds(step * (lanes // BLOCK) + part, 1)
        shares = [jnp.sum(ref[:, at, :], axis=0) for ref in share_refs]
        pooled_ref[0, :, part * BLOCK : (part + 1) * BLOCK] = sum(shares[1:], shares[0]) / mine

    place = lax.broadcasted_iota(jnp.int32, (ROW, lanes), 0)
    own = own_ref[...]
    pieces = []
    sums = [jnp.zeros((1, lanes), F32)] * slots
    for owner in range(devices):
        weights = own_route(own, slots, owner)
        sums = [sums[slot] + weights[slot] * scaled[owner] for slot in range(slots)]
    for slot in range(slots):
        spread = jnp.broadcast_to(sums[slot], (ROW, lanes)) / (side * side)
        pieces.append(jnp.where(place < side, spread, 0.0))
    tile_grad = jnp.concatenate(pieces, axis=0)

    for pair in range(lanes // 128):
        span = pl.ds(pair * 128, 128)
        firsts, seconds = [], []
        for high in range(side):
            rows = slope_ref[high, :, span] * tile_grad[:, pair * 128 : (pair + 1) * 128]
            if pitch > kept:
                rows = jnp.concatenate([rows, jnp.zeros((pitch - kept, 128), F32)], axis=0)
            first, second = pair_rows(rows)
            firsts.append(first)
            seconds.append(second)
        weights = pair_weights(w_ref, span, True)
        sums = pair_conv(
            jnp.concatenate(firsts, axis=0), jnp.concatenate(seconds, axis=0), weights, pitch, TURNED
        )
        for high in range(side):
            for slot in range(slots):
                for wide in range(side):
                    at = slot * ROW + wide
                    out_ref[slot, high, wide, :, span] = sums[high][at : at + 1]


def params(mebibytes):
    return pltpu.CompilerParams(vmem_limit_bytes=mebibytes * 2**20)


def cost(flops, moved):
    return pl.CostEstimate(flops=flops, bytes_accessed=moved, transcendentals=0)


def swap(value, axis, step):
    return lax.ppermute(value, axis, [(i, i ^ step) for i in range(lax.axis_size(axis))])


def sum_over_slide(terms, beside):
    count = lax.axis_size("slide")
    total = terms.astype(F32) + swap(terms, "slide", 1).astype(F32)
    step = 2
    while step < count:
        sent = total.astype(BF16)
        if 2 * step < count:
            other = swap(sent, "slide", step)
        else:
            half = sent.shape[1] // 2
            second = lax.axis_index("slide") % 2 == 1
            part = swap(jnp.where(second, sent[:, half:], sent[:, :half]), "slide", step)
            part, beside = lax.optimization_barrier((part, beside))
            rest = swap(part, "slide", 1)
            low = jnp.where(second, rest, part)
            other = jnp.concatenate([low, jnp.where(second, part, rest)], axis=1)
        total = sent.astype(F32) + other.astype(F32)
        step *= 2
    return total, beside


def shards(tiles, tile_counts, tile_weights, slide_of, owner_map, cotangent, conv_weight):
    _, slots, side, _, channels = tiles.shape
    taps, width, _ = conv_weight.shape
    devices = lax.axis_size("tile")
    lanes = channels // devices
    blocks = channels // BLOCK
    mine = lax.axis_index("tile").astype(jnp.int32).reshape(1)
    slides = slide_of[:, :, 0]
    packed = lanes == BLOCK and devices + 1 <= slots * side
    scalars = (tile_counts, tile_weights, slides, owner_map)
    kept = slots * ROW
    macs = slots * side * side * taps * width * channels

    chunks, info, routes = pl.pallas_call(
        functools.partial(pack_kernel, packed),
        out_shape=(
            jax.ShapeDtypeStruct((devices, slots, side, ROW, lanes), BF16),
            jax.ShapeDtypeStruct((1, max(lanes, 128)), F32),
            jax.ShapeDtypeStruct((1, 128), F32),
        ),
        in_specs=[smem_whole()] * 4 + [vmem_whole()] * 2,
        out_specs=(vmem_whole(), vmem_whole(), vmem_whole()),
        compiler_params=params(56),
    )(*scalars, tiles, cotangent)
    got = lax.all_to_all(chunks, "tile", 0, 0, tiled=True)

    halves = 2 if packed else 1
    slope, *sent = pl.pallas_call(
        local_kernel,
        grid=(channels // STEP,),
        out_shape=(
            jax.ShapeDtypeStruct((side, kept, channels), F32),
        )
        + (jax.ShapeDtypeStruct((devices // halves, blocks, BLOCK), F32),) * halves,
        in_specs=[
            smem_whole(),
            pl.BlockSpec((1, 128), lambda j: (0, 0)),
            pl.BlockSpec((1, slots, side, side, STEP), lambda j: (0, 0, 0, 0, j)),
            pl.BlockSpec((taps, width, STEP), lambda j: (0, 0, j)),
        ],
        out_specs=(
            pl.BlockSpec((side, kept, STEP), lambda j: (0, 0, j)),
        )
        + (pl.BlockSpec((devices // halves, blocks, BLOCK), lambda j: (0, 0, 0)),) * halves,
        compiler_params=params(56),
        cost_estimate=cost(8 * macs, 4 * 2**20),
    )(mine, routes, tiles, conv_weight)
    if packed:
        toward = sent[0] + swap(sent[1], "tile", 1)
    else:
        toward = sent[0]

    got, slope, _ = lax.optimization_barrier((got, slope, toward))
    if packed:
        shares = [toward[:1]]
        shares += [swap(toward[i : i + 1], "tile", 2 * i) for i in range(1, devices // 2)]
    else:
        shares = [lax.all_to_all(toward, "tile", 0, 0, tiled=True)]

    if packed:
        extra = ()
        cot_args = (got,) * (1 + STEP // BLOCK)
        cot_specs = [
            pl.BlockSpec(
                (devices, 1, 1, ROW, lanes), lambda j: (0, devices // side, devices % side, 0, 0)
            )
        ]
        for part in range(STEP // BLOCK):
            cot_specs.append(
                pl.BlockSpec(
                    (devices, 1, 1, ROW, lanes),
                    lambda j, part=part: (
                        0,
                        (j * (STEP // BLOCK) + part) // side,
                        (j * (STEP // BLOCK) + part) % side,
                        0,
                        0,
                    ),
                )
            )
    else:
        cot_all = lax.all_gather(cotangent[0], "tile", axis=0, tiled=True).astype(F32)
        info_all = lax.all_gather(info, "tile", axis=0, tiled=True)
        extra = (lax.dynamic_slice_in_dim(cot_all, mine[0] * lanes, lanes, 1), info_all)
        cot_args = (info_all,) + (cot_all,) * (STEP // BLOCK)
        cot_specs = [pl.BlockSpec((devices, 128), lambda j: (0, 0))]
        for part in range(STEP // BLOCK):
            cot_specs.append(
                pl.BlockSpec((devices, BLOCK), lambda j, part=part: (0, j * (STEP // BLOCK) + part))
            )
    pitch_all = slots * devices * ROW
    if lanes % 128 == 0:
        scratch = [pltpu.VMEM((2, side * pitch_all, BLOCK), BF16)] * 2
    else:
        scratch = [
            pltpu.VMEM((3, (side + 2) * pitch_all, lanes), BF16),
            pltpu.VMEM(((side + 2) * pitch_all, lanes), BF16),
        ]
    if packed:
        weight_spec = pl.BlockSpec((taps, width, lanes), lambda j, my: (0, 0, my[0]))
        weight = conv_weight
    else:
        weight_spec = pl.BlockSpec((taps, width, lanes), lambda j, my: (0, 0, 0))
        weight = lax.dynamic_slice_in_dim(conv_weight, mine[0] * lanes, lanes, 2)
    whole = lambda value: pl.BlockSpec(value.shape, lambda j, my: (0,) * value.ndim)
    terms = pl.pallas_call(
        functools.partial(weight_kernel, packed),
        out_shape=jax.ShapeDtypeStruct((taps, width, lanes), BF16),
        grid_spec=pltpu.PrefetchScalarGridSpec(
            num_scalar_prefetch=1,
            grid=(1,),
            in_specs=[whole(got), weight_spec] + [whole(value) for value in extra],
            out_specs=pl.BlockSpec((taps, width, lanes), lambda j, my: (0, 0, 0)),
            scratch_shapes=scratch,
        ),
        compiler_params=params(48),
        cost_estimate=cost(16 * macs, 4 * 2**20),
    )(mine, got, weight, *extra)

    terms, shares = lax.optimization_barrier((terms, shares))
    grads, pooled = pl.pallas_call(
        functools.partial(input_kernel, packed),
        grid=(channels // STEP,),
        out_shape=(
            jax.ShapeDtypeStruct((slots, side, side, 1, channels), F32),
            jax.ShapeDtypeStruct((1, 1, channels), F32),
        ),
        in_specs=[
            smem_whole(),
            pl.BlockSpec((1, 128), lambda j: (0, 0)),
            pl.BlockSpec((side, kept, STEP), lambda j: (0, 0, j)),
            pl.BlockSpec((taps, width, STEP), lambda j: (0, 0, j)),
        ]
        + cot_specs
        + [pl.BlockSpec((part.shape[0], blocks, BLOCK), lambda j: (0, 0, 0)) for part in shares],
        out_specs=(
            pl.BlockSpec((slots, side, side, 1, STEP), lambda j: (0, 0, 0, 0, j)),
            pl.BlockSpec((1, 1, STEP), lambda j: (0, 0, j)),
        ),
        compiler_params=params(56),
        cost_estimate=cost(8 * macs, 4 * 2**20),
    )(mine, routes, slope, conv_weight, *cot_args, *shares)
    total, (grads, pooled) = sum_over_slide(terms, (grads, pooled))
    weight_grads = total / LOSS_SCALE
    input_grads = jnp.transpose(grads, (3, 0, 1, 2, 4))
    return (pooled, input_grads, weight_grads)


def solution(mesh):
    return jax.shard_map(
        shards,
        mesh=mesh,
        in_specs=(
            P("slide", "tile", None, None, None),
            P("slide", "tile"),
            P("slide", "tile"),
            P("slide", "tile", None),
            P("slide", None),
            P("slide", "tile", None),
            P(),
        ),
        out_specs=(
            P("slide", "tile", None),
            P("slide", "tile", None, None, None),
            P(None, None, "tile"),
        ),
        check_vma=False,
    )
```

```python
import functools

import jax
import jax.numpy as jnp
from jax import lax
from jax.experimental import pallas as pl
from jax.experimental.pallas import tpu as pltpu
from jax.sharding import PartitionSpec as P

LOSS_SCALE = 512.0
BLOCK = 256
STEP = 1024
ROW = 8
F32 = jnp.float32
BF16 = jnp.bfloat16


def vmem_whole():
    return pl.BlockSpec(memory_space=pltpu.VMEM)


def smem_whole():
    return pl.BlockSpec(memory_space=pltpu.SMEM)


def own_scalars(counts_ref, weights_ref, slide_ref, owner_ref, slots):
    coefs, targets = [], []
    for slot in range(slots):
        live = counts_ref[0, 0] > slot
        coefs.append(jnp.where(live, weights_ref[0, slot], 0.0))
        targets.append(owner_ref[0, slide_ref[0, slot]])
    return coefs, targets


def block_diagonal(tap, mask):
    width, channels = tap.shape
    if channels == width:
        return tap
    return jnp.concatenate([tap] * (channels // width), axis=0) * mask


def diagonal_mask(channels, width):
    row = lax.broadcasted_iota(jnp.int32, (channels, channels), 0) // width
    col = lax.broadcasted_iota(jnp.int32, (channels, channels), 1) // width
    return (row == col).astype(F32).astype(BF16)


def shifted(rows):
    count = rows.shape[0]
    return (
        pltpu.roll(rows, 1, 0).astype(BF16),
        rows.astype(BF16),
        pltpu.roll(rows, count - 1, 0).astype(BF16),
    )


def conv_taps(rows_ref, weight_of, pitch, count, flip, dims):
    total = None
    for offset in range(9):
        row_off, col_off = divmod(offset, 3)
        if flip:
            row_off, col_off = 2 - row_off, 2 - col_off
        rows = rows_ref[col_off, pl.ds(row_off * pitch, count), :]
        term = lax.dot_general(rows, weight_of(offset), dims, preferred_element_type=F32)
        total = term if total is None else total + term
    return total


def left_half(count):
    return lax.broadcasted_iota(jnp.int32, (count, 128), 1) < 64


def split(low, middle, high):
    left = left_half(low.shape[0])
    turned = pltpu.roll(middle, 64, 1)
    first = (jnp.where(left, low, turned), jnp.where(left, high, 0.0))
    second = (jnp.where(left, turned, low), jnp.where(left, 0.0, high))
    return tuple(jnp.concatenate(parts, axis=1).astype(BF16) for parts in (first, second))


def joined(first, second):
    left = left_half(first.shape[0])
    low = jnp.where(left, first[:, :128], second[:, :128])
    middle = pltpu.roll(jnp.where(left, second[:, :128], first[:, :128]), 64, 1)
    high = jnp.where(left, first[:, 128:], second[:, 128:])
    return low, middle, high


def pair_weights(w_ref, lanes, backward):
    rows = []
    for outer in (-1, 0, 1):
        taps = []
        for inner in (-1, 0, 1):
            row, col = (-outer, -inner) if backward else (inner, outer)
            taps.append(w_ref[3 * (row + 1) + col + 1, :, lanes].astype(F32))
        rows.append(split(*taps))
    empty = jnp.zeros(rows[0][0].shape, BF16)
    first = jnp.concatenate([rows[0][0], rows[1][0], rows[2][0], empty], axis=0)
    second = jnp.concatenate([rows[1][1], rows[0][1], empty, rows[2][1]], axis=0)
    return first, second


def pair_rows(rows):
    return split(pltpu.roll(rows, 1, 0), rows, pltpu.roll(rows, rows.shape[0] - 1, 0))


def pair_conv(first, second, weights, pitch, dims):
    first = lax.dot_general(first, weights[0], dims, preferred_element_type=F32)
    second = lax.dot_general(second, weights[1], dims, preferred_element_type=F32)
    side = first.shape[0] // pitch
    parts = []
    for high in range(side):
        span = slice(high * pitch, (high + 1) * pitch)
        parts.append(joined(first[span], second[span]))
    sums = []
    for high in range(side):
        total = parts[high][1]
        if high > 0:
            total = total + parts[high - 1][0]
        if high + 1 < side:
            total = total + parts[high + 1][2]
        sums.append(total)
    return sums


def slope_of(pre):
    sigma = jax.nn.sigmoid(pre)
    return sigma, sigma * (1.0 + pre * (1.0 - sigma))


PLAIN = (((1,), (0,)), ((), ()))
TURNED = (((1,), (1,)), ((), ()))


def routing_of(info, slots):
    devices = info.shape[0]
    owners = lax.broadcasted_iota(jnp.int32, (devices, 128), 1).astype(F32)
    routes = []
    total = jnp.zeros((1, 128), F32)
    for slot in range(slots):
        coef = (
            info[:, slot : slot + 1]
            + info[:, slots + slot : slots + slot + 1]
            + info[:, 2 * slots + slot : 2 * slots + slot + 1]
        )
        target = info[:, 3 * slots + slot : 3 * slots + slot + 1]
        route = jnp.where(target == owners, coef, 0.0)
        routes.append(route)
        total = total + jnp.sum(route, axis=0, keepdims=True)
    return routes, jnp.maximum(total, 1.0)


def scaled_rows(cot, denominator, base=0):
    owners = cot.shape[0]
    same = (lax.broadcasted_iota(jnp.int32, (owners, 128), 0) ^ base) == lax.broadcasted_iota(
        jnp.int32, (owners, 128), 1
    )
    column = jnp.sum(jnp.where(same, denominator, 0.0), axis=1, keepdims=True)
    return (LOSS_SCALE * cot / column).astype(BF16).astype(F32)


def info_row(coefs, targets, lanes):
    slots = len(coefs)
    lane = lax.broadcasted_iota(jnp.int32, (1, lanes), 1)
    value = jnp.zeros((1, lanes), F32)
    for slot in range(slots):
        for part in range(3):
            value = jnp.where(lane == part * slots + slot, coefs[slot], value)
        value = jnp.where(lane == 3 * slots + slot, targets[slot].astype(F32), value)
    high = value.astype(BF16).astype(F32)
    middle = (value - high).astype(BF16).astype(F32)
    low = (value - high - middle).astype(BF16).astype(F32)
    value = jnp.where((lane >= slots) & (lane < 2 * slots), middle, high)
    return jnp.where((lane >= 2 * slots) & (lane < 3 * slots), low, value)


def own_row(coefs, targets):
    slots = len(coefs)
    lane = lax.broadcasted_iota(jnp.int32, (1, 128), 1)
    value = jnp.zeros((1, 128), F32)
    for slot in range(slots):
        value = jnp.where(lane == slot, coefs[slot], value)
        value = jnp.where(lane == slots + slot, targets[slot].astype(F32), value)
    return value


def own_route(own, slots, owner):
    return [
        jnp.where(own[:, slots + slot : slots + slot + 1] == owner, own[:, slot : slot + 1], 0.0)
        for slot in range(slots)
    ]


def pack_kernel(
    counts_ref,
    weights_ref,
    slide_ref,
    owner_ref,
    x_ref,
    cot_ref,
    out_ref,
    own_ref,
    flat_ref,
):
    devices, groups, _, lanes = out_ref.shape
    _, slots, side, _, channels = x_ref.shape
    rows = slots * side * side
    for index in range(slots * side):
        values = x_ref[0, index // side, index % side].astype(F32)
        flat_ref[pl.ds(index * side, side), :] = values
    flat_ref[pl.ds(rows, 1), :] = cot_ref[0].astype(F32)
    coefs, targets = own_scalars(counts_ref, weights_ref, slide_ref, owner_ref, slots)
    own_ref[...] = own_row(coefs, targets)
    info = info_row(coefs, targets, lanes)
    flat_ref[pl.ds(rows + 1, 1), :] = jnp.concatenate([info] * devices, axis=1)
    spare = groups * ROW - rows - 2
    flat_ref[pl.ds(rows + 2, spare), :] = jnp.zeros((spare, channels), F32)
    for device in range(devices):
        part = flat_ref[:, pl.ds(device * lanes, lanes)].astype(BF16)
        out_ref[device] = part.reshape(groups, ROW, lanes)


def local_kernel(my_ref, own_ref, cot_ref, x_ref, w_ref, slope_ref, *share_refs):
    step = pl.program_id(0)
    side, kept, lanes = slope_ref.shape
    slots = kept // ROW
    devices = len(share_refs) * (share_refs[0].shape[0] - 1)
    totals = []
    for pair in range(lanes // 128):
        span = pl.ds(pair * 128, 128)
        pieces = []
        for high in range(side):
            for slot in range(slots):
                pieces += [x_ref[0, slot, high, :, span].astype(F32), jnp.zeros((ROW - side, 128), F32)]
        first, second = pair_rows(jnp.concatenate(pieces, axis=0))
        pres = pair_conv(first, second, pair_weights(w_ref, span, False), kept, PLAIN)
        total = jnp.zeros((kept, 128), F32)
        for high in range(side):
            pre = pres[high]
            sigma, slope = slope_of(pre)
            slope_ref[high, :, span] = slope
            total = total + pre * sigma
        totals.append(total)
    total = jnp.concatenate(totals, axis=1)
    place = lax.broadcasted_iota(jnp.int32, (ROW, lanes), 0)
    own = own_ref[...]
    means = []
    for slot in range(slots):
        here = jnp.where(place < side, total[slot * ROW : (slot + 1) * ROW], 0.0)
        mean = jnp.sum(here, axis=0, keepdims=True) / (side * side)
        means.append(mean.astype(BF16).astype(F32))
    for index in range(devices):
        owner = index if len(share_refs) == 1 else my_ref[0] ^ index
        share = jnp.zeros((1, lanes), F32)
        for mean, weight in zip(means, own_route(own, slots, jnp.float32(owner))):
            share = share + weight * mean
        place_ref = share_refs[index % len(share_refs)]
        for part in range(lanes // BLOCK):
            at = pl.ds(step * (lanes // BLOCK) + part, 1)
            place_ref[index // len(share_refs), at, :] = share[:, part * BLOCK : (part + 1) * BLOCK]
    for part in range(lanes // BLOCK):
        at = pl.ds(step * (lanes // BLOCK) + part, 1)
        for place_ref in share_refs:
            span = slice(part * BLOCK, (part + 1) * BLOCK)
            place_ref[devices // len(share_refs), at, :] = cot_ref[0, :, span].astype(F32)


def weight_kernel(packed, side, my_ref, got_ref, w_ref, out_ref, rows_ref, grad_ref, flat_ref):
    del my_ref
    devices, groups, _, lanes = got_ref.shape
    slots = groups * ROW // (side * side)
    width = w_ref.shape[1]
    part = devices * ROW
    pitch = slots * part
    flat_ref[...] = got_ref[...].astype(F32).reshape(devices, groups * ROW, lanes)
    cot = flat_ref[:, slots * side * side, :]
    info = flat_ref[:, slots * side * side + 1, :]
    routes, denominator = routing_of(info, slots)
    scaled = scaled_rows(cot, denominator)
    place = lax.broadcasted_iota(jnp.int32, (devices, ROW, lanes), 1)
    tile_grads = []
    for slot in range(slots):
        rows = jnp.zeros((devices, lanes), F32)
        for owner in range(devices):
            rows = rows + routes[slot][:, owner : owner + 1] * scaled[owner : owner + 1]
        spread = jnp.broadcast_to(rows[:, None, :], (devices, ROW, lanes)) / (side * side)
        tile_grads.append(jnp.where(place < side, spread, 0.0).reshape(part, lanes))
    tile_grad = jnp.concatenate(tile_grads, axis=0)

    if packed:
        for pair in range(lanes // 128):
            span = pl.ds(pair * 128, 128)
            for high in range(side):
                rows = []
                for slot in range(slots):
                    here = flat_ref[:, pl.ds((slot * side + high) * side, ROW), span]
                    here = jnp.where(place[:, :, :128] < side, here, 0.0)
                    rows.append(here.reshape(part, 128))
                first, second = pair_rows(jnp.concatenate(rows, axis=0))
                rows_ref[0, pl.ds(high * pitch, pitch), :] = first
                rows_ref[1, pl.ds(high * pitch, pitch), :] = second
            first, second = rows_ref[0, :, :], rows_ref[1, :, :]
            pres = pair_conv(first, second, pair_weights(w_ref, span, False), pitch, PLAIN)
            grads = [slope_of(pre)[1] * tile_grad[:, pair * 128 : (pair + 1) * 128] for pre in pres]
            none = jnp.zeros((pitch, 128), F32)
            for high in range(side):
                after = grads[high + 1] if high + 1 < side else none
                before = grads[high - 1] if high > 0 else none
                moved = split(after, grads[high], before)
                for index in range(2):
                    grad_ref[index, pl.ds(high * pitch, pitch), :] = moved[index]
            products = [
                lax.dot_general(
                    rows_ref[index, :, :], grad_ref[index, :, :], (((0,), (0,)), ((), ())),
                    preferred_element_type=F32,
                )
                for index in range(2)
            ]
            for col, quarter, other in ((0, 0, 1), (1, 1, 0), (2, 2, 3)):
                taps = joined(
                    products[0][quarter * width : (quarter + 1) * width],
                    products[1][other * width : (other + 1) * width],
                )
                for row in range(3):
                    out_ref[3 * row + col, :, span] = taps[row].astype(BF16)
        return

    zero = jnp.zeros((pitch, lanes), BF16)
    for col in range(3):
        rows_ref[col, pl.ds(0, pitch), :] = zero
        rows_ref[col, pl.ds((side + 1) * pitch, pitch), :] = zero
    grad_ref[pl.ds(0, pitch), :] = zero
    grad_ref[pl.ds((side + 1) * pitch, pitch), :] = zero
    for high in range(side):
        for slot in range(slots):
            here = flat_ref[:, pl.ds((slot * side + high) * side, ROW), :]
            rows = jnp.where(place < side, here, 0.0)
            for col, moved in enumerate(shifted(rows.reshape(part, lanes))):
                rows_ref[col, pl.ds((high + 1) * pitch + slot * part, part), :] = moved
    mask = diagonal_mask(lanes, width) if lanes > width else None
    pre = conv_taps(
        rows_ref,
        lambda tap: block_diagonal(w_ref[tap], mask),
        pitch,
        side * pitch,
        False,
        (((1,), (0,)), ((), ())),
    )
    sigma = jax.nn.sigmoid(pre)
    slope = sigma * (1.0 + pre * (1.0 - sigma))
    for high in range(side):
        here = slope[high * pitch : (high + 1) * pitch] * tile_grad
        grad_ref[pl.ds((high + 1) * pitch, pitch), :] = here.astype(BF16)
    group = lax.broadcasted_iota(jnp.int32, (width, lanes), 1) // width
    for offset in range(9):
        row_off, col_off = divmod(offset, 3)
        product = lax.dot_general(
            rows_ref[col_off, pl.ds(pitch, side * pitch), :],
            grad_ref[pl.ds((2 - row_off) * pitch, side * pitch), :],
            (((0,), (0,)), ((), ())),
            preferred_element_type=F32,
        )
        result = product[:width]
        for index in range(1, lanes // width):
            result = jnp.where(group == index, product[index * width : (index + 1) * width], result)
        out_ref[offset] = result.astype(BF16)


def input_kernel(
    packed,
    my_ref,
    own_ref,
    slope_ref,
    w_ref,
    info_ref,
    *refs,
):
    *refs, out_ref, pooled_ref = refs
    step = pl.program_id(0)
    side, kept, lanes = slope_ref.shape
    slots = kept // ROW
    devices = info_ref.shape[0]
    info = info_ref[:, 0].astype(F32)[:, (slots * side * side + 1) % ROW, :]
    _, denominator = routing_of(info, slots)
    owners = lax.broadcasted_iota(jnp.int32, (1, 128), 1)
    mine = jnp.sum(jnp.where(owners == my_ref[0], denominator, 0.0), axis=1, keepdims=True)
    base = my_ref[0] if packed else 0
    cots = []
    for part in range(lanes // BLOCK):
        at = pl.ds(step * (lanes // BLOCK) + part, 1)
        if packed:
            shares = [ref[0, at, :] for ref in refs]
            rows = [ref[row, at, :] for ref in refs for row in (1, 2)]
            cots.append(jnp.concatenate(rows, axis=0))
        else:
            shares = [jnp.sum(refs[0][:, at, :], axis=0)]
            cots.append(refs[1][:, at, :].reshape(devices, BLOCK))
        pooled_ref[0, :, part * BLOCK : (part + 1) * BLOCK] = sum(shares[1:], shares[0]) / mine
    scaled = scaled_rows(jnp.concatenate(cots, axis=1), denominator, base)

    place = lax.broadcasted_iota(jnp.int32, (ROW, lanes), 0)
    own = own_ref[...]
    pieces = []
    owner = (lax.broadcasted_iota(jnp.int32, (devices, 1), 0) ^ base).astype(F32)
    for weight in own_route(own, slots, owner):
        row = jnp.sum(weight * scaled, axis=0, keepdims=True)
        spread = jnp.broadcast_to(row, (ROW, lanes)) / (side * side)
        pieces.append(jnp.where(place < side, spread, 0.0))
    tile_grad = jnp.concatenate(pieces, axis=0)

    for pair in range(lanes // 128):
        span = pl.ds(pair * 128, 128)
        here = tile_grad[:, pair * 128 : (pair + 1) * 128]
        rows = jnp.concatenate([slope_ref[high, :, span] * here for high in range(side)], axis=0)
        first, second = pair_rows(rows)
        sums = pair_conv(first, second, pair_weights(w_ref, span, True), kept, TURNED)
        for high in range(side):
            for slot in range(slots):
                for wide in range(side):
                    at = slot * ROW + wide
                    out_ref[slot, high, wide, :, span] = sums[high][at : at + 1]


def params(mebibytes):
    return pltpu.CompilerParams(vmem_limit_bytes=mebibytes * 2**20)


def cost(flops, moved):
    return pl.CostEstimate(flops=flops, bytes_accessed=moved, transcendentals=0)


def swap(value, axis, step):
    return lax.ppermute(value, axis, [(i, i ^ step) for i in range(lax.axis_size(axis))])


def sum_over_slide(terms, beside):
    count = lax.axis_size("slide")
    second = lax.axis_index("slide") % 2 == 1
    low, high = jnp.split(terms, 2, axis=1)
    sent = swap(jnp.where(second, low, high), "slide", 1)
    total = jnp.where(second, high, low).astype(F32) + sent.astype(F32)
    step = 2
    while step < count:
        sent = total.astype(BF16)
        other = swap(sent, "slide", step)
        if 2 * step >= count:
            other, beside = lax.optimization_barrier((other, beside))
        total = sent.astype(F32) + other.astype(F32)
        step *= 2
    half = total.astype(BF16)
    rest = swap(half, "slide", 1)
    whole = [jnp.where(second, rest, half), jnp.where(second, half, rest)]
    return jnp.concatenate(whole, axis=1).astype(F32), beside


def shards(tiles, tile_counts, tile_weights, slide_of, owner_map, cotangent, conv_weight):
    _, slots, side, _, channels = tiles.shape
    taps, width, _ = conv_weight.shape
    devices = lax.axis_size("tile")
    lanes = channels // devices
    blocks = channels // BLOCK
    mine = lax.axis_index("tile").astype(jnp.int32).reshape(1)
    slides = slide_of[:, :, 0]
    packed = lanes == BLOCK
    groups = -(-(slots * side * side + 2) // ROW)
    kept = slots * ROW
    macs = slots * side * side * taps * width * channels

    chunks, routes = pl.pallas_call(
        pack_kernel,
        out_shape=(
            jax.ShapeDtypeStruct((devices, groups, ROW, lanes), BF16),
            jax.ShapeDtypeStruct((1, 128), F32),
        ),
        in_specs=[smem_whole()] * 4 + [vmem_whole()] * 2,
        out_specs=(vmem_whole(), vmem_whole()),
        scratch_shapes=[pltpu.VMEM((groups * ROW, channels), F32)],
        compiler_params=params(56),
    )(tile_counts, tile_weights, slides, owner_map, tiles, cotangent)
    got = lax.all_to_all(chunks, "tile", 0, 0, tiled=True)

    halves = 2 if packed else 1
    slope, *sent = pl.pallas_call(
        local_kernel,
        grid=(channels // STEP,),
        out_shape=(
            jax.ShapeDtypeStruct((side, kept, channels), F32),
        )
        + (jax.ShapeDtypeStruct((devices // halves + 1, blocks, BLOCK), F32),) * halves,
        in_specs=[
            smem_whole(),
            pl.BlockSpec((1, 128), lambda j: (0, 0)),
            pl.BlockSpec((1, 1, STEP), lambda j: (0, 0, j)),
            pl.BlockSpec((1, slots, side, side, STEP), lambda j: (0, 0, 0, 0, j)),
            pl.BlockSpec((taps, width, STEP), lambda j: (0, 0, j)),
        ],
        out_specs=(
            pl.BlockSpec((side, kept, STEP), lambda j: (0, 0, j)),
        )
        + (pl.BlockSpec((devices // halves + 1, blocks, BLOCK), lambda j: (0, 0, 0)),) * halves,
        compiler_params=params(56),
        cost_estimate=cost(8 * macs, 4 * 2**20),
    )(mine, routes, cotangent, tiles, conv_weight)
    if packed:
        half = devices // 2
        other = swap(sent[1], "tile", 1)
        toward = sent[0][:half] + other[:half]
        cots = [sent[0][half:], other[half:]]
        toward = [jnp.concatenate([toward[i : i + 1], *cots]) for i in range(half)]
    else:
        toward = sent[0]
    got, slope, _ = lax.optimization_barrier((got, slope, toward))
    if packed:
        shares = toward[:1] + [swap(toward[i], "tile", 2 * i) for i in range(1, half)]
    else:
        shares = [lax.all_to_all(toward[:devices], "tile", 0, 0, tiled=True)]
        shares.append(lax.all_gather(toward[devices:], "tile", axis=0, tiled=True))
    info_block = (slots * side * side + 1) // ROW
    pitch_all = slots * devices * ROW
    if packed:
        scratch = [pltpu.VMEM((2, side * pitch_all, BLOCK), BF16)] * 2
    else:
        scratch = [
            pltpu.VMEM((3, (side + 2) * pitch_all, lanes), BF16),
            pltpu.VMEM(((side + 2) * pitch_all, lanes), BF16),
        ]
    scratch.append(pltpu.VMEM((devices, groups * ROW, lanes), F32))
    if packed:
        weight_spec = pl.BlockSpec((taps, width, lanes), lambda j, my: (0, 0, my[0]))
        weight = conv_weight
    else:
        weight_spec = pl.BlockSpec((taps, width, lanes), lambda j, my: (0, 0, 0))
        weight = lax.dynamic_slice_in_dim(conv_weight, mine[0] * lanes, lanes, 2)
    terms = pl.pallas_call(
        functools.partial(weight_kernel, packed, side),
        out_shape=jax.ShapeDtypeStruct((taps, width, lanes), BF16),
        grid_spec=pltpu.PrefetchScalarGridSpec(
            num_scalar_prefetch=1,
            grid=(1,),
            in_specs=[pl.BlockSpec(got.shape, lambda j, my: (0, 0, 0, 0)), weight_spec],
            out_specs=pl.BlockSpec((taps, width, lanes), lambda j, my: (0, 0, 0)),
            scratch_shapes=scratch,
        ),
        compiler_params=params(20),
        cost_estimate=cost(16 * macs, 4 * 2**20),
    )(mine, got, weight)

    terms, shares = lax.optimization_barrier((terms, shares))
    grads, pooled = pl.pallas_call(
        functools.partial(input_kernel, packed),
        grid=(channels // STEP,),
        out_shape=(
            jax.ShapeDtypeStruct((slots, side, side, 1, channels), F32),
            jax.ShapeDtypeStruct((1, 1, channels), F32),
        ),
        in_specs=[
            smem_whole(),
            pl.BlockSpec((1, 128), lambda j: (0, 0)),
            pl.BlockSpec((side, kept, STEP), lambda j: (0, 0, j)),
            pl.BlockSpec((taps, width, STEP), lambda j: (0, 0, j)),
            pl.BlockSpec((devices, 1, ROW, lanes), lambda j: (0, info_block, 0, 0)),
        ]
        + [pl.BlockSpec((part.shape[0], blocks, BLOCK), lambda j: (0, 0, 0)) for part in shares],
        out_specs=(
            pl.BlockSpec((slots, side, side, 1, STEP), lambda j: (0, 0, 0, 0, j)),
            pl.BlockSpec((1, 1, STEP), lambda j: (0, 0, j)),
        ),
        compiler_params=params(16),
        cost_estimate=cost(8 * macs, 4 * 2**20),
    )(
        mine,
        routes,
        pltpu.with_memory_space_constraint(slope, pltpu.HBM),
        conv_weight,
        got,
        *shares,
    )
    total, (grads, pooled) = sum_over_slide(terms, (grads, pooled))
    weight_grads = total / LOSS_SCALE
    input_grads = jnp.transpose(grads, (3, 0, 1, 2, 4))
    return (pooled, input_grads, weight_grads)


def solution(mesh):
    return jax.shard_map(
        shards,
        mesh=mesh,
        in_specs=(
            P("slide", "tile", None, None, None),
            P("slide", "tile"),
            P("slide", "tile"),
            P("slide", "tile", None),
            P("slide", None),
            P("slide", "tile", None),
            P(),
        ),
        out_specs=(
            P("slide", "tile", None),
            P("slide", "tile", None, None, None),
            P(None, None, "tile"),
        ),
        check_vma=False,
    )
```

```python
import functools

import jax
import jax.numpy as jnp
from jax import lax
from jax.experimental import pallas as pl
from jax.experimental.pallas import tpu as pltpu
from jax.sharding import PartitionSpec as P

LOSS_SCALE = 512.0
BLOCK = 256
STEP = 1024
ROW = 8
F32 = jnp.float32
BF16 = jnp.bfloat16


def vmem_whole():
    return pl.BlockSpec(memory_space=pltpu.VMEM)


def smem_whole():
    return pl.BlockSpec(memory_space=pltpu.SMEM)


def own_scalars(counts_ref, weights_ref, slide_ref, owner_ref, slots):
    coefs, targets = [], []
    for slot in range(slots):
        live = counts_ref[0, 0] > slot
        coefs.append(jnp.where(live, weights_ref[0, slot], 0.0))
        targets.append(owner_ref[0, slide_ref[0, slot]])
    return coefs, targets


def block_diagonal(tap, mask):
    width, channels = tap.shape
    if channels == width:
        return tap
    return jnp.concatenate([tap] * (channels // width), axis=0) * mask


def diagonal_mask(channels, width):
    row = lax.broadcasted_iota(jnp.int32, (channels, channels), 0) // width
    col = lax.broadcasted_iota(jnp.int32, (channels, channels), 1) // width
    return (row == col).astype(F32).astype(BF16)


def shifted(rows):
    count = rows.shape[0]
    return (
        pltpu.roll(rows, 1, 0).astype(BF16),
        rows.astype(BF16),
        pltpu.roll(rows, count - 1, 0).astype(BF16),
    )


def conv_taps(rows_ref, weight_of, pitch, count, flip, dims):
    total = None
    for offset in range(9):
        row_off, col_off = divmod(offset, 3)
        if flip:
            row_off, col_off = 2 - row_off, 2 - col_off
        rows = rows_ref[col_off, pl.ds(row_off * pitch, count), :]
        term = lax.dot_general(rows, weight_of(offset), dims, preferred_element_type=F32)
        total = term if total is None else total + term
    return total


def left_half(count):
    return lax.broadcasted_iota(jnp.int32, (count, 128), 1) < 64


def split(low, middle, high):
    left = left_half(low.shape[0])
    turned = pltpu.roll(middle, 64, 1)
    first = (jnp.where(left, low, turned), jnp.where(left, high, 0.0))
    second = (jnp.where(left, turned, low), jnp.where(left, 0.0, high))
    return tuple(jnp.concatenate(parts, axis=1).astype(BF16) for parts in (first, second))


def joined(first, second):
    left = left_half(first.shape[0])
    low = jnp.where(left, first[:, :128], second[:, :128])
    middle = pltpu.roll(jnp.where(left, second[:, :128], first[:, :128]), 64, 1)
    high = jnp.where(left, first[:, 128:], second[:, 128:])
    return low, middle, high


def pair_weights(w_ref, lanes, backward):
    rows = []
    for outer in (-1, 0, 1):
        taps = []
        for inner in (-1, 0, 1):
            row, col = (-outer, -inner) if backward else (inner, outer)
            taps.append(w_ref[3 * (row + 1) + col + 1, :, lanes].astype(F32))
        rows.append(split(*taps))
    empty = jnp.zeros(rows[0][0].shape, BF16)
    first = jnp.concatenate([rows[0][0], rows[1][0], rows[2][0], empty], axis=0)
    second = jnp.concatenate([rows[1][1], rows[0][1], empty, rows[2][1]], axis=0)
    return first, second


def pair_rows(rows):
    return split(pltpu.roll(rows, 1, 0), rows, pltpu.roll(rows, rows.shape[0] - 1, 0))


def pair_conv(first, second, weights, pitch, dims):
    first = lax.dot_general(first, weights[0], dims, preferred_element_type=F32)
    second = lax.dot_general(second, weights[1], dims, preferred_element_type=F32)
    side = first.shape[0] // pitch
    parts = []
    for high in range(side):
        span = slice(high * pitch, (high + 1) * pitch)
        parts.append(joined(first[span], second[span]))
    sums = []
    for high in range(side):
        total = parts[high][1]
        if high > 0:
            total = total + parts[high - 1][0]
        if high + 1 < side:
            total = total + parts[high + 1][2]
        sums.append(total)
    return sums


def slope_of(pre):
    sigma = jax.nn.sigmoid(pre)
    return sigma, sigma * (1.0 + pre * (1.0 - sigma))


PLAIN = (((1,), (0,)), ((), ()))
TURNED = (((1,), (1,)), ((), ()))


def routing_of(info, slots):
    devices = info.shape[0]
    owners = lax.broadcasted_iota(jnp.int32, (devices, 128), 1).astype(F32)
    routes = []
    total = jnp.zeros((1, 128), F32)
    for slot in range(slots):
        coef = (
            info[:, slot : slot + 1]
            + info[:, slots + slot : slots + slot + 1]
            + info[:, 2 * slots + slot : 2 * slots + slot + 1]
        )
        target = info[:, 3 * slots + slot : 3 * slots + slot + 1]
        route = jnp.where(target == owners, coef, 0.0)
        routes.append(route)
        total = total + jnp.sum(route, axis=0, keepdims=True)
    return routes, jnp.maximum(total, 1.0)


def scaled_rows(cot, denominator, base=0):
    owners = cot.shape[0]
    same = (lax.broadcasted_iota(jnp.int32, (owners, 128), 0) ^ base) == lax.broadcasted_iota(
        jnp.int32, (owners, 128), 1
    )
    column = jnp.sum(jnp.where(same, denominator, 0.0), axis=1, keepdims=True)
    return (LOSS_SCALE * cot / column).astype(BF16).astype(F32)


def info_row(coefs, targets, lanes):
    slots = len(coefs)
    lane = lax.broadcasted_iota(jnp.int32, (1, lanes), 1)
    value = jnp.zeros((1, lanes), F32)
    for slot in range(slots):
        for part in range(3):
            value = jnp.where(lane == part * slots + slot, coefs[slot], value)
        value = jnp.where(lane == 3 * slots + slot, targets[slot].astype(F32), value)
    high = value.astype(BF16).astype(F32)
    middle = (value - high).astype(BF16).astype(F32)
    low = (value - high - middle).astype(BF16).astype(F32)
    value = jnp.where((lane >= slots) & (lane < 2 * slots), middle, high)
    return jnp.where((lane >= 2 * slots) & (lane < 3 * slots), low, value)


def own_row(coefs, targets):
    slots = len(coefs)
    lane = lax.broadcasted_iota(jnp.int32, (1, 128), 1)
    value = jnp.zeros((1, 128), F32)
    for slot in range(slots):
        value = jnp.where(lane == slot, coefs[slot], value)
        value = jnp.where(lane == slots + slot, targets[slot].astype(F32), value)
    return value


def own_route(own, slots, owner):
    return [
        jnp.where(own[:, slots + slot : slots + slot + 1] == owner, own[:, slot : slot + 1], 0.0)
        for slot in range(slots)
    ]


def pack_kernel(
    counts_ref,
    weights_ref,
    slide_ref,
    owner_ref,
    x_ref,
    cot_ref,
    out_ref,
    own_ref,
    flat_ref,
):
    devices, groups, _, lanes = out_ref.shape
    _, slots, side, _, channels = x_ref.shape
    rows = slots * side * side
    for index in range(slots * side):
        values = x_ref[0, index // side, index % side].astype(F32)
        flat_ref[pl.ds(index * side, side), :] = values
    flat_ref[pl.ds(rows, 1), :] = cot_ref[0].astype(F32)
    coefs, targets = own_scalars(counts_ref, weights_ref, slide_ref, owner_ref, slots)
    own_ref[...] = own_row(coefs, targets)
    info = info_row(coefs, targets, lanes)
    flat_ref[pl.ds(rows + 1, 1), :] = jnp.concatenate([info] * devices, axis=1)
    spare = groups * ROW - rows - 2
    flat_ref[pl.ds(rows + 2, spare), :] = jnp.zeros((spare, channels), F32)
    for device in range(devices):
        part = flat_ref[:, pl.ds(device * lanes, lanes)].astype(BF16)
        out_ref[device] = part.reshape(groups, ROW, lanes)


def local_kernel(my_ref, own_ref, cot_ref, x_ref, w_ref, slope_ref, *share_refs):
    step = pl.program_id(0)
    side, kept, lanes = slope_ref.shape
    slots = kept // ROW
    devices = len(share_refs) * (share_refs[0].shape[0] - 1)
    totals = []
    for pair in range(lanes // 128):
        span = pl.ds(pair * 128, 128)
        pieces = []
        for high in range(side):
            for slot in range(slots):
                pieces += [x_ref[0, slot, high, :, span].astype(F32), jnp.zeros((ROW - side, 128), F32)]
        first, second = pair_rows(jnp.concatenate(pieces, axis=0))
        pres = pair_conv(first, second, pair_weights(w_ref, span, False), kept, PLAIN)
        total = jnp.zeros((kept, 128), F32)
        for high in range(side):
            pre = pres[high]
            sigma, slope = slope_of(pre)
            slope_ref[high, :, span] = slope
            total = total + pre * sigma
        totals.append(total)
    total = jnp.concatenate(totals, axis=1)
    place = lax.broadcasted_iota(jnp.int32, (ROW, lanes), 0)
    own = own_ref[...]
    means = []
    for slot in range(slots):
        here = jnp.where(place < side, total[slot * ROW : (slot + 1) * ROW], 0.0)
        mean = jnp.sum(here, axis=0, keepdims=True) / (side * side)
        means.append(mean.astype(BF16).astype(F32))
    for index in range(devices):
        owner = index if len(share_refs) == 1 else my_ref[0] ^ index
        share = jnp.zeros((1, lanes), F32)
        for mean, weight in zip(means, own_route(own, slots, jnp.float32(owner))):
            share = share + weight * mean
        place_ref = share_refs[index % len(share_refs)]
        for part in range(lanes // BLOCK):
            at = pl.ds(step * (lanes // BLOCK) + part, 1)
            place_ref[index // len(share_refs), at, :] = share[:, part * BLOCK : (part + 1) * BLOCK]
    for part in range(lanes // BLOCK):
        at = pl.ds(step * (lanes // BLOCK) + part, 1)
        for place_ref in share_refs:
            span = slice(part * BLOCK, (part + 1) * BLOCK)
            place_ref[devices // len(share_refs), at, :] = cot_ref[0, :, span].astype(F32)


def weight_kernel(packed, side, my_ref, got_ref, w_ref, out_ref, rows_ref, grad_ref, flat_ref):
    del my_ref
    devices, groups, _, lanes = got_ref.shape
    slots = groups * ROW // (side * side)
    width = w_ref.shape[1]
    part = devices * ROW
    pitch = slots * part
    flat_ref[...] = got_ref[...].astype(F32).reshape(devices, groups * ROW, lanes)
    tail = got_ref[:, groups - 1].astype(F32)
    cot = tail[:, slots * side * side % ROW, :]
    info = tail[:, slots * side * side % ROW + 1, :]
    routes, denominator = routing_of(info, slots)
    scaled = scaled_rows(cot, denominator)
    place = lax.broadcasted_iota(jnp.int32, (devices, ROW, lanes), 1)
    tile_grads = []
    for slot in range(slots):
        rows = jnp.zeros((devices, lanes), F32)
        for owner in range(devices):
            rows = rows + routes[slot][:, owner : owner + 1] * scaled[owner : owner + 1]
        spread = jnp.broadcast_to(rows[:, None, :], (devices, ROW, lanes)) / (side * side)
        tile_grads.append(jnp.where(place < side, spread, 0.0).reshape(part, lanes))
    tile_grad = jnp.concatenate(tile_grads, axis=0)

    if packed:
        for pair in range(lanes // 128):
            span = pl.ds(pair * 128, 128)
            for high in range(side):
                rows = []
                for slot in range(slots):
                    here = flat_ref[:, pl.ds((slot * side + high) * side, ROW), span]
                    here = jnp.where(place[:, :, :128] < side, here, 0.0)
                    rows.append(here.reshape(part, 128))
                first, second = pair_rows(jnp.concatenate(rows, axis=0))
                rows_ref[0, pl.ds(high * pitch, pitch), :] = first
                rows_ref[1, pl.ds(high * pitch, pitch), :] = second
            first, second = rows_ref[0, :, :], rows_ref[1, :, :]
            pres = pair_conv(first, second, pair_weights(w_ref, span, False), pitch, PLAIN)
            grads = [slope_of(pre)[1] * tile_grad[:, pair * 128 : (pair + 1) * 128] for pre in pres]
            none = jnp.zeros((pitch, 128), F32)
            turned = jnp.concatenate([none, *grads, none], axis=0).astype(BF16).T
            count = side * pitch
            products = []
            for index in range(2):
                low, middle, high = (
                    turned[index * width : (index + 1) * width, at * pitch : at * pitch + count]
                    for at in (2, 1, 0)
                )
                empty = jnp.zeros(low.shape, BF16)
                order = [middle, low, empty, high] if index else [low, middle, high, empty]
                product = jnp.dot(
                    jnp.concatenate(order, axis=0), rows_ref[index, :, :], preferred_element_type=F32
                )
                products.append(product.T)
            for col, quarter, other in ((0, 0, 1), (1, 1, 0), (2, 2, 3)):
                taps = joined(
                    products[0][quarter * width : (quarter + 1) * width],
                    products[1][other * width : (other + 1) * width],
                )
                for row in range(3):
                    out_ref[3 * row + col, :, span] = taps[row].astype(BF16)
        return

    zero = jnp.zeros((pitch, lanes), BF16)
    for col in range(3):
        rows_ref[col, pl.ds(0, pitch), :] = zero
        rows_ref[col, pl.ds((side + 1) * pitch, pitch), :] = zero
    grad_ref[pl.ds(0, pitch), :] = zero
    grad_ref[pl.ds((side + 1) * pitch, pitch), :] = zero
    for high in range(side):
        for slot in range(slots):
            here = flat_ref[:, pl.ds((slot * side + high) * side, ROW), :]
            rows = jnp.where(place < side, here, 0.0)
            for col, moved in enumerate(shifted(rows.reshape(part, lanes))):
                rows_ref[col, pl.ds((high + 1) * pitch + slot * part, part), :] = moved
    mask = diagonal_mask(lanes, width) if lanes > width else None
    pre = conv_taps(
        rows_ref,
        lambda tap: block_diagonal(w_ref[tap], mask),
        pitch,
        side * pitch,
        False,
        (((1,), (0,)), ((), ())),
    )
    sigma = jax.nn.sigmoid(pre)
    slope = sigma * (1.0 + pre * (1.0 - sigma))
    for high in range(side):
        here = slope[high * pitch : (high + 1) * pitch] * tile_grad
        grad_ref[pl.ds((high + 1) * pitch, pitch), :] = here.astype(BF16)
    group = lax.broadcasted_iota(jnp.int32, (width, lanes), 1) // width
    for offset in range(9):
        row_off, col_off = divmod(offset, 3)
        product = lax.dot_general(
            rows_ref[col_off, pl.ds(pitch, side * pitch), :],
            grad_ref[pl.ds((2 - row_off) * pitch, side * pitch), :],
            (((0,), (0,)), ((), ())),
            preferred_element_type=F32,
        )
        result = product[:width]
        for index in range(1, lanes // width):
            result = jnp.where(group == index, product[index * width : (index + 1) * width], result)
        out_ref[offset] = result.astype(BF16)


def input_kernel(
    packed,
    my_ref,
    own_ref,
    slope_ref,
    w_ref,
    info_ref,
    *refs,
):
    *refs, out_ref, pooled_ref = refs
    step = pl.program_id(0)
    side, kept, lanes = slope_ref.shape
    slots = kept // ROW
    devices = info_ref.shape[0]
    info = info_ref[:, 0].astype(F32)[:, (slots * side * side + 1) % ROW, :]
    _, denominator = routing_of(info, slots)
    owners = lax.broadcasted_iota(jnp.int32, (1, 128), 1)
    mine = jnp.sum(jnp.where(owners == my_ref[0], denominator, 0.0), axis=1, keepdims=True)
    base = my_ref[0] if packed else 0
    cots = []
    for part in range(lanes // BLOCK):
        at = pl.ds(step * (lanes // BLOCK) + part, 1)
        if packed:
            shares = [ref[0, at, :] for ref in refs]
            rows = [ref[row, at, :] for ref in refs for row in (1, 2)]
            cots.append(jnp.concatenate(rows, axis=0))
        else:
            shares = [jnp.sum(refs[0][:, at, :], axis=0)]
            cots.append(refs[1][:, at, :].reshape(devices, BLOCK))
        pooled_ref[0, :, part * BLOCK : (part + 1) * BLOCK] = sum(shares[1:], shares[0]) / mine
    scaled = scaled_rows(jnp.concatenate(cots, axis=1), denominator, base)

    place = lax.broadcasted_iota(jnp.int32, (ROW, lanes), 0)
    own = own_ref[...]
    pieces = []
    owner = (lax.broadcasted_iota(jnp.int32, (devices, 1), 0) ^ base).astype(F32)
    for weight in own_route(own, slots, owner):
        row = jnp.sum(weight * scaled, axis=0, keepdims=True)
        spread = jnp.broadcast_to(row, (ROW, lanes)) / (side * side)
        pieces.append(jnp.where(place < side, spread, 0.0))
    tile_grad = jnp.concatenate(pieces, axis=0)

    for pair in range(lanes // 128):
        span = pl.ds(pair * 128, 128)
        here = tile_grad[:, pair * 128 : (pair + 1) * 128]
        rows = jnp.concatenate([slope_ref[high, :, span] * here for high in range(side)], axis=0)
        first, second = pair_rows(rows)
        sums = pair_conv(first, second, pair_weights(w_ref, span, True), kept, TURNED)
        for high in range(side):
            for slot in range(slots):
                for wide in range(side):
                    at = slot * ROW + wide
                    out_ref[slot, high, wide, :, span] = sums[high][at : at + 1]


def params(mebibytes):
    return pltpu.CompilerParams(vmem_limit_bytes=mebibytes * 2**20)


def cost(flops, moved):
    return pl.CostEstimate(flops=flops, bytes_accessed=moved, transcendentals=0)


def swap(value, axis, step):
    return lax.ppermute(value, axis, [(i, i ^ step) for i in range(lax.axis_size(axis))])


def sum_over_slide(terms, beside):
    count = lax.axis_size("slide")
    second = lax.axis_index("slide") % 2 == 1
    low, high = jnp.split(terms, 2, axis=1)
    sent = swap(jnp.where(second, low, high), "slide", 1)
    total = jnp.where(second, high, low).astype(F32) + sent.astype(F32)
    step = 2
    while step < count:
        sent = total.astype(BF16)
        other = swap(sent, "slide", step)
        if 2 * step >= count:
            other, beside = lax.optimization_barrier((other, beside))
        total = sent.astype(F32) + other.astype(F32)
        step *= 2
    half = total.astype(BF16)
    rest = swap(half, "slide", 1)
    whole = [jnp.where(second, rest, half), jnp.where(second, half, rest)]
    return jnp.concatenate(whole, axis=1).astype(F32), beside


def shards(tiles, tile_counts, tile_weights, slide_of, owner_map, cotangent, conv_weight):
    _, slots, side, _, channels = tiles.shape
    taps, width, _ = conv_weight.shape
    devices = lax.axis_size("tile")
    lanes = channels // devices
    blocks = channels // BLOCK
    mine = lax.axis_index("tile").astype(jnp.int32).reshape(1)
    slides = slide_of[:, :, 0]
    packed = lanes == BLOCK
    groups = -(-(slots * side * side + 2) // ROW)
    kept = slots * ROW
    macs = slots * side * side * taps * width * channels

    chunks, routes = pl.pallas_call(
        pack_kernel,
        out_shape=(
            jax.ShapeDtypeStruct((devices, groups, ROW, lanes), BF16),
            jax.ShapeDtypeStruct((1, 128), F32),
        ),
        in_specs=[smem_whole()] * 4 + [vmem_whole()] * 2,
        out_specs=(vmem_whole(), vmem_whole()),
        scratch_shapes=[pltpu.VMEM((groups * ROW, channels), F32)],
        compiler_params=params(56),
    )(tile_counts, tile_weights, slides, owner_map, tiles, cotangent)
    got = lax.all_to_all(chunks, "tile", 0, 0, tiled=True)

    halves = 2 if packed else 1
    slope, *sent = pl.pallas_call(
        local_kernel,
        grid=(channels // STEP,),
        out_shape=(
            jax.ShapeDtypeStruct((side, kept, channels), F32),
        )
        + (jax.ShapeDtypeStruct((devices // halves + 1, blocks, BLOCK), F32),) * halves,
        in_specs=[
            smem_whole(),
            pl.BlockSpec((1, 128), lambda j: (0, 0)),
            pl.BlockSpec((1, 1, STEP), lambda j: (0, 0, j)),
            pl.BlockSpec((1, slots, side, side, STEP), lambda j: (0, 0, 0, 0, j)),
            pl.BlockSpec((taps, width, STEP), lambda j: (0, 0, j)),
        ],
        out_specs=(
            pl.BlockSpec((side, kept, STEP), lambda j: (0, 0, j)),
        )
        + (pl.BlockSpec((devices // halves + 1, blocks, BLOCK), lambda j: (0, 0, 0)),) * halves,
        compiler_params=params(56),
        cost_estimate=cost(8 * macs, 4 * 2**20),
    )(mine, routes, cotangent, tiles, conv_weight)
    if packed:
        half = devices // 2
        other = swap(sent[1], "tile", 1)
        toward = sent[0][:half] + other[:half]
        cots = [sent[0][half:], other[half:]]
        toward = [jnp.concatenate([toward[i : i + 1], *cots]) for i in range(half)]
    else:
        toward = sent[0]
    got, slope, _ = lax.optimization_barrier((got, slope, toward))
    if packed:
        shares = toward[:1] + [swap(toward[i], "tile", 2 * i) for i in range(1, half)]
    else:
        shares = [lax.all_to_all(toward[:devices], "tile", 0, 0, tiled=True)]
        shares.append(lax.all_gather(toward[devices:], "tile", axis=0, tiled=True))
    info_block = (slots * side * side + 1) // ROW
    pitch_all = slots * devices * ROW
    if packed:
        scratch = [pltpu.VMEM((2, side * pitch_all, BLOCK), BF16)] * 2
    else:
        scratch = [
            pltpu.VMEM((3, (side + 2) * pitch_all, lanes), BF16),
            pltpu.VMEM(((side + 2) * pitch_all, lanes), BF16),
        ]
    scratch.append(pltpu.VMEM((devices, groups * ROW, lanes), F32))
    if packed:
        weight_spec = pl.BlockSpec((taps, width, lanes), lambda j, my: (0, 0, my[0]))
        weight = conv_weight
    else:
        weight_spec = pl.BlockSpec((taps, width, lanes), lambda j, my: (0, 0, 0))
        weight = lax.dynamic_slice_in_dim(conv_weight, mine[0] * lanes, lanes, 2)
    terms = pl.pallas_call(
        functools.partial(weight_kernel, packed, side),
        out_shape=jax.ShapeDtypeStruct((taps, width, lanes), BF16),
        grid_spec=pltpu.PrefetchScalarGridSpec(
            num_scalar_prefetch=1,
            grid=(1,),
            in_specs=[pl.BlockSpec(got.shape, lambda j, my: (0, 0, 0, 0)), weight_spec],
            out_specs=pl.BlockSpec((taps, width, lanes), lambda j, my: (0, 0, 0)),
            scratch_shapes=scratch,
        ),
        compiler_params=params(20),
        cost_estimate=cost(16 * macs, 4 * 2**20),
    )(mine, got, weight)

    terms, shares = lax.optimization_barrier((terms, shares))
    grads, pooled = pl.pallas_call(
        functools.partial(input_kernel, packed),
        grid=(channels // STEP,),
        out_shape=(
            jax.ShapeDtypeStruct((slots, side, side, 1, channels), F32),
            jax.ShapeDtypeStruct((1, 1, channels), F32),
        ),
        in_specs=[
            smem_whole(),
            pl.BlockSpec((1, 128), lambda j: (0, 0)),
            pl.BlockSpec((side, kept, STEP), lambda j: (0, 0, j)),
            pl.BlockSpec((taps, width, STEP), lambda j: (0, 0, j)),
            pl.BlockSpec((devices, 1, ROW, lanes), lambda j: (0, info_block, 0, 0)),
        ]
        + [pl.BlockSpec((part.shape[0], blocks, BLOCK), lambda j: (0, 0, 0)) for part in shares],
        out_specs=(
            pl.BlockSpec((slots, side, side, 1, STEP), lambda j: (0, 0, 0, 0, j)),
            pl.BlockSpec((1, 1, STEP), lambda j: (0, 0, j)),
        ),
        compiler_params=params(16),
        cost_estimate=cost(8 * macs, 4 * 2**20),
    )(
        mine,
        routes,
        pltpu.with_memory_space_constraint(slope, pltpu.HBM),
        conv_weight,
        got,
        *shares,
    )
    total, (grads, pooled) = sum_over_slide(terms, (grads, pooled))
    weight_grads = total / LOSS_SCALE
    input_grads = jnp.transpose(grads, (3, 0, 1, 2, 4))
    return (pooled, input_grads, weight_grads)


def solution(mesh):
    return jax.shard_map(
        shards,
        mesh=mesh,
        in_specs=(
            P("slide", "tile", None, None, None),
            P("slide", "tile"),
            P("slide", "tile"),
            P("slide", "tile", None),
            P("slide", None),
            P("slide", "tile", None),
            P(),
        ),
        out_specs=(
            P("slide", "tile", None),
            P("slide", "tile", None, None, None),
            P(None, None, "tile"),
        ),
        check_vma=False,
    )
```

```python
import functools

import jax
import jax.numpy as jnp
from jax import lax
from jax.experimental import pallas as pl
from jax.experimental.pallas import tpu as pltpu
from jax.sharding import PartitionSpec as P

LOSS_SCALE = 512.0
BLOCK = 256
STEP = 1024
ROW = 8
F32 = jnp.float32
BF16 = jnp.bfloat16


def vmem_whole():
    return pl.BlockSpec(memory_space=pltpu.VMEM)


def smem_whole():
    return pl.BlockSpec(memory_space=pltpu.SMEM)


def own_scalars(counts_ref, weights_ref, slide_ref, owner_ref, slots):
    coefs, targets = [], []
    for slot in range(slots):
        live = counts_ref[0, 0] > slot
        coefs.append(jnp.where(live, weights_ref[0, slot], 0.0))
        targets.append(owner_ref[0, slide_ref[0, slot]])
    return coefs, targets


def block_diagonal(tap, mask):
    width, channels = tap.shape
    if channels == width:
        return tap
    return jnp.concatenate([tap] * (channels // width), axis=0) * mask


def diagonal_mask(channels, width):
    row = lax.broadcasted_iota(jnp.int32, (channels, channels), 0) // width
    col = lax.broadcasted_iota(jnp.int32, (channels, channels), 1) // width
    return (row == col).astype(F32).astype(BF16)


def shifted(rows):
    count = rows.shape[0]
    return (
        pltpu.roll(rows, 1, 0).astype(BF16),
        rows.astype(BF16),
        pltpu.roll(rows, count - 1, 0).astype(BF16),
    )


def conv_taps(rows_ref, weight_of, pitch, count, flip, dims):
    total = None
    for offset in range(9):
        row_off, col_off = divmod(offset, 3)
        if flip:
            row_off, col_off = 2 - row_off, 2 - col_off
        rows = rows_ref[col_off, pl.ds(row_off * pitch, count), :]
        term = lax.dot_general(rows, weight_of(offset), dims, preferred_element_type=F32)
        total = term if total is None else total + term
    return total


def left_half(count):
    return lax.broadcasted_iota(jnp.int32, (count, 128), 1) < 64


def split(low, middle, high):
    left = left_half(low.shape[0])
    turned = pltpu.roll(middle, 64, 1)
    first = (jnp.where(left, low, turned), jnp.where(left, high, 0.0))
    second = (jnp.where(left, turned, low), jnp.where(left, 0.0, high))
    return tuple(jnp.concatenate(parts, axis=1).astype(BF16) for parts in (first, second))


def joined(first, second):
    left = left_half(first.shape[0])
    low = jnp.where(left, first[:, :128], second[:, :128])
    middle = pltpu.roll(jnp.where(left, second[:, :128], first[:, :128]), 64, 1)
    high = jnp.where(left, first[:, 128:], second[:, 128:])
    return low, middle, high


def pair_weights(w_ref, lanes, backward):
    rows = []
    for outer in (-1, 0, 1):
        taps = []
        for inner in (-1, 0, 1):
            row, col = (-outer, -inner) if backward else (inner, outer)
            taps.append(w_ref[3 * (row + 1) + col + 1, :, lanes].astype(F32))
        rows.append(split(*taps))
    empty = jnp.zeros(rows[0][0].shape, BF16)
    first = jnp.concatenate([rows[0][0], rows[1][0], rows[2][0], empty], axis=0)
    second = jnp.concatenate([rows[1][1], rows[0][1], empty, rows[2][1]], axis=0)
    return first, second


def pair_rows(rows):
    return split(pltpu.roll(rows, 1, 0), rows, pltpu.roll(rows, rows.shape[0] - 1, 0))


def pair_conv(first, second, weights, pitch, dims):
    first = lax.dot_general(first, weights[0], dims, preferred_element_type=F32)
    second = lax.dot_general(second, weights[1], dims, preferred_element_type=F32)
    side = first.shape[0] // pitch
    parts = []
    for high in range(side):
        span = slice(high * pitch, (high + 1) * pitch)
        parts.append(joined(first[span], second[span]))
    sums = []
    for high in range(side):
        total = parts[high][1]
        if high > 0:
            total = total + parts[high - 1][0]
        if high + 1 < side:
            total = total + parts[high + 1][2]
        sums.append(total)
    return sums


def slope_of(pre):
    sigma = jax.nn.sigmoid(pre)
    return sigma, sigma * (1.0 + pre * (1.0 - sigma))


PLAIN = (((1,), (0,)), ((), ()))
TURNED = (((1,), (1,)), ((), ()))


def routing_of(info, slots, cores):
    devices = info.shape[0]
    core = (lax.broadcasted_iota(jnp.int32, (devices, 1), 0) % cores).astype(F32)
    owners = lax.broadcasted_iota(jnp.int32, (devices, 128), 1).astype(F32)
    routes = []
    total = jnp.zeros((1, 128), F32)
    for slot in range(slots):
        coef = (
            info[:, slot : slot + 1]
            + info[:, slots + slot : slots + slot + 1]
            + info[:, 2 * slots + slot : 2 * slots + slot + 1]
        )
        target = info[:, 3 * slots + slot : 3 * slots + slot + 1] * cores + core
        route = jnp.where(target == owners, coef, 0.0)
        routes.append(route)
        total = total + jnp.sum(route, axis=0, keepdims=True)
    return routes, jnp.maximum(total, 1.0)


def scaled_rows(cot, denominator, ids):
    same = ids == lax.broadcasted_iota(jnp.int32, (cot.shape[0], 128), 1)
    column = jnp.sum(jnp.where(same, denominator, 0.0), axis=1, keepdims=True)
    return (LOSS_SCALE * cot / column).astype(BF16).astype(F32)


def info_row(coefs, targets, lanes):
    slots = len(coefs)
    lane = lax.broadcasted_iota(jnp.int32, (1, lanes), 1)
    value = jnp.zeros((1, lanes), F32)
    for slot in range(slots):
        for part in range(3):
            value = jnp.where(lane == part * slots + slot, coefs[slot], value)
        value = jnp.where(lane == 3 * slots + slot, targets[slot].astype(F32), value)
    high = value.astype(BF16).astype(F32)
    middle = (value - high).astype(BF16).astype(F32)
    low = (value - high - middle).astype(BF16).astype(F32)
    value = jnp.where((lane >= slots) & (lane < 2 * slots), middle, high)
    return jnp.where((lane >= 2 * slots) & (lane < 3 * slots), low, value)


def own_row(coefs, targets):
    slots = len(coefs)
    lane = lax.broadcasted_iota(jnp.int32, (1, 128), 1)
    value = jnp.zeros((1, 128), F32)
    for slot in range(slots):
        value = jnp.where(lane == slot, coefs[slot], value)
        value = jnp.where(lane == slots + slot, targets[slot].astype(F32), value)
    return value


def own_route(own, slots, owner):
    return [
        jnp.where(own[:, slots + slot : slots + slot + 1] == owner, own[:, slot : slot + 1], 0.0)
        for slot in range(slots)
    ]


def pack_kernel(
    counts_ref,
    weights_ref,
    slide_ref,
    owner_ref,
    x_ref,
    cot_ref,
    out_ref,
    own_ref,
    flat_ref,
):
    devices, groups, _, lanes = out_ref.shape
    _, slots, side, _, channels = x_ref.shape
    rows = slots * side * side
    for index in range(slots * side):
        values = x_ref[0, index // side, index % side].astype(F32)
        flat_ref[pl.ds(index * side, side), :] = values
    flat_ref[pl.ds(rows, 1), :] = cot_ref[0].astype(F32)
    coefs, targets = own_scalars(counts_ref, weights_ref, slide_ref, owner_ref, slots)
    own_ref[...] = own_row(coefs, targets)
    info = info_row(coefs, targets, lanes)
    flat_ref[pl.ds(rows + 1, 1), :] = jnp.concatenate([info] * devices, axis=1)
    spare = groups * ROW - rows - 2
    flat_ref[pl.ds(rows + 2, spare), :] = jnp.zeros((spare, channels), F32)
    for device in range(devices):
        part = flat_ref[:, pl.ds(device * lanes, lanes)].astype(BF16)
        out_ref[device] = part.reshape(groups, ROW, lanes)


def local_kernel(cores, my_ref, own_ref, cot_ref, x_ref, w_ref, slope_ref, *share_refs):
    step = pl.program_id(0)
    side, kept, lanes = slope_ref.shape
    slots = kept // ROW
    devices = len(share_refs) * (share_refs[0].shape[0] - 1)
    totals = []
    for pair in range(lanes // 128):
        span = pl.ds(pair * 128, 128)
        pieces = []
        for high in range(side):
            for slot in range(slots):
                pieces += [x_ref[0, slot, high, :, span].astype(F32), jnp.zeros((ROW - side, 128), F32)]
        first, second = pair_rows(jnp.concatenate(pieces, axis=0))
        pres = pair_conv(first, second, pair_weights(w_ref, span, False), kept, PLAIN)
        total = jnp.zeros((kept, 128), F32)
        for high in range(side):
            pre = pres[high]
            sigma, slope = slope_of(pre)
            slope_ref[high, :, span] = slope
            total = total + pre * sigma
        totals.append(total)
    total = jnp.concatenate(totals, axis=1)
    place = lax.broadcasted_iota(jnp.int32, (ROW, lanes), 0)
    own = own_ref[...]
    means = []
    for slot in range(slots):
        here = jnp.where(place < side, total[slot * ROW : (slot + 1) * ROW], 0.0)
        mean = jnp.sum(here, axis=0, keepdims=True) / (side * side)
        means.append(mean.astype(BF16).astype(F32))
    for index in range(devices):
        owner = index if len(share_refs) == 1 else (my_ref[0] // cores) ^ index
        share = jnp.zeros((1, lanes), F32)
        for mean, weight in zip(means, own_route(own, slots, jnp.float32(owner))):
            share = share + weight * mean
        place_ref = share_refs[index % len(share_refs)]
        for part in range(lanes // BLOCK):
            at = pl.ds(step * (lanes // BLOCK) + part, 1)
            place_ref[index // len(share_refs), at, :] = share[:, part * BLOCK : (part + 1) * BLOCK]
    for part in range(lanes // BLOCK):
        at = pl.ds(step * (lanes // BLOCK) + part, 1)
        for place_ref in share_refs:
            span = slice(part * BLOCK, (part + 1) * BLOCK)
            place_ref[devices // len(share_refs), at, :] = cot_ref[0, :, span].astype(F32)


def weight_kernel(packed, cores, side, my_ref, got_ref, w_ref, out_ref, rows_ref, grad_ref, flat_ref):
    del my_ref
    devices, groups, _, lanes = got_ref.shape
    slots = groups * ROW // (side * side)
    width = w_ref.shape[1]
    part = devices * ROW
    pitch = slots * part
    flat_ref[...] = got_ref[...].astype(F32).reshape(devices, groups * ROW, lanes)
    tail = got_ref[:, groups - 1].astype(F32)
    cot = tail[:, slots * side * side % ROW, :]
    info = tail[:, slots * side * side % ROW + 1, :]
    routes, denominator = routing_of(info, slots, cores)
    scaled = scaled_rows(cot, denominator, lax.broadcasted_iota(jnp.int32, (devices, 128), 0))
    place = lax.broadcasted_iota(jnp.int32, (devices, ROW, lanes), 1)
    tile_grads = []
    for slot in range(slots):
        rows = jnp.zeros((devices, lanes), F32)
        for owner in range(devices):
            rows = rows + routes[slot][:, owner : owner + 1] * scaled[owner : owner + 1]
        spread = jnp.broadcast_to(rows[:, None, :], (devices, ROW, lanes)) / (side * side)
        tile_grads.append(jnp.where(place < side, spread, 0.0).reshape(part, lanes))
    tile_grad = jnp.concatenate(tile_grads, axis=0)

    if packed:
        for pair in range(lanes // 128):
            span = pl.ds(pair * 128, 128)
            for high in range(side):
                rows = []
                for slot in range(slots):
                    here = flat_ref[:, pl.ds((slot * side + high) * side, ROW), span]
                    here = jnp.where(place[:, :, :128] < side, here, 0.0)
                    rows.append(here.reshape(part, 128))
                first, second = pair_rows(jnp.concatenate(rows, axis=0))
                rows_ref[0, pl.ds(high * pitch, pitch), :] = first
                rows_ref[1, pl.ds(high * pitch, pitch), :] = second
            first, second = rows_ref[0, :, :], rows_ref[1, :, :]
            pres = pair_conv(first, second, pair_weights(w_ref, span, False), pitch, PLAIN)
            grads = [slope_of(pre)[1] * tile_grad[:, pair * 128 : (pair + 1) * 128] for pre in pres]
            none = jnp.zeros((pitch, 128), F32)
            turned = jnp.concatenate([none, *grads, none], axis=0).astype(BF16).T
            count = side * pitch
            products = []
            for index in range(2):
                low, middle, high = (
                    turned[index * width : (index + 1) * width, at * pitch : at * pitch + count]
                    for at in (2, 1, 0)
                )
                empty = jnp.zeros(low.shape, BF16)
                order = [middle, low, empty, high] if index else [low, middle, high, empty]
                product = jnp.dot(
                    jnp.concatenate(order, axis=0), rows_ref[index, :, :], preferred_element_type=F32
                )
                products.append(product.T)
            for col, quarter, other in ((0, 0, 1), (1, 1, 0), (2, 2, 3)):
                taps = joined(
                    products[0][quarter * width : (quarter + 1) * width],
                    products[1][other * width : (other + 1) * width],
                )
                for row in range(3):
                    out_ref[3 * row + col, :, span] = taps[row].astype(BF16)
        return

    zero = jnp.zeros((pitch, lanes), BF16)
    for col in range(3):
        rows_ref[col, pl.ds(0, pitch), :] = zero
        rows_ref[col, pl.ds((side + 1) * pitch, pitch), :] = zero
    grad_ref[pl.ds(0, pitch), :] = zero
    grad_ref[pl.ds((side + 1) * pitch, pitch), :] = zero
    for high in range(side):
        for slot in range(slots):
            here = flat_ref[:, pl.ds((slot * side + high) * side, ROW), :]
            rows = jnp.where(place < side, here, 0.0)
            for col, moved in enumerate(shifted(rows.reshape(part, lanes))):
                rows_ref[col, pl.ds((high + 1) * pitch + slot * part, part), :] = moved
    mask = diagonal_mask(lanes, width) if lanes > width else None
    pre = conv_taps(
        rows_ref,
        lambda tap: block_diagonal(w_ref[tap], mask),
        pitch,
        side * pitch,
        False,
        (((1,), (0,)), ((), ())),
    )
    sigma = jax.nn.sigmoid(pre)
    slope = sigma * (1.0 + pre * (1.0 - sigma))
    for high in range(side):
        here = slope[high * pitch : (high + 1) * pitch] * tile_grad
        grad_ref[pl.ds((high + 1) * pitch, pitch), :] = here.astype(BF16)
    group = lax.broadcasted_iota(jnp.int32, (width, lanes), 1) // width
    for offset in range(9):
        row_off, col_off = divmod(offset, 3)
        product = lax.dot_general(
            rows_ref[col_off, pl.ds(pitch, side * pitch), :],
            grad_ref[pl.ds((2 - row_off) * pitch, side * pitch), :],
            (((0,), (0,)), ((), ())),
            preferred_element_type=F32,
        )
        result = product[:width]
        for index in range(1, lanes // width):
            result = jnp.where(group == index, product[index * width : (index + 1) * width], result)
        out_ref[offset] = result.astype(BF16)


def input_kernel(
    packed,
    cores,
    my_ref,
    own_ref,
    slope_ref,
    w_ref,
    info_ref,
    *refs,
):
    *refs, out_ref, pooled_ref = refs
    step = pl.program_id(0)
    side, kept, lanes = slope_ref.shape
    slots = kept // ROW
    devices = info_ref.shape[0] // cores
    info = info_ref[:, 0].astype(F32)[:, (slots * side * side + 1) % ROW, :]
    _, denominator = routing_of(info, slots, cores)
    owners = lax.broadcasted_iota(jnp.int32, (1, 128), 1)
    mine = jnp.sum(jnp.where(owners == my_ref[0], denominator, 0.0), axis=1, keepdims=True)
    base = my_ref[0] // cores if packed else 0
    cots = []
    for part in range(lanes // BLOCK):
        at = pl.ds(step * (lanes // BLOCK) + part, 1)
        if packed:
            shares = [ref[0, at, :] for ref in refs]
            rows = [ref[row, at, :] for ref in refs for row in (1, 2)]
            cots.append(jnp.concatenate(rows, axis=0))
        else:
            shares = [jnp.sum(refs[0][:, at, :], axis=0)]
            cots.append(refs[1][:, at, :].reshape(devices, BLOCK))
        pooled_ref[0, :, part * BLOCK : (part + 1) * BLOCK] = sum(shares[1:], shares[0]) / mine
    ids = (lax.broadcasted_iota(jnp.int32, (devices, 128), 0) ^ base) * cores + my_ref[0] % cores
    scaled = scaled_rows(jnp.concatenate(cots, axis=1), denominator, ids)

    place = lax.broadcasted_iota(jnp.int32, (ROW, lanes), 0)
    own = own_ref[...]
    pieces = []
    owner = (lax.broadcasted_iota(jnp.int32, (devices, 1), 0) ^ base).astype(F32)
    for weight in own_route(own, slots, owner):
        row = jnp.sum(weight * scaled, axis=0, keepdims=True)
        spread = jnp.broadcast_to(row, (ROW, lanes)) / (side * side)
        pieces.append(jnp.where(place < side, spread, 0.0))
    tile_grad = jnp.concatenate(pieces, axis=0)

    for pair in range(lanes // 128):
        span = pl.ds(pair * 128, 128)
        here = tile_grad[:, pair * 128 : (pair + 1) * 128]
        rows = jnp.concatenate([slope_ref[high, :, span] * here for high in range(side)], axis=0)
        first, second = pair_rows(rows)
        sums = pair_conv(first, second, pair_weights(w_ref, span, True), kept, TURNED)
        for high in range(side):
            for slot in range(slots):
                for wide in range(side):
                    at = slot * ROW + wide
                    out_ref[slot, high, wide, :, span] = sums[high][at : at + 1]


def params(mebibytes):
    return pltpu.CompilerParams(vmem_limit_bytes=mebibytes * 2**20)


def cost(flops, moved):
    return pl.CostEstimate(flops=flops, bytes_accessed=moved, transcendentals=0)


def swap(value, axis, step):
    return lax.ppermute(value, axis, [(i, i ^ step) for i in range(lax.axis_size(axis))])


def sum_over_slide(terms, cores, beside):
    count = lax.axis_size("slide")
    total, step = terms, cores
    while step < count:
        sent = total.astype(BF16)
        other = swap(sent, "slide", step)
        if 2 * step >= count:
            other, beside = lax.optimization_barrier((other, beside))
        total = sent.astype(F32) + other.astype(F32)
        step *= 2
    if cores == 2:
        second = lax.axis_index("slide") % 2 == 1
        half = total.astype(BF16)
        rest = swap(half, "slide", 1)
        whole = [jnp.where(second, rest, half), jnp.where(second, half, rest)]
        total = jnp.concatenate(whole, axis=2)
    return total.astype(F32), beside


def shards(tiles, tile_counts, tile_weights, slide_of, owner_map, cotangent, conv_weight):
    _, slots, side, _, channels = tiles.shape
    taps, width, _ = conv_weight.shape
    devices = lax.axis_size("tile")
    count = lax.axis_size("slide")
    packed = channels // devices == BLOCK and count % 2 == 0
    cores = 2 if packed else 1
    exchange = devices * cores
    lanes = channels // exchange
    blocks = channels // BLOCK
    mine = lax.axis_index("tile") * cores + lax.axis_index("slide") % cores
    mine = mine.astype(jnp.int32).reshape(1)
    slides = slide_of[:, :, 0]
    groups = -(-(slots * side * side + 2) // ROW)
    kept = slots * ROW
    macs = slots * side * side * taps * width * channels

    chunks, routes = pl.pallas_call(
        pack_kernel,
        out_shape=(
            jax.ShapeDtypeStruct((exchange, groups, ROW, lanes), BF16),
            jax.ShapeDtypeStruct((1, 128), F32),
        ),
        in_specs=[smem_whole()] * 4 + [vmem_whole()] * 2,
        out_specs=(vmem_whole(), vmem_whole()),
        scratch_shapes=[pltpu.VMEM((groups * ROW, channels), F32)],
        compiler_params=params(56),
    )(tile_counts, tile_weights, slides, owner_map, tiles, cotangent)
    if packed:
        chips = [
            [tile * count + chip * cores + core for tile in range(devices) for core in range(cores)]
            for chip in range(count // cores)
        ]
        got = lax.all_to_all(
            chunks, ("tile", "slide"), 0, 0, tiled=True, axis_index_groups=chips
        )
    else:
        got = lax.all_to_all(chunks, "tile", 0, 0, tiled=True)

    halves = 2 if packed else 1
    slope, *sent = pl.pallas_call(
        functools.partial(local_kernel, cores),
        grid=(channels // STEP,),
        out_shape=(
            jax.ShapeDtypeStruct((side, kept, channels), F32),
        )
        + (jax.ShapeDtypeStruct((devices // halves + 1, blocks, BLOCK), F32),) * halves,
        in_specs=[
            smem_whole(),
            pl.BlockSpec((1, 128), lambda j: (0, 0)),
            pl.BlockSpec((1, 1, STEP), lambda j: (0, 0, j)),
            pl.BlockSpec((1, slots, side, side, STEP), lambda j: (0, 0, 0, 0, j)),
            pl.BlockSpec((taps, width, STEP), lambda j: (0, 0, j)),
        ],
        out_specs=(
            pl.BlockSpec((side, kept, STEP), lambda j: (0, 0, j)),
        )
        + (pl.BlockSpec((devices // halves + 1, blocks, BLOCK), lambda j: (0, 0, 0)),) * halves,
        compiler_params=params(56),
        cost_estimate=cost(8 * macs, 4 * 2**20),
    )(mine, routes, cotangent, tiles, conv_weight)
    if packed:
        half = devices // 2
        other = swap(sent[1], "tile", 1)
        toward = sent[0][:half] + other[:half]
        cots = [sent[0][half:], other[half:]]
        toward = [jnp.concatenate([toward[i : i + 1], *cots]) for i in range(half)]
    else:
        toward = sent[0]
    got, slope, _ = lax.optimization_barrier((got, slope, toward))
    if packed:
        shares = toward[:1] + [swap(toward[i], "tile", 2 * i) for i in range(1, half)]
    else:
        shares = [lax.all_to_all(toward[:devices], "tile", 0, 0, tiled=True)]
        shares.append(lax.all_gather(toward[devices:], "tile", axis=0, tiled=True))
    info_block = (slots * side * side + 1) // ROW
    pitch_all = slots * exchange * ROW
    if packed:
        scratch = [pltpu.VMEM((2, side * pitch_all, BLOCK), BF16)] * 2
    else:
        scratch = [
            pltpu.VMEM((3, (side + 2) * pitch_all, lanes), BF16),
            pltpu.VMEM(((side + 2) * pitch_all, lanes), BF16),
        ]
    scratch.append(pltpu.VMEM((exchange, groups * ROW, lanes), F32))
    if packed:
        weight_spec = pl.BlockSpec((taps, width, lanes), lambda j, my: (0, 0, my[0]))
        weight = conv_weight
    else:
        weight_spec = pl.BlockSpec((taps, width, lanes), lambda j, my: (0, 0, 0))
        weight = lax.dynamic_slice_in_dim(conv_weight, mine[0] * lanes, lanes, 2)
    terms = pl.pallas_call(
        functools.partial(weight_kernel, packed, cores, side),
        out_shape=jax.ShapeDtypeStruct((taps, width, lanes), BF16),
        grid_spec=pltpu.PrefetchScalarGridSpec(
            num_scalar_prefetch=1,
            grid=(1,),
            in_specs=[pl.BlockSpec(got.shape, lambda j, my: (0, 0, 0, 0)), weight_spec],
            out_specs=pl.BlockSpec((taps, width, lanes), lambda j, my: (0, 0, 0)),
            scratch_shapes=scratch,
        ),
        compiler_params=params(20),
        cost_estimate=cost(16 * macs, 4 * 2**20),
    )(mine, got, weight)

    terms, shares = lax.optimization_barrier((terms, shares))
    grads, pooled = pl.pallas_call(
        functools.partial(input_kernel, packed, cores),
        grid=(channels // STEP,),
        out_shape=(
            jax.ShapeDtypeStruct((slots, side, side, 1, channels), F32),
            jax.ShapeDtypeStruct((1, 1, channels), F32),
        ),
        in_specs=[
            smem_whole(),
            pl.BlockSpec((1, 128), lambda j: (0, 0)),
            pl.BlockSpec((side, kept, STEP), lambda j: (0, 0, j)),
            pl.BlockSpec((taps, width, STEP), lambda j: (0, 0, j)),
            pl.BlockSpec((exchange, 1, ROW, lanes), lambda j: (0, info_block, 0, 0)),
        ]
        + [pl.BlockSpec((part.shape[0], blocks, BLOCK), lambda j: (0, 0, 0)) for part in shares],
        out_specs=(
            pl.BlockSpec((slots, side, side, 1, STEP), lambda j: (0, 0, 0, 0, j)),
            pl.BlockSpec((1, 1, STEP), lambda j: (0, 0, j)),
        ),
        compiler_params=params(16),
        cost_estimate=cost(8 * macs, 4 * 2**20),
    )(
        mine,
        routes,
        pltpu.with_memory_space_constraint(slope, pltpu.HBM),
        conv_weight,
        got,
        *shares,
    )
    total, (grads, pooled) = sum_over_slide(terms, cores, (grads, pooled))
    weight_grads = total / LOSS_SCALE
    input_grads = jnp.transpose(grads, (3, 0, 1, 2, 4))
    return (pooled, input_grads, weight_grads)


def solution(mesh):
    return jax.shard_map(
        shards,
        mesh=mesh,
        in_specs=(
            P("slide", "tile", None, None, None),
            P("slide", "tile"),
            P("slide", "tile"),
            P("slide", "tile", None),
            P("slide", None),
            P("slide", "tile", None),
            P(),
        ),
        out_specs=(
            P("slide", "tile", None),
            P("slide", "tile", None, None, None),
            P(None, None, "tile"),
        ),
        check_vma=False,
    )
```

```python
import functools

import jax
import jax.numpy as jnp
from jax import lax
from jax.experimental import pallas as pl
from jax.experimental.pallas import tpu as pltpu
from jax.sharding import PartitionSpec as P

LOSS_SCALE = 512.0
BLOCK = 256
STEP = 1024
ROW = 8
F32 = jnp.float32
BF16 = jnp.bfloat16


def vmem_whole():
    return pl.BlockSpec(memory_space=pltpu.VMEM)


def smem_whole():
    return pl.BlockSpec(memory_space=pltpu.SMEM)


def own_scalars(counts_ref, weights_ref, slide_ref, owner_ref, slots):
    coefs, targets = [], []
    for slot in range(slots):
        live = counts_ref[0, 0] > slot
        coefs.append(jnp.where(live, weights_ref[0, slot], 0.0))
        targets.append(owner_ref[0, slide_ref[0, slot]])
    return coefs, targets


def block_diagonal(tap, mask):
    width, channels = tap.shape
    if channels == width:
        return tap
    return jnp.concatenate([tap] * (channels // width), axis=0) * mask


def diagonal_mask(channels, width):
    row = lax.broadcasted_iota(jnp.int32, (channels, channels), 0) // width
    col = lax.broadcasted_iota(jnp.int32, (channels, channels), 1) // width
    return (row == col).astype(F32).astype(BF16)


def shifted(rows):
    count = rows.shape[0]
    return (
        pltpu.roll(rows, 1, 0).astype(BF16),
        rows.astype(BF16),
        pltpu.roll(rows, count - 1, 0).astype(BF16),
    )


def conv_taps(rows_ref, weight_of, pitch, count, flip, dims):
    total = None
    for offset in range(9):
        row_off, col_off = divmod(offset, 3)
        if flip:
            row_off, col_off = 2 - row_off, 2 - col_off
        rows = rows_ref[col_off, pl.ds(row_off * pitch, count), :]
        term = lax.dot_general(rows, weight_of(offset), dims, preferred_element_type=F32)
        total = term if total is None else total + term
    return total


def left_half(count):
    return lax.broadcasted_iota(jnp.int32, (count, 128), 1) < 64


def split(low, middle, high):
    left = left_half(low.shape[0])
    turned = pltpu.roll(middle, 64, 1)
    first = (jnp.where(left, low, turned), jnp.where(left, high, 0.0))
    second = (jnp.where(left, turned, low), jnp.where(left, 0.0, high))
    return tuple(jnp.concatenate(parts, axis=1).astype(BF16) for parts in (first, second))


def joined(first, second):
    left = left_half(first.shape[0])
    low = jnp.where(left, first[:, :128], second[:, :128])
    middle = pltpu.roll(jnp.where(left, second[:, :128], first[:, :128]), 64, 1)
    high = jnp.where(left, first[:, 128:], second[:, 128:])
    return low, middle, high


def pair_weights(w_ref, lanes, backward):
    rows = []
    for outer in (-1, 0, 1):
        taps = []
        for inner in (-1, 0, 1):
            row, col = (-outer, -inner) if backward else (inner, outer)
            taps.append(w_ref[3 * (row + 1) + col + 1, :, lanes].astype(F32))
        rows.append(split(*taps))
    empty = jnp.zeros(rows[0][0].shape, BF16)
    first = jnp.concatenate([rows[0][0], rows[1][0], rows[2][0], empty], axis=0)
    second = jnp.concatenate([rows[1][1], rows[0][1], empty, rows[2][1]], axis=0)
    return first, second


def pair_rows(rows):
    return split(pltpu.roll(rows, 1, 0), rows, pltpu.roll(rows, rows.shape[0] - 1, 0))


def pair_conv(first, second, weights, pitch, dims):
    first = lax.dot_general(first, weights[0], dims, preferred_element_type=F32)
    second = lax.dot_general(second, weights[1], dims, preferred_element_type=F32)
    side = first.shape[0] // pitch
    parts = []
    for high in range(side):
        span = slice(high * pitch, (high + 1) * pitch)
        parts.append(joined(first[span], second[span]))
    sums = []
    for high in range(side):
        total = parts[high][1]
        if high > 0:
            total = total + parts[high - 1][0]
        if high + 1 < side:
            total = total + parts[high + 1][2]
        sums.append(total)
    return sums


def slope_of(pre):
    sigma = jax.nn.sigmoid(pre)
    return sigma, sigma * (1.0 + pre * (1.0 - sigma))


PLAIN = (((1,), (0,)), ((), ()))
TURNED = (((1,), (1,)), ((), ()))


def routing_of(info, slots, cores):
    devices = info.shape[0]
    core = (lax.broadcasted_iota(jnp.int32, (devices, 1), 0) % cores).astype(F32)
    owners = lax.broadcasted_iota(jnp.int32, (devices, 128), 1).astype(F32)
    routes = []
    total = jnp.zeros((1, 128), F32)
    for slot in range(slots):
        coef = (
            info[:, slot : slot + 1]
            + info[:, slots + slot : slots + slot + 1]
            + info[:, 2 * slots + slot : 2 * slots + slot + 1]
        )
        target = info[:, 3 * slots + slot : 3 * slots + slot + 1] * cores + core
        route = jnp.where(target == owners, coef, 0.0)
        routes.append(route)
        total = total + jnp.sum(route, axis=0, keepdims=True)
    return routes, jnp.maximum(total, 1.0)


def scaled_rows(cot, denominator, ids):
    same = ids == lax.broadcasted_iota(jnp.int32, (cot.shape[0], 128), 1)
    column = jnp.sum(jnp.where(same, denominator, 0.0), axis=1, keepdims=True)
    return (LOSS_SCALE * cot / column).astype(BF16).astype(F32)


def info_row(coefs, targets, lanes):
    slots = len(coefs)
    lane = lax.broadcasted_iota(jnp.int32, (1, lanes), 1)
    value = jnp.zeros((1, lanes), F32)
    for slot in range(slots):
        for part in range(3):
            value = jnp.where(lane == part * slots + slot, coefs[slot], value)
        value = jnp.where(lane == 3 * slots + slot, targets[slot].astype(F32), value)
    high = value.astype(BF16).astype(F32)
    middle = (value - high).astype(BF16).astype(F32)
    low = (value - high - middle).astype(BF16).astype(F32)
    value = jnp.where((lane >= slots) & (lane < 2 * slots), middle, high)
    return jnp.where((lane >= 2 * slots) & (lane < 3 * slots), low, value)


def own_row(coefs, targets):
    slots = len(coefs)
    lane = lax.broadcasted_iota(jnp.int32, (1, 128), 1)
    value = jnp.zeros((1, 128), F32)
    for slot in range(slots):
        value = jnp.where(lane == slot, coefs[slot], value)
        value = jnp.where(lane == slots + slot, targets[slot].astype(F32), value)
    return value


def own_route(own, slots, owner):
    return [
        jnp.where(own[:, slots + slot : slots + slot + 1] == owner, own[:, slot : slot + 1], 0.0)
        for slot in range(slots)
    ]


def pack_kernel(
    counts_ref,
    weights_ref,
    slide_ref,
    owner_ref,
    x_ref,
    cot_ref,
    out_ref,
    own_ref,
    flat_ref,
):
    devices, groups, _, lanes = out_ref.shape
    _, slots, side, _, channels = x_ref.shape
    rows = slots * side * side
    for index in range(slots * side):
        values = x_ref[0, index // side, index % side].astype(F32)
        flat_ref[pl.ds(index * side, side), :] = values
    flat_ref[pl.ds(rows, 1), :] = cot_ref[0].astype(F32)
    coefs, targets = own_scalars(counts_ref, weights_ref, slide_ref, owner_ref, slots)
    own_ref[...] = own_row(coefs, targets)
    info = info_row(coefs, targets, lanes)
    flat_ref[pl.ds(rows + 1, 1), :] = jnp.concatenate([info] * devices, axis=1)
    spare = groups * ROW - rows - 2
    flat_ref[pl.ds(rows + 2, spare), :] = jnp.zeros((spare, channels), F32)
    for device in range(devices):
        part = flat_ref[:, pl.ds(device * lanes, lanes)].astype(BF16)
        out_ref[device] = part.reshape(groups, ROW, lanes)


def local_kernel(cores, my_ref, own_ref, cot_ref, x_ref, w_ref, slope_ref, *share_refs):
    step = pl.program_id(0)
    side, kept, lanes = slope_ref.shape
    slots = kept // ROW
    devices = len(share_refs) * (share_refs[0].shape[0] - 1)
    totals = []
    for pair in range(lanes // 128):
        span = pl.ds(pair * 128, 128)
        pieces = []
        for high in range(side):
            for slot in range(slots):
                pieces += [x_ref[0, slot, high, :, span].astype(F32), jnp.zeros((ROW - side, 128), F32)]
        first, second = pair_rows(jnp.concatenate(pieces, axis=0))
        pres = pair_conv(first, second, pair_weights(w_ref, span, False), kept, PLAIN)
        total = jnp.zeros((kept, 128), F32)
        for high in range(side):
            pre = pres[high]
            sigma, slope = slope_of(pre)
            slope_ref[high, :, span] = slope
            total = total + pre * sigma
        totals.append(total)
    total = jnp.concatenate(totals, axis=1)
    place = lax.broadcasted_iota(jnp.int32, (ROW, lanes), 0)
    own = own_ref[...]
    means = []
    for slot in range(slots):
        here = jnp.where(place < side, total[slot * ROW : (slot + 1) * ROW], 0.0)
        mean = jnp.sum(here, axis=0, keepdims=True) / (side * side)
        means.append(mean.astype(BF16).astype(F32))
    for index in range(devices):
        owner = index if len(share_refs) == 1 else (my_ref[0] // cores) ^ index
        share = jnp.zeros((1, lanes), F32)
        for mean, weight in zip(means, own_route(own, slots, jnp.float32(owner))):
            share = share + weight * mean
        place_ref = share_refs[index % len(share_refs)]
        for part in range(lanes // BLOCK):
            at = pl.ds(step * (lanes // BLOCK) + part, 1)
            place_ref[index // len(share_refs), at, :] = share[:, part * BLOCK : (part + 1) * BLOCK]
    for part in range(lanes // BLOCK):
        at = pl.ds(step * (lanes // BLOCK) + part, 1)
        for place_ref in share_refs:
            span = slice(part * BLOCK, (part + 1) * BLOCK)
            place_ref[devices // len(share_refs), at, :] = cot_ref[0, :, span].astype(F32)


def weight_kernel(
    packed, cores, side, my_ref, got_ref, w_ref, out_ref, below_ref, rows_ref, grad_ref, flat_ref
):
    del my_ref
    devices, groups, _, lanes = got_ref.shape
    slots = groups * ROW // (side * side)
    width = w_ref.shape[1]
    part = devices * ROW
    pitch = slots * part
    flat_ref[...] = got_ref[...].astype(F32).reshape(devices, groups * ROW, lanes)
    tail = got_ref[:, groups - 1].astype(F32)
    cot = tail[:, slots * side * side % ROW, :]
    info = tail[:, slots * side * side % ROW + 1, :]
    routes, denominator = routing_of(info, slots, cores)
    below_ref[...] = denominator
    scaled = scaled_rows(cot, denominator, lax.broadcasted_iota(jnp.int32, (devices, 128), 0))
    place = lax.broadcasted_iota(jnp.int32, (devices, ROW, lanes), 1)
    tile_grads = []
    for slot in range(slots):
        rows = jnp.zeros((devices, lanes), F32)
        for owner in range(devices):
            rows = rows + routes[slot][:, owner : owner + 1] * scaled[owner : owner + 1]
        spread = jnp.broadcast_to(rows[:, None, :], (devices, ROW, lanes)) / (side * side)
        tile_grads.append(jnp.where(place < side, spread, 0.0).reshape(part, lanes))
    tile_grad = jnp.concatenate(tile_grads, axis=0)

    if packed:
        for pair in range(lanes // 128):
            span = pl.ds(pair * 128, 128)
            for high in range(side):
                rows = []
                for slot in range(slots):
                    here = flat_ref[:, pl.ds((slot * side + high) * side, ROW), span]
                    here = jnp.where(place[:, :, :128] < side, here, 0.0)
                    rows.append(here.reshape(part, 128))
                first, second = pair_rows(jnp.concatenate(rows, axis=0))
                rows_ref[0, pl.ds(high * pitch, pitch), :] = first
                rows_ref[1, pl.ds(high * pitch, pitch), :] = second
            first, second = rows_ref[0, :, :], rows_ref[1, :, :]
            pres = pair_conv(first, second, pair_weights(w_ref, span, False), pitch, PLAIN)
            grads = [slope_of(pre)[1] * tile_grad[:, pair * 128 : (pair + 1) * 128] for pre in pres]
            none = jnp.zeros((pitch, 128), F32)
            turned = jnp.concatenate([none, *grads, none], axis=0).astype(BF16).T
            count = side * pitch
            products = []
            for index in range(2):
                low, middle, high = (
                    turned[index * width : (index + 1) * width, at * pitch : at * pitch + count]
                    for at in (2, 1, 0)
                )
                empty = jnp.zeros(low.shape, BF16)
                order = [middle, low, empty, high] if index else [low, middle, high, empty]
                product = jnp.dot(
                    jnp.concatenate(order, axis=0), rows_ref[index, :, :], preferred_element_type=F32
                )
                products.append(product.T)
            for col, quarter, other in ((0, 0, 1), (1, 1, 0), (2, 2, 3)):
                taps = joined(
                    products[0][quarter * width : (quarter + 1) * width],
                    products[1][other * width : (other + 1) * width],
                )
                for row in range(3):
                    out_ref[3 * row + col, :, span] = taps[row].astype(BF16)
        return

    zero = jnp.zeros((pitch, lanes), BF16)
    for col in range(3):
        rows_ref[col, pl.ds(0, pitch), :] = zero
        rows_ref[col, pl.ds((side + 1) * pitch, pitch), :] = zero
    grad_ref[pl.ds(0, pitch), :] = zero
    grad_ref[pl.ds((side + 1) * pitch, pitch), :] = zero
    for high in range(side):
        for slot in range(slots):
            here = flat_ref[:, pl.ds((slot * side + high) * side, ROW), :]
            rows = jnp.where(place < side, here, 0.0)
            for col, moved in enumerate(shifted(rows.reshape(part, lanes))):
                rows_ref[col, pl.ds((high + 1) * pitch + slot * part, part), :] = moved
    mask = diagonal_mask(lanes, width) if lanes > width else None
    pre = conv_taps(
        rows_ref,
        lambda tap: block_diagonal(w_ref[tap], mask),
        pitch,
        side * pitch,
        False,
        (((1,), (0,)), ((), ())),
    )
    sigma = jax.nn.sigmoid(pre)
    slope = sigma * (1.0 + pre * (1.0 - sigma))
    for high in range(side):
        here = slope[high * pitch : (high + 1) * pitch] * tile_grad
        grad_ref[pl.ds((high + 1) * pitch, pitch), :] = here.astype(BF16)
    group = lax.broadcasted_iota(jnp.int32, (width, lanes), 1) // width
    for offset in range(9):
        row_off, col_off = divmod(offset, 3)
        product = lax.dot_general(
            rows_ref[col_off, pl.ds(pitch, side * pitch), :],
            grad_ref[pl.ds((2 - row_off) * pitch, side * pitch), :],
            (((0,), (0,)), ((), ())),
            preferred_element_type=F32,
        )
        result = product[:width]
        for index in range(1, lanes // width):
            result = jnp.where(group == index, product[index * width : (index + 1) * width], result)
        out_ref[offset] = result.astype(BF16)


def input_kernel(
    packed,
    cores,
    my_ref,
    own_ref,
    slope_ref,
    w_ref,
    below_ref,
    *refs,
):
    *refs, out_ref, pooled_ref = refs
    step = pl.program_id(0)
    side, kept, lanes = slope_ref.shape
    slots = kept // ROW
    devices = 2 * len(refs) if packed else refs[1].shape[0]
    denominator = below_ref[...]
    owners = lax.broadcasted_iota(jnp.int32, (1, 128), 1)
    mine = jnp.sum(jnp.where(owners == my_ref[0], denominator, 0.0), axis=1, keepdims=True)
    base = my_ref[0] // cores if packed else 0
    cots = []
    for part in range(lanes // BLOCK):
        at = pl.ds(step * (lanes // BLOCK) + part, 1)
        if packed:
            shares = [ref[0, at, :] for ref in refs]
            rows = [ref[row, at, :] for ref in refs for row in (1, 2)]
            cots.append(jnp.concatenate(rows, axis=0))
        else:
            shares = [jnp.sum(refs[0][:, at, :], axis=0)]
            cots.append(refs[1][:, at, :].reshape(devices, BLOCK))
        pooled_ref[0, :, part * BLOCK : (part + 1) * BLOCK] = sum(shares[1:], shares[0]) / mine
    ids = (lax.broadcasted_iota(jnp.int32, (devices, 128), 0) ^ base) * cores + my_ref[0] % cores
    cot = jnp.concatenate(cots, axis=1)
    scaled = scaled_rows(cot, denominator, ids)

    place = lax.broadcasted_iota(jnp.int32, (ROW, lanes), 0)
    own = own_ref[...]
    pieces = []
    owner = (lax.broadcasted_iota(jnp.int32, (devices, 1), 0) ^ base).astype(F32)
    for weight in own_route(own, slots, owner):
        row = jnp.sum(weight * scaled, axis=0, keepdims=True)
        spread = jnp.broadcast_to(row, (ROW, lanes)) / (side * side)
        pieces.append(jnp.where(place < side, spread, 0.0))
    tile_grad = jnp.concatenate(pieces, axis=0)

    for pair in range(lanes // 128):
        span = pl.ds(pair * 128, 128)
        here = tile_grad[:, pair * 128 : (pair + 1) * 128]
        rows = jnp.concatenate([slope_ref[high, :, span] * here for high in range(side)], axis=0)
        first, second = pair_rows(rows)
        sums = pair_conv(first, second, pair_weights(w_ref, span, True), kept, TURNED)
        for high in range(side):
            for slot in range(slots):
                for wide in range(side):
                    at = slot * ROW + wide
                    out_ref[slot, high, wide, :, span] = sums[high][at : at + 1]


def params(mebibytes):
    return pltpu.CompilerParams(vmem_limit_bytes=mebibytes * 2**20)


def cost(flops, moved):
    return pl.CostEstimate(flops=flops, bytes_accessed=moved, transcendentals=0)


def swap(value, axis, step):
    return lax.ppermute(value, axis, [(i, i ^ step) for i in range(lax.axis_size(axis))])


def sum_over_slide(terms, cores, beside):
    count = lax.axis_size("slide")
    total, step = terms, cores
    while step < count:
        sent = total.astype(BF16)
        other = swap(sent, "slide", step)
        if 2 * step >= count:
            other, beside = lax.optimization_barrier((other, beside))
        total = sent.astype(F32) + other.astype(F32)
        step *= 2
    if cores == 2:
        second = lax.axis_index("slide") % 2 == 1
        half = total.astype(BF16)
        rest = swap(half, "slide", 1)
        whole = [jnp.where(second, rest, half), jnp.where(second, half, rest)]
        total = jnp.concatenate(whole, axis=2)
    return total.astype(F32), beside


def shards(tiles, tile_counts, tile_weights, slide_of, owner_map, cotangent, conv_weight):
    _, slots, side, _, channels = tiles.shape
    taps, width, _ = conv_weight.shape
    devices = lax.axis_size("tile")
    count = lax.axis_size("slide")
    packed = channels // devices == BLOCK and count % 2 == 0
    cores = 2 if packed else 1
    exchange = devices * cores
    lanes = channels // exchange
    blocks = channels // BLOCK
    mine = lax.axis_index("tile") * cores + lax.axis_index("slide") % cores
    mine = mine.astype(jnp.int32).reshape(1)
    slides = slide_of[:, :, 0]
    groups = -(-(slots * side * side + 2) // ROW)
    kept = slots * ROW
    macs = slots * side * side * taps * width * channels

    chunks, routes = pl.pallas_call(
        pack_kernel,
        out_shape=(
            jax.ShapeDtypeStruct((exchange, groups, ROW, lanes), BF16),
            jax.ShapeDtypeStruct((1, 128), F32),
        ),
        in_specs=[smem_whole()] * 4 + [vmem_whole()] * 2,
        out_specs=(vmem_whole(), vmem_whole()),
        scratch_shapes=[pltpu.VMEM((groups * ROW, channels), F32)],
        compiler_params=params(56),
    )(tile_counts, tile_weights, slides, owner_map, tiles, cotangent)
    if packed:
        chips = [
            [tile * count + chip * cores + core for tile in range(devices) for core in range(cores)]
            for chip in range(count // cores)
        ]
        got = lax.all_to_all(
            chunks, ("tile", "slide"), 0, 0, tiled=True, axis_index_groups=chips
        )
    else:
        got = lax.all_to_all(chunks, "tile", 0, 0, tiled=True)

    halves = 2 if packed else 1
    slope, *sent = pl.pallas_call(
        functools.partial(local_kernel, cores),
        grid=(channels // STEP,),
        out_shape=(
            jax.ShapeDtypeStruct((side, kept, channels), F32),
        )
        + (jax.ShapeDtypeStruct((devices // halves + 1, blocks, BLOCK), F32),) * halves,
        in_specs=[
            smem_whole(),
            pl.BlockSpec((1, 128), lambda j: (0, 0)),
            pl.BlockSpec((1, 1, STEP), lambda j: (0, 0, j)),
            pl.BlockSpec((1, slots, side, side, STEP), lambda j: (0, 0, 0, 0, j)),
            pl.BlockSpec((taps, width, STEP), lambda j: (0, 0, j)),
        ],
        out_specs=(
            pl.BlockSpec((side, kept, STEP), lambda j: (0, 0, j)),
        )
        + (pl.BlockSpec((devices // halves + 1, blocks, BLOCK), lambda j: (0, 0, 0)),) * halves,
        compiler_params=params(56),
        cost_estimate=cost(8 * macs, 4 * 2**20),
    )(mine, routes, cotangent, tiles, conv_weight)
    if packed:
        half = devices // 2
        other = swap(sent[1], "tile", 1)
        toward = sent[0][:half] + other[:half]
        cots = [sent[0][half:], other[half:]]
        toward = [jnp.concatenate([toward[i : i + 1], *cots]) for i in range(half)]
    else:
        toward = sent[0]
    got, slope, _ = lax.optimization_barrier((got, slope, toward))
    if packed:
        shares = toward[:1] + [swap(toward[i], "tile", 2 * i) for i in range(1, half)]
    else:
        shares = [lax.all_to_all(toward[:devices], "tile", 0, 0, tiled=True)]
        shares.append(lax.all_gather(toward[devices:], "tile", axis=0, tiled=True))
    pitch_all = slots * exchange * ROW
    if packed:
        scratch = [pltpu.VMEM((2, side * pitch_all, BLOCK), BF16)] * 2
    else:
        scratch = [
            pltpu.VMEM((3, (side + 2) * pitch_all, lanes), BF16),
            pltpu.VMEM(((side + 2) * pitch_all, lanes), BF16),
        ]
    scratch.append(pltpu.VMEM((exchange, groups * ROW, lanes), F32))
    if packed:
        weight_spec = pl.BlockSpec((taps, width, lanes), lambda j, my: (0, 0, my[0]))
        weight = conv_weight
    else:
        weight_spec = pl.BlockSpec((taps, width, lanes), lambda j, my: (0, 0, 0))
        weight = lax.dynamic_slice_in_dim(conv_weight, mine[0] * lanes, lanes, 2)
    terms, below = pl.pallas_call(
        functools.partial(weight_kernel, packed, cores, side),
        out_shape=(
            jax.ShapeDtypeStruct((taps, width, lanes), BF16),
            jax.ShapeDtypeStruct((1, 128), F32),
        ),
        grid_spec=pltpu.PrefetchScalarGridSpec(
            num_scalar_prefetch=1,
            grid=(1,),
            in_specs=[pl.BlockSpec(got.shape, lambda j, my: (0, 0, 0, 0)), weight_spec],
            out_specs=(
                pl.BlockSpec((taps, width, lanes), lambda j, my: (0, 0, 0)),
                pl.BlockSpec((1, 128), lambda j, my: (0, 0)),
            ),
            scratch_shapes=scratch,
        ),
        compiler_params=params(20),
        cost_estimate=cost(16 * macs, 4 * 2**20),
    )(mine, got, weight)

    terms, shares = lax.optimization_barrier((terms, shares))
    grads, pooled = pl.pallas_call(
        functools.partial(input_kernel, packed, cores),
        grid=(channels // STEP,),
        out_shape=(
            jax.ShapeDtypeStruct((slots, side, side, 1, channels), F32),
            jax.ShapeDtypeStruct((1, 1, channels), F32),
        ),
        in_specs=[
            smem_whole(),
            pl.BlockSpec((1, 128), lambda j: (0, 0)),
            pl.BlockSpec((side, kept, STEP), lambda j: (0, 0, j)),
            pl.BlockSpec((taps, width, STEP), lambda j: (0, 0, j)),
            pl.BlockSpec((1, 128), lambda j: (0, 0)),
        ]
        + [pl.BlockSpec((part.shape[0], blocks, BLOCK), lambda j: (0, 0, 0)) for part in shares],
        out_specs=(
            pl.BlockSpec((slots, side, side, 1, STEP), lambda j: (0, 0, 0, 0, j)),
            pl.BlockSpec((1, 1, STEP), lambda j: (0, 0, j)),
        ),
        compiler_params=params(16),
        cost_estimate=cost(8 * macs, 4 * 2**20),
    )(
        mine,
        routes,
        pltpu.with_memory_space_constraint(slope, pltpu.HBM),
        conv_weight,
        below,
        *shares,
    )
    total, (grads, pooled) = sum_over_slide(terms, cores, (grads, pooled))
    weight_grads = total / LOSS_SCALE
    input_grads = jnp.transpose(grads, (3, 0, 1, 2, 4))
    return (pooled, input_grads, weight_grads)


def solution(mesh):
    return jax.shard_map(
        shards,
        mesh=mesh,
        in_specs=(
            P("slide", "tile", None, None, None),
            P("slide", "tile"),
            P("slide", "tile"),
            P("slide", "tile", None),
            P("slide", None),
            P("slide", "tile", None),
            P(),
        ),
        out_specs=(
            P("slide", "tile", None),
            P("slide", "tile", None, None, None),
            P(None, None, "tile"),
        ),
        check_vma=False,
    )
```

```python
import functools

import jax
import jax.numpy as jnp
from jax import lax
from jax.experimental import pallas as pl
from jax.experimental.pallas import tpu as pltpu
from jax.sharding import PartitionSpec as P

LOSS_SCALE = 512.0
BLOCK = 256
STEP = 1024
ROW = 8
F32 = jnp.float32
BF16 = jnp.bfloat16


def vmem_whole():
    return pl.BlockSpec(memory_space=pltpu.VMEM)


def smem_whole():
    return pl.BlockSpec(memory_space=pltpu.SMEM)


def own_scalars(counts_ref, weights_ref, slide_ref, owner_ref, slots):
    coefs, targets = [], []
    for slot in range(slots):
        live = counts_ref[0, 0] > slot
        coefs.append(jnp.where(live, weights_ref[0, slot], 0.0))
        targets.append(owner_ref[0, slide_ref[0, slot]])
    return coefs, targets


def block_diagonal(tap, mask):
    width, channels = tap.shape
    if channels == width:
        return tap
    return jnp.concatenate([tap] * (channels // width), axis=0) * mask


def diagonal_mask(channels, width):
    row = lax.broadcasted_iota(jnp.int32, (channels, channels), 0) // width
    col = lax.broadcasted_iota(jnp.int32, (channels, channels), 1) // width
    return (row == col).astype(F32).astype(BF16)


def shifted(rows):
    count = rows.shape[0]
    return (
        pltpu.roll(rows, 1, 0).astype(BF16),
        rows.astype(BF16),
        pltpu.roll(rows, count - 1, 0).astype(BF16),
    )


def conv_taps(rows_ref, weight_of, pitch, count, flip, dims):
    total = None
    for offset in range(9):
        row_off, col_off = divmod(offset, 3)
        if flip:
            row_off, col_off = 2 - row_off, 2 - col_off
        rows = rows_ref[col_off, pl.ds(row_off * pitch, count), :]
        term = lax.dot_general(rows, weight_of(offset), dims, preferred_element_type=F32)
        total = term if total is None else total + term
    return total


def left_half(count):
    return lax.broadcasted_iota(jnp.int32, (count, 128), 1) < 64


def split(low, middle, high):
    left = left_half(low.shape[0])
    turned = pltpu.roll(middle, 64, 1)
    first = (jnp.where(left, low, turned), jnp.where(left, high, 0.0))
    second = (jnp.where(left, turned, low), jnp.where(left, 0.0, high))
    return tuple(jnp.concatenate(parts, axis=1).astype(BF16) for parts in (first, second))


def joined(first, second):
    left = left_half(first.shape[0])
    low = jnp.where(left, first[:, :128], second[:, :128])
    middle = pltpu.roll(jnp.where(left, second[:, :128], first[:, :128]), 64, 1)
    high = jnp.where(left, first[:, 128:], second[:, 128:])
    return low, middle, high


def pair_weights(w_ref, lanes, backward):
    rows = []
    for outer in (-1, 0, 1):
        taps = []
        for inner in (-1, 0, 1):
            row, col = (-outer, -inner) if backward else (inner, outer)
            taps.append(w_ref[3 * (row + 1) + col + 1, :, lanes].astype(F32))
        rows.append(split(*taps))
    empty = jnp.zeros(rows[0][0].shape, BF16)
    first = jnp.concatenate([rows[0][0], rows[1][0], rows[2][0], empty], axis=0)
    second = jnp.concatenate([rows[1][1], rows[0][1], empty, rows[2][1]], axis=0)
    return first, second


def pair_rows(rows):
    return split(pltpu.roll(rows, 1, 0), rows, pltpu.roll(rows, rows.shape[0] - 1, 0))


def pair_conv(first, second, weights, pitch, dims):
    first = lax.dot_general(first, weights[0], dims, preferred_element_type=F32)
    second = lax.dot_general(second, weights[1], dims, preferred_element_type=F32)
    side = first.shape[0] // pitch
    parts = []
    for high in range(side):
        span = slice(high * pitch, (high + 1) * pitch)
        parts.append(joined(first[span], second[span]))
    sums = []
    for high in range(side):
        total = parts[high][1]
        if high > 0:
            total = total + parts[high - 1][0]
        if high + 1 < side:
            total = total + parts[high + 1][2]
        sums.append(total)
    return sums


def slope_of(pre):
    sigma = jax.nn.sigmoid(pre)
    return sigma, sigma * (1.0 + pre * (1.0 - sigma))


PLAIN = (((1,), (0,)), ((), ()))
TURNED = (((1,), (1,)), ((), ()))


def routing_of(info, slots, cores):
    devices = info.shape[0]
    core = (lax.broadcasted_iota(jnp.int32, (devices, 1), 0) % cores).astype(F32)
    owners = lax.broadcasted_iota(jnp.int32, (devices, 128), 1).astype(F32)
    routes = []
    total = jnp.zeros((1, 128), F32)
    for slot in range(slots):
        coef = (
            info[:, slot : slot + 1]
            + info[:, slots + slot : slots + slot + 1]
            + info[:, 2 * slots + slot : 2 * slots + slot + 1]
        )
        target = info[:, 3 * slots + slot : 3 * slots + slot + 1] * cores + core
        route = jnp.where(target == owners, coef, 0.0)
        routes.append(route)
        total = total + jnp.sum(route, axis=0, keepdims=True)
    return routes, jnp.maximum(total, 1.0)


def scaled_rows(cot, denominator, ids):
    same = ids == lax.broadcasted_iota(jnp.int32, (cot.shape[0], 128), 1)
    column = jnp.sum(jnp.where(same, denominator, 0.0), axis=1, keepdims=True)
    return (LOSS_SCALE * cot / column).astype(BF16).astype(F32)


def info_row(coefs, targets, lanes):
    slots = len(coefs)
    lane = lax.broadcasted_iota(jnp.int32, (1, lanes), 1)
    value = jnp.zeros((1, lanes), F32)
    for slot in range(slots):
        for part in range(3):
            value = jnp.where(lane == part * slots + slot, coefs[slot], value)
        value = jnp.where(lane == 3 * slots + slot, targets[slot].astype(F32), value)
    high = value.astype(BF16).astype(F32)
    middle = (value - high).astype(BF16).astype(F32)
    low = (value - high - middle).astype(BF16).astype(F32)
    value = jnp.where((lane >= slots) & (lane < 2 * slots), middle, high)
    return jnp.where((lane >= 2 * slots) & (lane < 3 * slots), low, value)


def own_row(coefs, targets):
    slots = len(coefs)
    lane = lax.broadcasted_iota(jnp.int32, (1, 128), 1)
    value = jnp.zeros((1, 128), F32)
    for slot in range(slots):
        value = jnp.where(lane == slot, coefs[slot], value)
        value = jnp.where(lane == slots + slot, targets[slot].astype(F32), value)
    return value


def own_route(own, slots, owner):
    return [
        jnp.where(own[:, slots + slot : slots + slot + 1] == owner, own[:, slot : slot + 1], 0.0)
        for slot in range(slots)
    ]


def pack_kernel(
    counts_ref,
    weights_ref,
    slide_ref,
    owner_ref,
    x_ref,
    cot_ref,
    out_ref,
    own_ref,
    flat_ref,
):
    devices, groups, _, lanes = out_ref.shape
    _, slots, side, _, channels = x_ref.shape
    rows = slots * side * side
    for index in range(slots * side):
        values = x_ref[0, index // side, index % side].astype(F32)
        flat_ref[pl.ds(index * side, side), :] = values
    flat_ref[pl.ds(rows, 1), :] = cot_ref[0].astype(F32)
    coefs, targets = own_scalars(counts_ref, weights_ref, slide_ref, owner_ref, slots)
    own_ref[...] = own_row(coefs, targets)
    info = info_row(coefs, targets, lanes)
    flat_ref[pl.ds(rows + 1, 1), :] = jnp.concatenate([info] * devices, axis=1)
    spare = groups * ROW - rows - 2
    flat_ref[pl.ds(rows + 2, spare), :] = jnp.zeros((spare, channels), F32)
    for device in range(devices):
        part = flat_ref[:, pl.ds(device * lanes, lanes)].astype(BF16)
        out_ref[device] = part.reshape(groups, ROW, lanes)


def local_kernel(cores, my_ref, own_ref, cot_ref, x_ref, w_ref, slope_ref, *share_refs):
    step = pl.program_id(0)
    side, kept, lanes = slope_ref.shape
    slots = kept // ROW
    devices = len(share_refs) * (share_refs[0].shape[0] - 1)
    totals = []
    for pair in range(lanes // 128):
        span = pl.ds(pair * 128, 128)
        pieces = []
        for high in range(side):
            for slot in range(slots):
                pieces += [x_ref[0, slot, high, :, span].astype(F32), jnp.zeros((ROW - side, 128), F32)]
        first, second = pair_rows(jnp.concatenate(pieces, axis=0))
        pres = pair_conv(first, second, pair_weights(w_ref, span, False), kept, PLAIN)
        total = jnp.zeros((kept, 128), F32)
        for high in range(side):
            pre = pres[high]
            sigma, slope = slope_of(pre)
            slope_ref[high, :, span] = slope.astype(BF16)
            total = total + pre * sigma
        totals.append(total)
    total = jnp.concatenate(totals, axis=1)
    place = lax.broadcasted_iota(jnp.int32, (ROW, lanes), 0)
    own = own_ref[...]
    means = []
    for slot in range(slots):
        here = jnp.where(place < side, total[slot * ROW : (slot + 1) * ROW], 0.0)
        mean = jnp.sum(here, axis=0, keepdims=True) / (side * side)
        means.append(mean.astype(BF16).astype(F32))
    for index in range(devices):
        owner = index if len(share_refs) == 1 else (my_ref[0] // cores) ^ index
        share = jnp.zeros((1, lanes), F32)
        for mean, weight in zip(means, own_route(own, slots, jnp.float32(owner))):
            share = share + weight * mean
        place_ref = share_refs[index % len(share_refs)]
        for part in range(lanes // BLOCK):
            at = pl.ds(step * (lanes // BLOCK) + part, 1)
            place_ref[index // len(share_refs), at, :] = share[:, part * BLOCK : (part + 1) * BLOCK]
    for part in range(lanes // BLOCK):
        at = pl.ds(step * (lanes // BLOCK) + part, 1)
        for place_ref in share_refs:
            span = slice(part * BLOCK, (part + 1) * BLOCK)
            place_ref[devices // len(share_refs), at, :] = cot_ref[0, :, span].astype(F32)


def weight_kernel(
    packed, cores, side, my_ref, got_ref, w_ref, out_ref, below_ref, rows_ref, grad_ref, flat_ref
):
    del my_ref
    devices, groups, _, lanes = got_ref.shape
    slots = groups * ROW // (side * side)
    width = w_ref.shape[1]
    part = devices * ROW
    pitch = slots * part
    flat_ref[...] = got_ref[...].astype(F32).reshape(devices, groups * ROW, lanes)
    tail = got_ref[:, groups - 1].astype(F32)
    cot = tail[:, slots * side * side % ROW, :]
    info = tail[:, slots * side * side % ROW + 1, :]
    routes, denominator = routing_of(info, slots, cores)
    below_ref[...] = denominator
    scaled = scaled_rows(cot, denominator, lax.broadcasted_iota(jnp.int32, (devices, 128), 0))
    place = lax.broadcasted_iota(jnp.int32, (devices, ROW, lanes), 1)
    tile_grads = []
    for slot in range(slots):
        rows = jnp.zeros((devices, lanes), F32)
        for owner in range(devices):
            rows = rows + routes[slot][:, owner : owner + 1] * scaled[owner : owner + 1]
        spread = jnp.broadcast_to(rows[:, None, :], (devices, ROW, lanes)) / (side * side)
        tile_grads.append(jnp.where(place < side, spread, 0.0).reshape(part, lanes))
    tile_grad = jnp.concatenate(tile_grads, axis=0)

    if packed:
        for pair in range(lanes // 128):
            span = pl.ds(pair * 128, 128)
            for high in range(side):
                rows = []
                for slot in range(slots):
                    here = flat_ref[:, pl.ds((slot * side + high) * side, ROW), span]
                    here = jnp.where(place[:, :, :128] < side, here, 0.0)
                    rows.append(here.reshape(part, 128))
                first, second = pair_rows(jnp.concatenate(rows, axis=0))
                rows_ref[0, pl.ds(high * pitch, pitch), :] = first
                rows_ref[1, pl.ds(high * pitch, pitch), :] = second
            first, second = rows_ref[0, :, :], rows_ref[1, :, :]
            pres = pair_conv(first, second, pair_weights(w_ref, span, False), pitch, PLAIN)
            grads = [slope_of(pre)[1] * tile_grad[:, pair * 128 : (pair + 1) * 128] for pre in pres]
            none = jnp.zeros((pitch, 128), F32)
            turned = jnp.concatenate([none, *grads, none], axis=0).astype(BF16).T
            count = side * pitch
            products = []
            for index in range(2):
                low, middle, high = (
                    turned[index * width : (index + 1) * width, at * pitch : at * pitch + count]
                    for at in (2, 1, 0)
                )
                empty = jnp.zeros(low.shape, BF16)
                order = [middle, low, empty, high] if index else [low, middle, high, empty]
                product = jnp.dot(
                    jnp.concatenate(order, axis=0), rows_ref[index, :, :], preferred_element_type=F32
                )
                products.append(product.T)
            for col, quarter, other in ((0, 0, 1), (1, 1, 0), (2, 2, 3)):
                taps = joined(
                    products[0][quarter * width : (quarter + 1) * width],
                    products[1][other * width : (other + 1) * width],
                )
                for row in range(3):
                    out_ref[3 * row + col, :, span] = taps[row].astype(BF16)
        return

    zero = jnp.zeros((pitch, lanes), BF16)
    for col in range(3):
        rows_ref[col, pl.ds(0, pitch), :] = zero
        rows_ref[col, pl.ds((side + 1) * pitch, pitch), :] = zero
    grad_ref[pl.ds(0, pitch), :] = zero
    grad_ref[pl.ds((side + 1) * pitch, pitch), :] = zero
    for high in range(side):
        for slot in range(slots):
            here = flat_ref[:, pl.ds((slot * side + high) * side, ROW), :]
            rows = jnp.where(place < side, here, 0.0)
            for col, moved in enumerate(shifted(rows.reshape(part, lanes))):
                rows_ref[col, pl.ds((high + 1) * pitch + slot * part, part), :] = moved
    mask = diagonal_mask(lanes, width) if lanes > width else None
    pre = conv_taps(
        rows_ref,
        lambda tap: block_diagonal(w_ref[tap], mask),
        pitch,
        side * pitch,
        False,
        (((1,), (0,)), ((), ())),
    )
    sigma = jax.nn.sigmoid(pre)
    slope = sigma * (1.0 + pre * (1.0 - sigma))
    for high in range(side):
        here = slope[high * pitch : (high + 1) * pitch] * tile_grad
        grad_ref[pl.ds((high + 1) * pitch, pitch), :] = here.astype(BF16)
    group = lax.broadcasted_iota(jnp.int32, (width, lanes), 1) // width
    for offset in range(9):
        row_off, col_off = divmod(offset, 3)
        product = lax.dot_general(
            rows_ref[col_off, pl.ds(pitch, side * pitch), :],
            grad_ref[pl.ds((2 - row_off) * pitch, side * pitch), :],
            (((0,), (0,)), ((), ())),
            preferred_element_type=F32,
        )
        result = product[:width]
        for index in range(1, lanes // width):
            result = jnp.where(group == index, product[index * width : (index + 1) * width], result)
        out_ref[offset] = result.astype(BF16)


def input_kernel(
    packed,
    cores,
    my_ref,
    own_ref,
    slope_ref,
    w_ref,
    below_ref,
    *refs,
):
    *refs, out_ref, pooled_ref = refs
    step = pl.program_id(0)
    side, kept, lanes = slope_ref.shape
    slots = kept // ROW
    devices = 2 * len(refs) if packed else refs[1].shape[0]
    denominator = below_ref[...]
    owners = lax.broadcasted_iota(jnp.int32, (1, 128), 1)
    mine = jnp.sum(jnp.where(owners == my_ref[0], denominator, 0.0), axis=1, keepdims=True)
    base = my_ref[0] // cores if packed else 0
    cots = []
    for part in range(lanes // BLOCK):
        at = pl.ds(step * (lanes // BLOCK) + part, 1)
        if packed:
            shares = [ref[0, at, :] for ref in refs]
            rows = [ref[row, at, :] for ref in refs for row in (1, 2)]
            cots.append(jnp.concatenate(rows, axis=0))
        else:
            shares = [jnp.sum(refs[0][:, at, :], axis=0)]
            cots.append(refs[1][:, at, :].reshape(devices, BLOCK))
        pooled_ref[0, :, part * BLOCK : (part + 1) * BLOCK] = sum(shares[1:], shares[0]) / mine
    ids = (lax.broadcasted_iota(jnp.int32, (devices, 128), 0) ^ base) * cores + my_ref[0] % cores
    cot = jnp.concatenate(cots, axis=1)
    scaled = scaled_rows(cot, denominator, ids)

    place = lax.broadcasted_iota(jnp.int32, (ROW, lanes), 0)
    own = own_ref[...]
    pieces = []
    owner = (lax.broadcasted_iota(jnp.int32, (devices, 1), 0) ^ base).astype(F32)
    for weight in own_route(own, slots, owner):
        row = jnp.sum(weight * scaled, axis=0, keepdims=True)
        spread = jnp.broadcast_to(row, (ROW, lanes)) / (side * side)
        pieces.append(jnp.where(place < side, spread, 0.0))
    tile_grad = jnp.concatenate(pieces, axis=0)

    for pair in range(lanes // 128):
        span = pl.ds(pair * 128, 128)
        here = tile_grad[:, pair * 128 : (pair + 1) * 128]
        rows = jnp.concatenate([slope_ref[high, :, span].astype(F32) * here for high in range(side)], axis=0)
        first, second = pair_rows(rows)
        sums = pair_conv(first, second, pair_weights(w_ref, span, True), kept, TURNED)
        for high in range(side):
            for slot in range(slots):
                for wide in range(side):
                    at = slot * ROW + wide
                    out_ref[slot, high, wide, :, span] = sums[high][at : at + 1]


def params(mebibytes):
    return pltpu.CompilerParams(vmem_limit_bytes=mebibytes * 2**20)


def cost(flops, moved):
    return pl.CostEstimate(flops=flops, bytes_accessed=moved, transcendentals=0)


def swap(value, axis, step):
    return lax.ppermute(value, axis, [(i, i ^ step) for i in range(lax.axis_size(axis))])


def sum_over_slide(terms, cores, beside):
    count = lax.axis_size("slide")
    total, step = terms, cores
    while step < count:
        sent = total.astype(BF16)
        other = swap(sent, "slide", step)
        if 2 * step >= count:
            other, beside = lax.optimization_barrier((other, beside))
        total = sent.astype(F32) + other.astype(F32)
        step *= 2
    if cores == 2:
        second = lax.axis_index("slide") % 2 == 1
        half = total.astype(BF16)
        rest = swap(half, "slide", 1)
        whole = [jnp.where(second, rest, half), jnp.where(second, half, rest)]
        total = jnp.concatenate(whole, axis=2)
    return total.astype(F32), beside


def shards(tiles, tile_counts, tile_weights, slide_of, owner_map, cotangent, conv_weight):
    _, slots, side, _, channels = tiles.shape
    taps, width, _ = conv_weight.shape
    devices = lax.axis_size("tile")
    count = lax.axis_size("slide")
    packed = channels // devices == BLOCK and count % 2 == 0
    cores = 2 if packed else 1
    exchange = devices * cores
    lanes = channels // exchange
    blocks = channels // BLOCK
    mine = lax.axis_index("tile") * cores + lax.axis_index("slide") % cores
    mine = mine.astype(jnp.int32).reshape(1)
    slides = slide_of[:, :, 0]
    groups = -(-(slots * side * side + 2) // ROW)
    kept = slots * ROW
    macs = slots * side * side * taps * width * channels

    chunks, routes = pl.pallas_call(
        pack_kernel,
        out_shape=(
            jax.ShapeDtypeStruct((exchange, groups, ROW, lanes), BF16),
            jax.ShapeDtypeStruct((1, 128), F32),
        ),
        in_specs=[smem_whole()] * 4 + [vmem_whole()] * 2,
        out_specs=(vmem_whole(), vmem_whole()),
        scratch_shapes=[pltpu.VMEM((groups * ROW, channels), F32)],
        compiler_params=params(56),
    )(tile_counts, tile_weights, slides, owner_map, tiles, cotangent)
    if packed:
        chips = [
            [tile * count + chip * cores + core for tile in range(devices) for core in range(cores)]
            for chip in range(count // cores)
        ]
        got = lax.all_to_all(
            chunks, ("tile", "slide"), 0, 0, tiled=True, axis_index_groups=chips
        )
    else:
        got = lax.all_to_all(chunks, "tile", 0, 0, tiled=True)

    halves = 2 if packed else 1
    slope, *sent = pl.pallas_call(
        functools.partial(local_kernel, cores),
        grid=(channels // STEP,),
        out_shape=(
            jax.ShapeDtypeStruct((side, kept, channels), BF16),
        )
        + (jax.ShapeDtypeStruct((devices // halves + 1, blocks, BLOCK), F32),) * halves,
        in_specs=[
            smem_whole(),
            pl.BlockSpec((1, 128), lambda j: (0, 0)),
            pl.BlockSpec((1, 1, STEP), lambda j: (0, 0, j)),
            pl.BlockSpec((1, slots, side, side, STEP), lambda j: (0, 0, 0, 0, j)),
            pl.BlockSpec((taps, width, STEP), lambda j: (0, 0, j)),
        ],
        out_specs=(
            pl.BlockSpec((side, kept, STEP), lambda j: (0, 0, j)),
        )
        + (pl.BlockSpec((devices // halves + 1, blocks, BLOCK), lambda j: (0, 0, 0)),) * halves,
        compiler_params=params(56),
        cost_estimate=cost(8 * macs, 4 * 2**20),
    )(mine, routes, cotangent, tiles, conv_weight)
    if packed:
        half = devices // 2
        other = swap(sent[1], "tile", 1)
        toward = sent[0][:half] + other[:half]
        cots = [sent[0][half:], other[half:]]
        toward = [jnp.concatenate([toward[i : i + 1], *cots]) for i in range(half)]
    else:
        toward = sent[0]
    got, slope, _ = lax.optimization_barrier((got, slope, toward))
    if packed:
        shares = toward[:1] + [swap(toward[i], "tile", 2 * i) for i in range(1, half)]
    else:
        shares = [lax.all_to_all(toward[:devices], "tile", 0, 0, tiled=True)]
        shares.append(lax.all_gather(toward[devices:], "tile", axis=0, tiled=True))
    pitch_all = slots * exchange * ROW
    if packed:
        scratch = [pltpu.VMEM((2, side * pitch_all, BLOCK), BF16)] * 2
    else:
        scratch = [
            pltpu.VMEM((3, (side + 2) * pitch_all, lanes), BF16),
            pltpu.VMEM(((side + 2) * pitch_all, lanes), BF16),
        ]
    scratch.append(pltpu.VMEM((exchange, groups * ROW, lanes), F32))
    if packed:
        weight_spec = pl.BlockSpec((taps, width, lanes), lambda j, my: (0, 0, my[0]))
        weight = conv_weight
    else:
        weight_spec = pl.BlockSpec((taps, width, lanes), lambda j, my: (0, 0, 0))
        weight = lax.dynamic_slice_in_dim(conv_weight, mine[0] * lanes, lanes, 2)
    terms, below = pl.pallas_call(
        functools.partial(weight_kernel, packed, cores, side),
        out_shape=(
            jax.ShapeDtypeStruct((taps, width, lanes), BF16),
            jax.ShapeDtypeStruct((1, 128), F32),
        ),
        grid_spec=pltpu.PrefetchScalarGridSpec(
            num_scalar_prefetch=1,
            grid=(1,),
            in_specs=[pl.BlockSpec(got.shape, lambda j, my: (0, 0, 0, 0)), weight_spec],
            out_specs=(
                pl.BlockSpec((taps, width, lanes), lambda j, my: (0, 0, 0)),
                pl.BlockSpec((1, 128), lambda j, my: (0, 0)),
            ),
            scratch_shapes=scratch,
        ),
        compiler_params=params(20),
        cost_estimate=cost(16 * macs, 4 * 2**20),
    )(mine, got, weight)

    terms, shares = lax.optimization_barrier((terms, shares))
    grads, pooled = pl.pallas_call(
        functools.partial(input_kernel, packed, cores),
        grid=(channels // STEP,),
        out_shape=(
            jax.ShapeDtypeStruct((slots, side, side, 1, channels), F32),
            jax.ShapeDtypeStruct((1, 1, channels), F32),
        ),
        in_specs=[
            smem_whole(),
            pl.BlockSpec((1, 128), lambda j: (0, 0)),
            pl.BlockSpec((side, kept, STEP), lambda j: (0, 0, j)),
            pl.BlockSpec((taps, width, STEP), lambda j: (0, 0, j)),
            pl.BlockSpec((1, 128), lambda j: (0, 0)),
        ]
        + [pl.BlockSpec((part.shape[0], blocks, BLOCK), lambda j: (0, 0, 0)) for part in shares],
        out_specs=(
            pl.BlockSpec((slots, side, side, 1, STEP), lambda j: (0, 0, 0, 0, j)),
            pl.BlockSpec((1, 1, STEP), lambda j: (0, 0, j)),
        ),
        compiler_params=params(16),
        cost_estimate=cost(8 * macs, 4 * 2**20),
    )(
        mine,
        routes,
        pltpu.with_memory_space_constraint(slope, pltpu.HBM),
        conv_weight,
        below,
        *shares,
    )
    total, (grads, pooled) = sum_over_slide(terms, cores, (grads, pooled))
    weight_grads = total / LOSS_SCALE
    input_grads = jnp.transpose(grads, (3, 0, 1, 2, 4))
    return (pooled, input_grads, weight_grads)


def solution(mesh):
    return jax.shard_map(
        shards,
        mesh=mesh,
        in_specs=(
            P("slide", "tile", None, None, None),
            P("slide", "tile"),
            P("slide", "tile"),
            P("slide", "tile", None),
            P("slide", None),
            P("slide", "tile", None),
            P(),
        ),
        out_specs=(
            P("slide", "tile", None),
            P("slide", "tile", None, None, None),
            P(None, None, "tile"),
        ),
        check_vma=False,
    )
```
